128 devices in a mesh: row: 8 (over x, y_hi), col: 16 (over y_lo, z, core).
Axes of the slice: x: 4, y: 4 (y_hi: 2, y_lo: 2; y = y_hi * 2 + y_lo), z: 4, core: 2. Of those that a mesh axis runs over, the one named last changes fastest.
Arguments:
- values: bfloat16 [8192, 8192], P('row', 'col'), as said below
- pattern: int32 [64, 64], P('row', 'col'), may hold values from 0 to 1, as said below
- filter_mask: int32 [64, 64], P('row', 'col'), may hold values 0 or 1
- assignment: int32 [64], replicated, may hold values from 0 to 63, as said below
Outputs:
- product: bfloat16 [8192, 8192], P('row', 'col')
- occupation: float32 [], replicated
The draws below stay inside these ranges and needn't reach their ends.
Inputs may be any that keep to these rules, and one draw needn't show every extreme that they name: `assignment`: each block index appears once. The block pattern of P is symmetric: pattern[a, b] equals pattern[c, assignment[a]] where assignment[c] = b; every block row and every block column of pattern holds at most 6 occupied blocks, and some row and some column hold exactly 6; the diagonal blocks of P are occupied. `values`: P is symmetric: entry (i, j) of P equals entry (j, i).
All inputs are finite; a program needn't handle non-finite values. No bound on the sum of `filter_mask` on one device may be relied on, other than what follows from the above.
Results may differ from the reference program's by a relative error of at most 0.0012.
Values may be sent and summed in bfloat16 or wider, within the bound.
A program may use at most 128 MiB of HBM per device.

```python
import jax
import jax.numpy as jnp

BS = 128
MATCHES = 3
MOST = 6
NB = 64
ORDER = 8192


def shared_order(key):
    return jax.random.permutation(key, NB).astype(jnp.int32)


def draw_assignment(key, part):
    order = shared_order(key)
    return order


def draw_pattern(key, part):
    order = shared_order(key)
    key = jax.random.fold_in(key, 23)
    first_key, second_key = jax.random.split(key)
    offsets = jax.random.permutation(first_key, NB - 3)[:MATCHES].astype(jnp.int32) + 2
    index = jnp.arange(NB, dtype=jnp.int32)
    rows = index[:, None]
    cols = index[None, :]
    centre = NB // 2
    band = jnp.abs(rows - cols) <= 1
    coins = jax.random.randint(second_key, (NB, NB), 0, 4, dtype=jnp.int32)
    coins = jnp.where(rows <= cols, coins, coins.T)
    forced = (rows == centre) | (cols == centre)
    sums = (rows + cols) % NB
    targets = (2 * centre + offsets) % NB
    paired = jnp.any(sums[:, :, None] == targets[None, None, :], axis=2)
    occupied = band | paired & ((coins < 3) | forced)
    return occupied.astype(jnp.int32)[order]


def draw_values(key, part):
    order = shared_order(key)
    key = jax.random.fold_in(key, 37)
    spread = (MOST * BS) ** (-0.25)
    raw = jax.random.normal(key, (ORDER, ORDER), jnp.float32)
    symmetric = (raw + raw.T) * (spread * 0.70710678)
    permuted = symmetric.reshape(NB, BS, ORDER)[order].reshape(ORDER, ORDER)
    return permuted.astype(jnp.bfloat16)


def touch_ends(drawn, key, low, top_value):
    spot = [jax.random.randint(jax.random.fold_in(key, axis), (), 0, length) for axis, length in enumerate(drawn.shape)]
    main_axis = drawn.shape.index(max(drawn.shape))
    neighbour = spot[:main_axis] + [(spot[main_axis] + 1) % drawn.shape[main_axis]] + spot[main_axis + 1:]
    return drawn.at[tuple(spot)].set(low).at[tuple(neighbour)].set(top_value)


def setup_inputs(seed: int = 0) -> dict:
    key_of = jax.random.split(jax.random.key(seed), 5)
    values = draw_values(jax.random.fold_in(key_of[4], 71), 0)
    pattern = draw_pattern(jax.random.fold_in(key_of[4], 71), 0)
    filter_mask = touch_ends((jax.random.randint(key_of[2], (NB, NB), 0, 2) < 1).astype(jnp.int32), jax.random.fold_in(key_of[2], 1), 0, 1)
    assignment = draw_assignment(jax.random.fold_in(key_of[4], 71), 0)
    return dict(values=values, pattern=pattern, filter_mask=filter_mask, assignment=assignment)


def reference(values, pattern, filter_mask, assignment):
    block_size = BS
    all_blocks = NB
    blocks = values.reshape(all_blocks, block_size, all_blocks, block_size)
    stored = (blocks * pattern[:, None, :, None].astype(jnp.bfloat16)).reshape(values.shape)
    inverse = jnp.zeros((all_blocks,), jnp.int32).at[assignment].set(jnp.arange(all_blocks, dtype=jnp.int32))
    density = jnp.take(stored.reshape(all_blocks, block_size, -1), inverse, axis=0).reshape(values.shape)
    square = jnp.dot(stored, density, preferred_element_type=jnp.float32)
    four_way = square.reshape(all_blocks, block_size, all_blocks, block_size)
    diagonal_blocks = four_way[jnp.arange(all_blocks, dtype=jnp.int32), :, assignment, :]
    occupation = jnp.sum(jnp.trace(diagonal_blocks, axis1=1, axis2=2))
    kept = four_way * filter_mask[:, None, :, None].astype(jnp.float32)
    return kept.reshape(square.shape).astype(jnp.bfloat16), occupation
```

```python
import jax
import jax.numpy as jnp
from jax import lax
from jax.experimental import pallas as pl
from jax.experimental.pallas import tpu as pltpu
from jax.sharding import PartitionSpec as P

BS = 128
CAP = 6
LIST = 128
CHUNKS = 2
PART = BS // CHUNKS
COPIES = 96
IX_C1B, IX_C1O, IX_C2, IX_C3, IX_R1B, IX_R1O, IX_R2, IX_R3 = range(0, 64, 8)
IX_MATCH = 64
MESH = pl.DeviceIdType.MESH


class Path:
    def __init__(self, refs):
        refs = list(refs)
        take = lambda: [refs.pop(0) for _ in range(CHUNKS)]
        self.first, self.send, self.send2 = take(), take(), take()
        self.second, self.third = take(), take()
        (self.l_own, self.l_in1, self.l_send2, self.l_own2, self.l_in2,
         self.l_send3, self.l_in3, self.l_final) = refs


def kernel(values, pattern_in, filter_in, assignment_in, out, occupation, *refs):
    refs = list(refs)
    take = lambda count: [refs.pop(0) for _ in range(count)]
    own, pattern, other_pattern, filter_mask, assignment = take(5)
    other = take(CHUNKS)
    C, R = Path(take(5 * CHUNKS + 8)), Path(take(5 * CHUNKS + 8))
    columns_panel, = take(1)
    rows = take(8)
    tacc, trecv, finished, table, load_sem, out_sem, send_sem, recv_sem = take(8)

    row, col = lax.axis_index("row"), lax.axis_index("col")
    x, y_hi = row // 2, row % 2
    y_lo, z, core = col // 8, (col // 2) % 4, col % 2

    def partners(position):
        even, odd = position + 1 - 2 * (position % 2), 3 - position
        a = even * (1 - core) + odd * core
        b = odd * (1 - core) + even * core
        return a, b, (position + 2) % 4

    xa, xb, xd = partners(x)
    za, zb, zd = partners(z)
    dev_xa, dev_xb = (xa * 2 + y_hi, col), (xb * 2 + y_hi, col)
    dev_yh = (x * 2 + 1 - y_hi, col)
    dev_za = (row, y_lo * 8 + za * 2 + core)
    dev_zb = (row, y_lo * 8 + zb * 2 + core)
    dev_yl = (row, (1 - y_lo) * 8 + z * 2 + core)
    other_col = col + 1 - 2 * core
    dev_core = (row, other_col)

    remote = []

    def copy(src, dst, device):
        index = len(remote)
        remote.append(pltpu.make_async_remote_copy(
            src_ref=src, dst_ref=dst, send_sem=send_sem.at[index],
            recv_sem=recv_sem.at[index], device_id=device, device_id_type=MESH,
        ))
        return remote[-1]

    def start(*copies):
        for one in copies:
            one.start()

    def landed(*copies):
        for one in copies:
            one.wait_recv()

    small = [
        pltpu.make_async_copy(src, dst, load_sem.at[4 + i])
        for i, (src, dst) in enumerate(
            ((pattern_in, pattern), (assignment_in, assignment), (filter_in, filter_mask))
        )
    ]
    loads = [
        pltpu.make_async_copy(values.at[:, :, q * BS:(q + 1) * BS], own.at[q], load_sem.at[q])
        for q in range(4)
    ]
    start(*small, *loads)
    barrier = pltpu.get_barrier_semaphore()
    for device in (dev_xa, dev_xb, dev_yh, dev_za, dev_zb, dev_yl, dev_core):
        pl.semaphore_signal(barrier, inc=1, device_id=device, device_id_type=MESH)

    zero = jnp.zeros((PART, BS), jnp.bfloat16)
    for path in (C, R):
        for k in range(CHUNKS):
            path.first[k][4 * CAP] = zero
            path.second[k][2 * CAP] = zero
            path.third[k][2 * CAP] = zero
    for ref in rows:
        ref[CAP] = jnp.zeros((BS, BS), jnp.bfloat16)

    def part(k):
        return slice(k * PART, (k + 1) * PART)

    def rank(flags):
        count = jnp.int32(0)
        places = [jnp.int32(0)] * CAP
        for t, flag in enumerate(flags):
            for j in range(min(CAP, t + 1)):
                places[j] = jnp.where((flag != 0) & (count == j), t, places[j])
            count = count + flag
        return places, count

    def rank_column(role, q):
        places, count = rank([pattern[q, t] for t in range(8)])
        C.l_own[role * LIST] = count
        for j in range(CAP):
            name = assignment[row * 8 + places[j]]
            C.l_own[role * LIST + 1 + j] = jnp.where(j < count, name, -1)
        return q, places, count

    def pack_column(ranked, k, dst, first):
        q, places, count = ranked
        for j in range(CAP):
            block = own[q, places[j], part(k), :]
            dst[first + j] = jnp.where(j < count, block, zero)

    for one in small:
        one.wait()
    ranked_columns = [rank_column(role, q) for role, q in enumerate((x, xb, xa, xd))]
    for one in loads:
        one.wait()
    for k in range(CHUNKS):
        pack_column(ranked_columns[2], k, C.send[k], 0)
        pack_column(ranked_columns[3], k, C.send[k], CAP)

    half = (1 - core) * 4
    r0m = copy(pattern, other_pattern, dev_core)
    r0 = [copy(own.at[:, pl.ds(half, 4), part(k)], other[k], dev_core) for k in range(CHUNKS)]

    def first_copies(path, device):
        return (
            copy(path.l_own.at[pl.ds(2 * LIST, 2 * LIST)], path.l_in1, device),
            [copy(path.send[k], path.first[k].at[pl.ds(2 * CAP, 2 * CAP)], device) for k in range(CHUNKS)],
        )

    c1m, c1 = first_copies(C, dev_xa)
    r1m, r1 = first_copies(R, dev_za)

    pl.semaphore_wait(barrier, 7)
    start(r0m, c1m)
    for k in range(CHUNKS):
        start(r0[k], c1[k])
    for k in range(CHUNKS):
        pack_column(ranked_columns[0], k, C.first[k], 0)
        pack_column(ranked_columns[1], k, C.first[k], CAP)

    def rank_row(role, q):
        line = core * 4 + q
        places, count = rank(
            [pattern[t, line] for t in range(4)] + [other_pattern[t, line] for t in range(4)]
        )
        R.l_own[role * LIST] = count
        for j in range(CAP):
            name = jnp.where(places[j] < 4, col * 4, other_col * 4 - 4) + places[j]
            R.l_own[role * LIST + 1 + j] = jnp.where(j < count, name, -1)
        return line, q, places, count

    def pack_row(ranked, k, dst, first):
        line, q, places, count = ranked
        for j in range(CAP):
            mine = places[j] < 4
            place = jnp.where(mine, places[j], places[j] - 4)
            block = jnp.where(mine, own[place, line, part(k), :], other[k][place, q])
            dst[first + j] = jnp.where(j < count, block, zero)

    landed(r0m)
    ranked_rows = [rank_row(role, q) for role, q in enumerate((z, zb, za, zd))]
    start(r1m)
    for k in range(CHUNKS):
        landed(r0[k])
        pack_row(ranked_rows[2], k, R.send[k], 0)
        pack_row(ranked_rows[3], k, R.send[k], CAP)
        start(r1[k])

    def merge(l1, at1, l2, at2, lout, ix, base1, base2, zero_slot):
        n1, n2 = l1[at1], l2[at2]
        lout[0] = n1 + n2
        for j in range(CAP):
            rest = jnp.clip(j - n1, 0, CAP - 1)
            in1, in2 = j < n1, j - n1 < n2
            lout[1 + j] = jnp.where(in1, l1[at1 + 1 + j], jnp.where(in2, l2[at2 + 1 + rest], -1))
            table[ix + j] = jnp.where(in1, base1 + j, jnp.where(in2, base2 + rest, zero_slot))

    def move(src, ix, dst):
        for j in range(CAP):
            dst[j] = src[table[ix + j]]

    def six(ref, k, first=0):
        return ref[k].at[pl.ds(first, CAP)]

    def later_copies(path, device2, device3):
        return (
            copy(path.l_send2, path.l_in2, device2),
            [copy(path.send2[k], six(path.second, k, CAP), device2) for k in range(CHUNKS)],
            copy(path.l_send3, path.l_in3, device3),
            [copy(six(path.third, k), six(path.third, k, CAP), device3) for k in range(CHUNKS)],
        )

    c2m, c2, c3m, c3 = later_copies(C, dev_xb, dev_yh)
    r2m, r2, r3m, r3 = later_copies(R, dev_zb, dev_yl)

    def lists1(path, in_copy, out_copy, ix_b, ix_o):
        landed(in_copy)
        merge(path.l_own, LIST, path.l_in1, LIST, path.l_send2, ix_b, CAP, 3 * CAP, 4 * CAP)
        start(out_copy)
        merge(path.l_own, 0, path.l_in1, 0, path.l_own2, ix_o, 0, 2 * CAP, 4 * CAP)

    def lists2(path, in_copy, out_copy, ix):
        landed(in_copy)
        merge(path.l_own2, 0, path.l_in2, 0, path.l_send3, ix, 0, CAP, 2 * CAP)
        start(out_copy)

    def lists3(path, in_copy, out_copies, ix):
        landed(in_copy)
        merge(path.l_send3, 0, path.l_in3, 0, path.l_final, ix, 0, CAP, 2 * CAP)
        start(*out_copies)

    def blocks1(path, in_copies, out_copies, ix_b, ix_o, k):
        landed(in_copies[k])
        move(path.first[k], ix_b, path.send2[k])
        start(out_copies[k])
        move(path.first[k], ix_o, path.second[k])

    def blocks2(path, in_copies, out_copies, ix, k):
        landed(in_copies[k])
        move(path.second[k], ix, path.third[k])
        start(out_copies[k])

    def names(path, role):
        return path.l_final.at[pl.ds(role * LIST, LIST)]

    c4am, c4bm = copy(names(C, 0), names(C, 2), dev_xa), copy(names(C, 0), names(C, 1), dev_xb)
    c5m = copy(names(C, 1), names(C, 3), dev_xa)
    r4am, r4bm = copy(names(R, 0), names(R, 2), dev_za), copy(names(R, 0), names(R, 1), dev_zb)
    r5m = copy(names(R, 1), names(R, 3), dev_za)
    fm = [copy(names(R, role), names(R, 4 + role), dev_core) for role in range(4)]

    def column(role, k):
        return columns_panel.at[pl.ds(role * CAP, CAP), part(k)]

    def line_of(role, k):
        return rows[role].at[pl.ds(0, CAP), part(k)]

    each = range(CHUNKS)
    c4a = [copy(column(0, k), column(2, k), dev_xa) for k in each]
    c4b = [copy(column(0, k), column(1, k), dev_xb) for k in each]
    c5 = [copy(column(1, k), column(3, k), dev_xa) for k in each]
    r4a = [copy(line_of(0, k), line_of(2, k), dev_za) for k in each]
    r4b = [copy(line_of(0, k), line_of(1, k), dev_zb) for k in each]
    r5 = [copy(line_of(1, k), line_of(3, k), dev_za) for k in each]
    f = [[copy(line_of(role, k), line_of(4 + role, k), dev_core) for k in each] for role in range(4)]

    def blocks3_column(k):
        landed(c3[k])
        for j in range(CAP):
            columns_panel[j, part(k), :] = C.third[k][table[IX_C3 + j]]
        start(c4b[k], c4a[k])

    def blocks3_row(k):
        landed(r3[k])
        for j in range(CAP):
            rows[0][j, part(k), :] = R.third[k][table[IX_R3 + j]]
        start(r4b[k], r4a[k], f[0][k])

    def squares(ref):
        total = jnp.zeros((8, BS), jnp.float32)
        for i in range(2 * CAP):
            block = ref[i].astype(jnp.float32)
            total = total + jnp.sum((block * block).reshape(PART // 8, 8, BS), axis=0)
        return total

    trace_devices = (dev_core, dev_xa, dev_za, dev_xb, dev_zb, dev_yh, dev_yl)
    trace = [copy(tacc.at[i], trecv.at[i], trace_devices[i]) for i in range(7)]

    def trace_step(i):
        landed(trace[i])
        tacc[i + 1] = tacc[i] + trecv[i]
        if i < 6:
            start(trace[i + 1])

    for k in each:
        pack_row(ranked_rows[0], k, R.first[k], 0)
        pack_row(ranked_rows[1], k, R.first[k], CAP)
    total = jnp.zeros((8, BS), jnp.float32)
    for k in each:
        total = total + squares(C.send[k])
        total = total + squares(C.first[k])
    tacc[0] = total
    start(trace[0])

    row_lag = 0.75
    steps = []
    for k in each:
        steps += [
            (1 + k, lambda k=k: blocks1(C, c1, c2, IX_C1B, IX_C1O, k)),
            (2 + k, lambda k=k: blocks2(C, c2, c3, IX_C2, k)),
            (3 + k, lambda k=k: blocks3_column(k)),
            (4 + k, lambda k=k: (landed(c4b[k]), start(c5[k]))),
            (1 + k + row_lag, lambda k=k: blocks1(R, r1, r2, IX_R1B, IX_R1O, k)),
            (2 + k + row_lag, lambda k=k: blocks2(R, r2, r3, IX_R2, k)),
            (3 + k + row_lag, lambda k=k: blocks3_row(k)),
            (4 + k + row_lag, lambda k=k: (landed(r4b[k]), start(r5[k], f[1][k]))),
            (4.2 + k + row_lag, lambda k=k: (landed(r4a[k]), start(f[2][k]))),
            (5 + k + row_lag, lambda k=k: (landed(r5[k]), start(f[3][k]))),
        ]
    steps += [
        (0.9, lambda: lists1(C, c1m, c2m, IX_C1B, IX_C1O)),
        (1.7, lambda: lists1(R, r1m, r2m, IX_R1B, IX_R1O)),
        (1.8, lambda: trace_step(0)),
        (1.9, lambda: lists2(C, c2m, c3m, IX_C2)),
        (2.7, lambda: lists2(R, r2m, r3m, IX_R2)),
        (2.9, lambda: lists3(C, c3m, (c4bm, c4am), IX_C3)),
        (3.1, lambda: trace_step(1)),
        (3.7, lambda: lists3(R, r3m, (r4bm, r4am, fm[0]), IX_R3)),
        (3.8, lambda: trace_step(2)),
        (4.1, lambda: (landed(c4bm), start(c5m))),
        (4.3, lambda: trace_step(3)),
        (4.8, lambda: (landed(r4bm), start(r5m, fm[1]))),
        (5.01, lambda: (landed(r4am), start(fm[2]))),
        (5.1, lambda: trace_step(4)),
        (5.8, lambda: (landed(r5m), start(fm[3]))),
        (5.85, lambda: trace_step(5)),
    ]
    for _, step in sorted(steps, key=lambda one: one[0]):
        step()

    late = [*r5, *f[1], *f[2], *f[3], r5m, *fm, *c5, c5m, *trace[5:]]
    for one in remote:
        if not any(one is other_one for other_one in late):
            one.wait_send()

    landed(c4am, c5m, *fm)

    def match(row_role, carry):
        have = [R.l_final[row_role * LIST + 1 + i] for i in range(CAP)]
        for t in range(4 * CAP):
            wanted = C.l_final[(t // CAP) * LIST + 1 + t % CAP]
            slot = jnp.int32(CAP)
            for i in range(CAP):
                slot = jnp.where(have[i] == wanted, i, slot)
            table[IX_MATCH + row_role * 4 * CAP + t] = slot
        return carry

    lax.fori_loop(0, 8, match, 0)
    trace_step(6)
    occupation[0, 0] = jnp.sum(tacc[7])

    for k in each:
        landed(c4a[k], c5[k])

    column_of = (x, xb, xa, xd)
    line_by_role = (
        [core * 4 + position for position in (z, zb, za, zd)]
        + [(1 - core) * 4 + position for position in (z, za, zb, zd)]
    )

    leaving = [
        pltpu.make_async_copy(finished.at[role], out.at[line_by_role[role]], out_sem.at[role])
        for role in range(8)
    ]

    def product(row_roles):
        for c in range(4):
            left = []
            for role in row_roles:
                base = IX_MATCH + (role * 4 + c) * CAP
                left.append(jnp.concatenate([rows[role][table[base + j]] for j in range(CAP)], axis=1))
            right = columns_panel[c * CAP:(c + 1) * CAP].reshape(CAP * BS, BS)
            total = jnp.dot(
                jnp.concatenate(left, axis=0), right, preferred_element_type=jnp.float32
            )
            q = column_of[c]
            for i, role in enumerate(row_roles):
                line = line_by_role[role]
                kept = jnp.where(filter_mask[q, line] != 0, total[i * BS:(i + 1) * BS], 0.0)
                finished[role, :, pl.ds(pl.multiple_of(q * BS, BS), BS)] = kept.astype(jnp.bfloat16)
        start(*[leaving[role] for role in row_roles])

    product((0, 1))
    product((2, 3))
    for role in (0, 1):
        landed(*f[role])
    product((4, 5))
    for role in (2, 3):
        landed(*f[role])
    product((6, 7))

    for one in late:
        one.wait_send()
    for one in leaving:
        one.wait()


def on_device(values, pattern, filter_mask, assignment):
    hbm = pl.BlockSpec(memory_space=pltpu.HBM)
    parts = lambda count: [pltpu.VMEM((count, PART, BS), jnp.bfloat16)] * CHUNKS
    lists = lambda *counts: [pltpu.SMEM((count * LIST,), jnp.int32) for count in counts]

    def path(final):
        return [
            *parts(4 * CAP + 1), *parts(2 * CAP), *parts(CAP), *parts(2 * CAP + 1),
            *parts(2 * CAP + 1), *lists(4, 2, 1, 1, 1, 1, 1, final),
        ]

    product, occupation = pl.pallas_call(
        kernel,
        out_shape=(
            jax.ShapeDtypeStruct((8, BS, 4 * BS), jnp.bfloat16),
            jax.ShapeDtypeStruct((1, 1), jnp.float32),
        ),
        in_specs=[hbm] * 4,
        out_specs=(hbm, pl.BlockSpec(memory_space=pltpu.SMEM)),
        scratch_shapes=[
            pltpu.VMEM((4, 8, BS, BS), jnp.bfloat16),
            pltpu.SMEM((4, 8), jnp.int32),
            pltpu.SMEM((4, 8), jnp.int32),
            pltpu.SMEM((4, 8), jnp.int32),
            pltpu.SMEM((64,), jnp.int32),
            *[pltpu.VMEM((4, 4, PART, BS), jnp.bfloat16)] * CHUNKS,
            *path(4),
            *path(8),
            pltpu.VMEM((4 * CAP, BS, BS), jnp.bfloat16),
            *[pltpu.VMEM((CAP + 1, BS, BS), jnp.bfloat16)] * 8,
            pltpu.VMEM((8, 8, BS), jnp.float32),
            pltpu.VMEM((7, 8, BS), jnp.float32),
            pltpu.VMEM((8, BS, 4 * BS), jnp.bfloat16),
            pltpu.SMEM((IX_MATCH + 8 * 4 * CAP,), jnp.int32),
            pltpu.SemaphoreType.DMA((7,)),
            pltpu.SemaphoreType.DMA((8,)),
            pltpu.SemaphoreType.DMA((COPIES,)),
            pltpu.SemaphoreType.DMA((COPIES,)),
        ],
        compiler_params=pltpu.CompilerParams(
            collective_id=0, has_side_effects=True, vmem_limit_bytes=63 * 1024 * 1024
        ),
        cost_estimate=pl.CostEstimate(
            flops=2 * 192 * BS**3, bytes_accessed=4 * 1024 * 1024, transcendentals=0
        ),
    )(values.reshape(8, BS, 4 * BS), pattern.T, filter_mask.T, assignment)
    return product.reshape(values.shape), occupation[0, 0]


def solution(mesh):
    in_specs = (P("row", "col"), P("row", "col"), P("row", "col"), P())
    out_specs = (P("row", "col"), P())
    return jax.shard_map(
        on_device, mesh=mesh, in_specs=in_specs, out_specs=out_specs, check_vma=False
    )
```

```python
import jax
import jax.numpy as jnp
from jax import lax
from jax.experimental import pallas as pl
from jax.experimental.pallas import tpu as pltpu
from jax.sharding import PartitionSpec as P

BS = 128
CAP = 6
LIST = 128
CHUNKS = 4
PART = BS // CHUNKS
COPIES = 160
IX_C1B, IX_C1O, IX_C2, IX_C3, IX_R1B, IX_R1O, IX_R2, IX_R3 = range(0, 64, 8)
IX_MATCH = 64
MESH = pl.DeviceIdType.MESH


class Path:
    def __init__(self, refs):
        refs = list(refs)
        take = lambda: [refs.pop(0) for _ in range(CHUNKS)]
        self.first, self.send, self.send2 = take(), take(), take()
        self.second, self.third = take(), take()
        (self.l_own, self.l_in1, self.l_send2, self.l_own2, self.l_in2,
         self.l_send3, self.l_in3, self.l_final) = refs


def kernel(values, pattern_in, filter_in, assignment_in, out, occupation, *refs):
    refs = list(refs)
    take = lambda count: [refs.pop(0) for _ in range(count)]
    own, pattern, other_pattern, filter_mask, assignment = take(5)
    other = take(CHUNKS)
    C, R = Path(take(5 * CHUNKS + 8)), Path(take(5 * CHUNKS + 8))
    columns_panel, = take(1)
    rows = take(8)
    tacc, trecv, finished, table, load_sem, out_sem, send_sem, recv_sem = take(8)

    row, col = lax.axis_index("row"), lax.axis_index("col")
    x, y_hi = row // 2, row % 2
    y_lo, z, core = col // 8, (col // 2) % 4, col % 2

    def partners(position):
        even, odd = position + 1 - 2 * (position % 2), 3 - position
        a = even * (1 - core) + odd * core
        b = odd * (1 - core) + even * core
        return a, b, (position + 2) % 4

    xa, xb, xd = partners(x)
    za, zb, zd = partners(z)
    dev_xa, dev_xb = (xa * 2 + y_hi, col), (xb * 2 + y_hi, col)
    dev_yh = (x * 2 + 1 - y_hi, col)
    dev_za = (row, y_lo * 8 + za * 2 + core)
    dev_zb = (row, y_lo * 8 + zb * 2 + core)
    dev_yl = (row, (1 - y_lo) * 8 + z * 2 + core)
    other_col = col + 1 - 2 * core
    dev_core = (row, other_col)

    remote = []

    def copy(src, dst, device):
        index = len(remote)
        remote.append(pltpu.make_async_remote_copy(
            src_ref=src, dst_ref=dst, send_sem=send_sem.at[index],
            recv_sem=recv_sem.at[index], device_id=device, device_id_type=MESH,
        ))
        return remote[-1]

    def start(*copies):
        for one in copies:
            one.start()

    def landed(*copies):
        for one in copies:
            one.wait_recv()

    small = [
        pltpu.make_async_copy(src, dst, load_sem.at[4 + i])
        for i, (src, dst) in enumerate(
            ((pattern_in, pattern), (assignment_in, assignment), (filter_in, filter_mask))
        )
    ]
    loads = [
        pltpu.make_async_copy(values.at[:, :, q * BS:(q + 1) * BS], own.at[q], load_sem.at[q])
        for q in range(4)
    ]
    start(*small, *loads)
    barrier = pltpu.get_barrier_semaphore()
    for device in (dev_xa, dev_xb, dev_yh, dev_za, dev_zb, dev_yl, dev_core):
        pl.semaphore_signal(barrier, inc=1, device_id=device, device_id_type=MESH)

    zero = jnp.zeros((PART, BS), jnp.bfloat16)
    for path in (C, R):
        for k in range(CHUNKS):
            path.first[k][4 * CAP] = zero
            path.second[k][2 * CAP] = zero
            path.third[k][2 * CAP] = zero
    for ref in rows:
        ref[CAP] = jnp.zeros((BS, BS), jnp.bfloat16)

    def part(k):
        return slice(k * PART, (k + 1) * PART)

    def rank(flags):
        count = jnp.int32(0)
        places = [jnp.int32(0)] * CAP
        for t, flag in enumerate(flags):
            for j in range(min(CAP, t + 1)):
                places[j] = jnp.where((flag != 0) & (count == j), t, places[j])
            count = count + flag
        return places, count

    def rank_column(role, q):
        places, count = rank([pattern[q, t] for t in range(8)])
        C.l_own[role * LIST] = count
        for j in range(CAP):
            name = assignment[row * 8 + places[j]]
            C.l_own[role * LIST + 1 + j] = jnp.where(j < count, name, -1)
        return q, places, count

    def pack_column(ranked, k, dst, first):
        q, places, count = ranked
        for j in range(CAP):
            block = own[q, places[j], part(k), :]
            dst[first + j] = jnp.where(j < count, block, zero)

    for one in small:
        one.wait()
    ranked_columns = [rank_column(role, q) for role, q in enumerate((x, xb, xa, xd))]
    for one in loads:
        one.wait()
    for k in range(CHUNKS):
        pack_column(ranked_columns[2], k, C.send[k], 0)
        pack_column(ranked_columns[3], k, C.send[k], CAP)

    half = (1 - core) * 4
    r0m = copy(pattern, other_pattern, dev_core)
    r0 = [copy(own.at[:, pl.ds(half, 4), part(k)], other[k], dev_core) for k in range(CHUNKS)]

    def first_copies(path, device):
        return (
            copy(path.l_own.at[pl.ds(2 * LIST, 2 * LIST)], path.l_in1, device),
            [copy(path.send[k], path.first[k].at[pl.ds(2 * CAP, 2 * CAP)], device) for k in range(CHUNKS)],
        )

    c1m, c1 = first_copies(C, dev_xa)
    r1m, r1 = first_copies(R, dev_za)

    pl.semaphore_wait(barrier, 7)
    start(r0m, c1m)
    for k in range(CHUNKS):
        start(r0[k], c1[k])
    for k in range(CHUNKS):
        pack_column(ranked_columns[0], k, C.first[k], 0)
        pack_column(ranked_columns[1], k, C.first[k], CAP)

    def rank_row(role, q):
        line = core * 4 + q
        places, count = rank(
            [pattern[t, line] for t in range(4)] + [other_pattern[t, line] for t in range(4)]
        )
        R.l_own[role * LIST] = count
        for j in range(CAP):
            name = jnp.where(places[j] < 4, col * 4, other_col * 4 - 4) + places[j]
            R.l_own[role * LIST + 1 + j] = jnp.where(j < count, name, -1)
        return line, q, places, count

    def pack_row(ranked, k, dst, first):
        line, q, places, count = ranked
        for j in range(CAP):
            mine = places[j] < 4
            place = jnp.where(mine, places[j], places[j] - 4)
            block = jnp.where(mine, own[place, line, part(k), :], other[k][place, q])
            dst[first + j] = jnp.where(j < count, block, zero)

    landed(r0m)
    ranked_rows = [rank_row(role, q) for role, q in enumerate((z, zb, za, zd))]
    start(r1m)
    for k in range(CHUNKS):
        landed(r0[k])
        pack_row(ranked_rows[2], k, R.send[k], 0)
        pack_row(ranked_rows[3], k, R.send[k], CAP)
        start(r1[k])

    def merge(l1, at1, l2, at2, lout, ix, base1, base2, zero_slot):
        n1, n2 = l1[at1], l2[at2]
        lout[0] = n1 + n2
        for j in range(CAP):
            rest = jnp.clip(j - n1, 0, CAP - 1)
            in1, in2 = j < n1, j - n1 < n2
            lout[1 + j] = jnp.where(in1, l1[at1 + 1 + j], jnp.where(in2, l2[at2 + 1 + rest], -1))
            table[ix + j] = jnp.where(in1, base1 + j, jnp.where(in2, base2 + rest, zero_slot))

    def move(src, ix, dst):
        for j in range(CAP):
            dst[j] = src[table[ix + j]]

    def six(ref, k, first=0):
        return ref[k].at[pl.ds(first, CAP)]

    def later_copies(path, device2, device3):
        return (
            copy(path.l_send2, path.l_in2, device2),
            [copy(path.send2[k], six(path.second, k, CAP), device2) for k in range(CHUNKS)],
            copy(path.l_send3, path.l_in3, device3),
            [copy(six(path.third, k), six(path.third, k, CAP), device3) for k in range(CHUNKS)],
        )

    c2m, c2, c3m, c3 = later_copies(C, dev_xb, dev_yh)
    r2m, r2, r3m, r3 = later_copies(R, dev_zb, dev_yl)

    def lists1(path, in_copy, out_copy, ix_b, ix_o):
        landed(in_copy)
        merge(path.l_own, LIST, path.l_in1, LIST, path.l_send2, ix_b, CAP, 3 * CAP, 4 * CAP)
        start(out_copy)
        merge(path.l_own, 0, path.l_in1, 0, path.l_own2, ix_o, 0, 2 * CAP, 4 * CAP)

    def lists2(path, in_copy, out_copy, ix):
        landed(in_copy)
        merge(path.l_own2, 0, path.l_in2, 0, path.l_send3, ix, 0, CAP, 2 * CAP)
        start(out_copy)

    def lists3(path, in_copy, out_copies, ix):
        landed(in_copy)
        merge(path.l_send3, 0, path.l_in3, 0, path.l_final, ix, 0, CAP, 2 * CAP)
        start(*out_copies)

    def blocks1(path, in_copies, out_copies, ix_b, ix_o, k):
        landed(in_copies[k])
        move(path.first[k], ix_b, path.send2[k])
        start(out_copies[k])
        move(path.first[k], ix_o, path.second[k])

    def blocks2(path, in_copies, out_copies, ix, k):
        landed(in_copies[k])
        move(path.second[k], ix, path.third[k])
        start(out_copies[k])

    def names(path, role):
        return path.l_final.at[pl.ds(role * LIST, LIST)]

    c4am, c4bm = copy(names(C, 0), names(C, 2), dev_xa), copy(names(C, 0), names(C, 1), dev_xb)
    c5m = copy(names(C, 1), names(C, 3), dev_xa)
    r4am, r4bm = copy(names(R, 0), names(R, 2), dev_za), copy(names(R, 0), names(R, 1), dev_zb)
    r5m = copy(names(R, 1), names(R, 3), dev_za)
    fm = [copy(names(R, role), names(R, 4 + role), dev_core) for role in range(4)]

    def column(role, k):
        return columns_panel.at[pl.ds(role * CAP, CAP), part(k)]

    def line_of(role, k):
        return rows[role].at[pl.ds(0, CAP), part(k)]

    each = range(CHUNKS)
    c4a = [copy(column(0, k), column(2, k), dev_xa) for k in each]
    c4b = [copy(column(0, k), column(1, k), dev_xb) for k in each]
    c5 = [copy(column(1, k), column(3, k), dev_xa) for k in each]
    r4a = [copy(line_of(0, k), line_of(2, k), dev_za) for k in each]
    r4b = [copy(line_of(0, k), line_of(1, k), dev_zb) for k in each]
    r5 = [copy(line_of(1, k), line_of(3, k), dev_za) for k in each]
    f = [[copy(line_of(role, k), line_of(4 + role, k), dev_core) for k in each] for role in range(4)]

    def blocks3_column(k):
        landed(c3[k])
        for j in range(CAP):
            columns_panel[j, part(k), :] = C.third[k][table[IX_C3 + j]]
        start(c4b[k], c4a[k])

    def blocks3_row(k):
        landed(r3[k])
        for j in range(CAP):
            rows[0][j, part(k), :] = R.third[k][table[IX_R3 + j]]
        start(r4b[k], r4a[k], f[0][k])

    def squares(ref):
        total = jnp.zeros((8, BS), jnp.float32)
        for i in range(2 * CAP):
            block = ref[i].astype(jnp.float32)
            total = total + jnp.sum((block * block).reshape(PART // 8, 8, BS), axis=0)
        return total

    trace_devices = (dev_core, dev_xa, dev_za, dev_xb, dev_zb, dev_yh, dev_yl)
    trace = [copy(tacc.at[i], trecv.at[i], trace_devices[i]) for i in range(7)]

    def trace_step(i):
        landed(trace[i])
        tacc[i + 1] = tacc[i] + trecv[i]
        if i < 6:
            start(trace[i + 1])

    for k in each:
        pack_row(ranked_rows[0], k, R.first[k], 0)
        pack_row(ranked_rows[1], k, R.first[k], CAP)
    total = jnp.zeros((8, BS), jnp.float32)
    for k in each:
        total = total + squares(C.send[k])
        total = total + squares(C.first[k])
    tacc[0] = total
    start(trace[0])

    row_lag, gap = 0.7, 1.7 / CHUNKS
    steps = []
    for k in each:
        at = 1 + k * gap
        steps += [
            (at, lambda k=k: blocks1(C, c1, c2, IX_C1B, IX_C1O, k)),
            (at + 1, lambda k=k: blocks2(C, c2, c3, IX_C2, k)),
            (at + 2, lambda k=k: blocks3_column(k)),
            (at + 3, lambda k=k: (landed(c4b[k]), start(c5[k]))),
            (at + row_lag, lambda k=k: blocks1(R, r1, r2, IX_R1B, IX_R1O, k)),
            (at + 1 + row_lag, lambda k=k: blocks2(R, r2, r3, IX_R2, k)),
            (at + 2 + row_lag, lambda k=k: blocks3_row(k)),
            (at + 3 + row_lag, lambda k=k: (landed(r4b[k]), start(r5[k], f[1][k]))),
            (at + 3.2 + row_lag, lambda k=k: (landed(r4a[k]), start(f[2][k]))),
            (at + 4 + row_lag, lambda k=k: (landed(r5[k]), start(f[3][k]))),
        ]
    last = (CHUNKS - 1) * gap + 0.02
    steps += [
        (0.99, lambda: lists1(C, c1m, c2m, IX_C1B, IX_C1O)),
        (0.99 + row_lag, lambda: lists1(R, r1m, r2m, IX_R1B, IX_R1O)),
        (1.01 + row_lag, lambda: trace_step(0)),
        (1.99, lambda: lists2(C, c2m, c3m, IX_C2)),
        (1.99 + row_lag, lambda: lists2(R, r2m, r3m, IX_R2)),
        (2.99, lambda: lists3(C, c3m, (c4bm, c4am), IX_C3)),
        (2 + last, lambda: trace_step(1)),
        (2.99 + row_lag, lambda: lists3(R, r3m, (r4bm, r4am, fm[0]), IX_R3)),
        (2 + last + row_lag, lambda: trace_step(2)),
        (4.01, lambda: (landed(c4bm), start(c5m))),
        (3 + last, lambda: trace_step(3)),
        (4.01 + row_lag, lambda: (landed(r4bm), start(r5m, fm[1]))),
        (4.21 + row_lag, lambda: (landed(r4am), start(fm[2]))),
        (3 + last + row_lag, lambda: trace_step(4)),
        (5.01 + row_lag, lambda: (landed(r5m), start(fm[3]))),
        (4 + last + row_lag, lambda: trace_step(5)),
    ]
    for _, step in sorted(steps, key=lambda one: one[0]):
        step()

    late = [*r5, *f[1], *f[2], *f[3], r5m, *fm, *c5, c5m, *trace[5:]]
    for one in remote:
        if not any(one is other_one for other_one in late):
            one.wait_send()

    landed(c4am, c5m, *fm)

    def match(row_role, carry):
        have = [R.l_final[row_role * LIST + 1 + i] for i in range(CAP)]
        for t in range(4 * CAP):
            wanted = C.l_final[(t // CAP) * LIST + 1 + t % CAP]
            slot = jnp.int32(CAP)
            for i in range(CAP):
                slot = jnp.where(have[i] == wanted, i, slot)
            table[IX_MATCH + row_role * 4 * CAP + t] = slot
        return carry

    lax.fori_loop(0, 8, match, 0)
    trace_step(6)
    occupation[0, 0] = jnp.sum(tacc[7])

    for k in each:
        landed(c4a[k], c5[k])

    column_of = (x, xb, xa, xd)
    line_by_role = (
        [core * 4 + position for position in (z, zb, za, zd)]
        + [(1 - core) * 4 + position for position in (z, za, zb, zd)]
    )

    leaving = [
        pltpu.make_async_copy(finished.at[role], out.at[line_by_role[role]], out_sem.at[role])
        for role in range(8)
    ]

    def product(row_roles):
        for c in range(4):
            left = []
            for role in row_roles:
                base = IX_MATCH + (role * 4 + c) * CAP
                left.append(jnp.concatenate([rows[role][table[base + j]] for j in range(CAP)], axis=1))
            right = columns_panel[c * CAP:(c + 1) * CAP].reshape(CAP * BS, BS)
            total = jnp.dot(
                jnp.concatenate(left, axis=0), right, preferred_element_type=jnp.float32
            )
            q = column_of[c]
            for i, role in enumerate(row_roles):
                line = line_by_role[role]
                kept = jnp.where(filter_mask[q, line] != 0, total[i * BS:(i + 1) * BS], 0.0)
                finished[role, :, pl.ds(pl.multiple_of(q * BS, BS), BS)] = kept.astype(jnp.bfloat16)
        start(*[leaving[role] for role in row_roles])

    product((0, 1))
    product((2, 3))
    for role in (0, 1):
        landed(*f[role])
    product((4, 5))
    for role in (2, 3):
        landed(*f[role])
    product((6, 7))

    for one in late:
        one.wait_send()
    for one in leaving:
        one.wait()


def on_device(values, pattern, filter_mask, assignment):
    hbm = pl.BlockSpec(memory_space=pltpu.HBM)
    parts = lambda count: [pltpu.VMEM((count, PART, BS), jnp.bfloat16)] * CHUNKS
    lists = lambda *counts: [pltpu.SMEM((count * LIST,), jnp.int32) for count in counts]

    def path(final):
        return [
            *parts(4 * CAP + 1), *parts(2 * CAP), *parts(CAP), *parts(2 * CAP + 1),
            *parts(2 * CAP + 1), *lists(4, 2, 1, 1, 1, 1, 1, final),
        ]

    product, occupation = pl.pallas_call(
        kernel,
        out_shape=(
            jax.ShapeDtypeStruct((8, BS, 4 * BS), jnp.bfloat16),
            jax.ShapeDtypeStruct((1, 1), jnp.float32),
        ),
        in_specs=[hbm] * 4,
        out_specs=(hbm, pl.BlockSpec(memory_space=pltpu.SMEM)),
        scratch_shapes=[
            pltpu.VMEM((4, 8, BS, BS), jnp.bfloat16),
            pltpu.SMEM((4, 8), jnp.int32),
            pltpu.SMEM((4, 8), jnp.int32),
            pltpu.SMEM((4, 8), jnp.int32),
            pltpu.SMEM((64,), jnp.int32),
            *[pltpu.VMEM((4, 4, PART, BS), jnp.bfloat16)] * CHUNKS,
            *path(4),
            *path(8),
            pltpu.VMEM((4 * CAP, BS, BS), jnp.bfloat16),
            *[pltpu.VMEM((CAP + 1, BS, BS), jnp.bfloat16)] * 8,
            pltpu.VMEM((8, 8, BS), jnp.float32),
            pltpu.VMEM((7, 8, BS), jnp.float32),
            pltpu.VMEM((8, BS, 4 * BS), jnp.bfloat16),
            pltpu.SMEM((IX_MATCH + 8 * 4 * CAP,), jnp.int32),
            pltpu.SemaphoreType.DMA((7,)),
            pltpu.SemaphoreType.DMA((8,)),
            pltpu.SemaphoreType.DMA((COPIES,)),
            pltpu.SemaphoreType.DMA((COPIES,)),
        ],
        compiler_params=pltpu.CompilerParams(
            collective_id=0, has_side_effects=True, vmem_limit_bytes=63 * 1024 * 1024
        ),
        cost_estimate=pl.CostEstimate(
            flops=2 * 192 * BS**3, bytes_accessed=4 * 1024 * 1024, transcendentals=0
        ),
    )(values.reshape(8, BS, 4 * BS), pattern.T, filter_mask.T, assignment)
    return product.reshape(values.shape), occupation[0, 0]


def solution(mesh):
    in_specs = (P("row", "col"), P("row", "col"), P("row", "col"), P())
    out_specs = (P("row", "col"), P())
    return jax.shard_map(
        on_device, mesh=mesh, in_specs=in_specs, out_specs=out_specs, check_vma=False
    )
```

```python
import jax
import jax.numpy as jnp
from jax import lax
from jax.experimental import pallas as pl
from jax.experimental.pallas import tpu as pltpu
from jax.sharding import PartitionSpec as P

BS = 128
CAP = 6
LIST = 128
CHUNKS = 2
PART = BS // CHUNKS
COPIES = 96
IX_C1B, IX_C1O, IX_C2, IX_C3, IX_R1B, IX_R1O, IX_R2, IX_R3 = range(0, 64, 8)
IX_MATCH = 64
MESH = pl.DeviceIdType.MESH


class Path:
    def __init__(self, refs):
        refs = list(refs)
        take = lambda: [refs.pop(0) for _ in range(CHUNKS)]
        self.first, self.send, self.send2 = take(), take(), take()
        self.second, self.third = take(), take()
        (self.l_own, self.l_in1, self.l_send2, self.l_own2, self.l_in2,
         self.l_send3, self.l_in3, self.l_final) = refs


def kernel(values, pattern_in, filter_in, assignment_in, out, occupation, *refs):
    refs = list(refs)
    take = lambda count: [refs.pop(0) for _ in range(count)]
    own, pattern, other_pattern, filter_mask, assignment = take(5)
    other = take(CHUNKS)
    C, R = Path(take(5 * CHUNKS + 8)), Path(take(5 * CHUNKS + 8))
    columns_panel, = take(1)
    rows = take(8)
    tacc, trecv, finished, table, load_sem, out_sem, send_sem, recv_sem = take(8)

    row, col = lax.axis_index("row"), lax.axis_index("col")
    x, y_hi = row // 2, row % 2
    y_lo, z, core = col // 8, (col // 2) % 4, col % 2

    def partners(position):
        even, odd = position + 1 - 2 * (position % 2), 3 - position
        a = even * (1 - core) + odd * core
        b = odd * (1 - core) + even * core
        return a, b, (position + 2) % 4

    xa, xb, xd = partners(x)
    za, zb, zd = partners(z)
    dev_xa, dev_xb = (xa * 2 + y_hi, col), (xb * 2 + y_hi, col)
    dev_yh = (x * 2 + 1 - y_hi, col)
    dev_za = (row, y_lo * 8 + za * 2 + core)
    dev_zb = (row, y_lo * 8 + zb * 2 + core)
    dev_yl = (row, (1 - y_lo) * 8 + z * 2 + core)
    other_col = col + 1 - 2 * core
    dev_core = (row, other_col)

    remote = []

    def copy(src, dst, device):
        index = len(remote)
        remote.append(pltpu.make_async_remote_copy(
            src_ref=src, dst_ref=dst, send_sem=send_sem.at[index],
            recv_sem=recv_sem.at[index], device_id=device, device_id_type=MESH,
        ))
        return remote[-1]

    def start(*copies):
        for one in copies:
            one.start()

    def landed(*copies):
        for one in copies:
            one.wait_recv()

    small = [
        pltpu.make_async_copy(src, dst, load_sem.at[4 + i])
        for i, (src, dst) in enumerate(
            ((pattern_in, pattern), (assignment_in, assignment), (filter_in, filter_mask))
        )
    ]
    loads = [
        pltpu.make_async_copy(values.at[:, :, q * BS:(q + 1) * BS], own.at[q], load_sem.at[q])
        for q in range(4)
    ]
    start(*small, *loads)
    barrier = pltpu.get_barrier_semaphore()
    for device in (dev_xa, dev_xb, dev_yh, dev_za, dev_zb, dev_yl, dev_core):
        pl.semaphore_signal(barrier, inc=1, device_id=device, device_id_type=MESH)

    zero = jnp.zeros((PART, BS), jnp.bfloat16)
    for path in (C, R):
        for k in range(CHUNKS):
            path.first[k][4 * CAP] = zero
            path.second[k][2 * CAP] = zero
            path.third[k][2 * CAP] = zero
    for ref in rows:
        ref[CAP] = jnp.zeros((BS, BS), jnp.bfloat16)

    def part(k):
        return slice(k * PART, (k + 1) * PART)

    def rank(flags):
        count = jnp.int32(0)
        places = [jnp.int32(0)] * CAP
        for t, flag in enumerate(flags):
            for j in range(min(CAP, t + 1)):
                places[j] = jnp.where((flag != 0) & (count == j), t, places[j])
            count = count + flag
        return places, count

    def rank_column(role, q):
        places, count = rank([pattern[q, t] for t in range(8)])
        C.l_own[role * LIST] = count
        for j in range(CAP):
            name = assignment[row * 8 + places[j]]
            C.l_own[role * LIST + 1 + j] = jnp.where(j < count, name, -1)
        return q, places, count

    def pack_column(ranked, k, dst, first):
        q, places, count = ranked
        for j in range(CAP):
            block = own[q, places[j], part(k), :]
            dst[first + j] = jnp.where(j < count, block, zero)

    for one in small:
        one.wait()
    ranked_columns = [rank_column(role, q) for role, q in enumerate((x, xb, xa, xd))]
    for one in loads:
        one.wait()
    for k in range(CHUNKS):
        pack_column(ranked_columns[2], k, C.send[k], 0)
        pack_column(ranked_columns[3], k, C.send[k], CAP)

    half = (1 - core) * 4
    r0m = copy(pattern, other_pattern, dev_core)
    r0 = [copy(own.at[:, pl.ds(half, 4), part(k)], other[k], dev_core) for k in range(CHUNKS)]

    def first_copies(path, device):
        return (
            copy(path.l_own.at[pl.ds(2 * LIST, 2 * LIST)], path.l_in1, device),
            [copy(path.send[k], path.first[k].at[pl.ds(2 * CAP, 2 * CAP)], device) for k in range(CHUNKS)],
        )

    c1m, c1 = first_copies(C, dev_xa)
    r1m, r1 = first_copies(R, dev_za)

    pl.semaphore_wait(barrier, 7)
    start(r0m, c1m)
    for k in range(CHUNKS):
        start(r0[k], c1[k])
    for k in range(CHUNKS):
        pack_column(ranked_columns[0], k, C.first[k], 0)
        pack_column(ranked_columns[1], k, C.first[k], CAP)

    def rank_row(role, q):
        line = core * 4 + q
        places, count = rank(
            [pattern[t, line] for t in range(4)] + [other_pattern[t, line] for t in range(4)]
        )
        R.l_own[role * LIST] = count
        for j in range(CAP):
            name = jnp.where(places[j] < 4, col * 4, other_col * 4 - 4) + places[j]
            R.l_own[role * LIST + 1 + j] = jnp.where(j < count, name, -1)
        return line, q, places, count

    def pack_row(ranked, k, dst, first):
        line, q, places, count = ranked
        for j in range(CAP):
            mine = places[j] < 4
            place = jnp.where(mine, places[j], places[j] - 4)
            block = jnp.where(mine, own[place, line, part(k), :], other[k][place, q])
            dst[first + j] = jnp.where(j < count, block, zero)

    landed(r0m)
    ranked_rows = [rank_row(role, q) for role, q in enumerate((z, zb, za, zd))]
    start(r1m)
    for k in range(CHUNKS):
        landed(r0[k])
        pack_row(ranked_rows[2], k, R.send[k], 0)
        pack_row(ranked_rows[3], k, R.send[k], CAP)
        start(r1[k])

    def merge(l1, at1, l2, at2, lout, ix, base1, base2, zero_slot):
        n1, n2 = l1[at1], l2[at2]
        lout[0] = n1 + n2
        for j in range(CAP):
            rest = jnp.clip(j - n1, 0, CAP - 1)
            in1, in2 = j < n1, j - n1 < n2
            lout[1 + j] = jnp.where(in1, l1[at1 + 1 + j], jnp.where(in2, l2[at2 + 1 + rest], -1))
            table[ix + j] = jnp.where(in1, base1 + j, jnp.where(in2, base2 + rest, zero_slot))

    def move(src, ix, dst):
        for j in range(CAP):
            dst[j] = src[table[ix + j]]

    def six(ref, k, first=0):
        return ref[k].at[pl.ds(first, CAP)]

    def later_copies(path, device2, device3):
        return (
            copy(path.l_send2, path.l_in2, device2),
            [copy(path.send2[k], six(path.second, k, CAP), device2) for k in range(CHUNKS)],
            copy(path.l_send3, path.l_in3, device3),
            [copy(six(path.third, k), six(path.third, k, CAP), device3) for k in range(CHUNKS)],
        )

    c2m, c2, c3m, c3 = later_copies(C, dev_xb, dev_yh)
    r2m, r2, r3m, r3 = later_copies(R, dev_zb, dev_yl)

    def lists1(path, in_copy, out_copy, ix_b, ix_o):
        landed(in_copy)
        merge(path.l_own, LIST, path.l_in1, LIST, path.l_send2, ix_b, CAP, 3 * CAP, 4 * CAP)
        start(out_copy)
        merge(path.l_own, 0, path.l_in1, 0, path.l_own2, ix_o, 0, 2 * CAP, 4 * CAP)

    def lists2(path, in_copy, out_copy, ix):
        landed(in_copy)
        merge(path.l_own2, 0, path.l_in2, 0, path.l_send3, ix, 0, CAP, 2 * CAP)
        start(out_copy)

    def lists3(path, in_copy, out_copies, ix):
        landed(in_copy)
        merge(path.l_send3, 0, path.l_in3, 0, path.l_final, ix, 0, CAP, 2 * CAP)
        start(*out_copies)

    def blocks1(path, in_copies, out_copies, ix_b, ix_o, k):
        landed(in_copies[k])
        move(path.first[k], ix_b, path.send2[k])
        start(out_copies[k])
        move(path.first[k], ix_o, path.second[k])

    def blocks2(path, in_copies, out_copies, ix, k):
        landed(in_copies[k])
        move(path.second[k], ix, path.third[k])
        start(out_copies[k])

    def names(path, role):
        return path.l_final.at[pl.ds(role * LIST, LIST)]

    c4am, c4bm = copy(names(C, 0), names(C, 2), dev_xa), copy(names(C, 0), names(C, 1), dev_xb)
    c5m = copy(names(C, 1), names(C, 3), dev_xa)
    r4am, r4bm = copy(names(R, 0), names(R, 2), dev_za), copy(names(R, 0), names(R, 1), dev_zb)
    r5m = copy(names(R, 1), names(R, 3), dev_za)
    fm = copy(R.l_final.at[pl.ds(0, 4 * LIST)], R.l_final.at[pl.ds(4 * LIST, 4 * LIST)], dev_core)

    def column(role, k):
        return columns_panel.at[pl.ds(role * CAP, CAP), part(k)]

    def line_of(role, k):
        return rows[role].at[pl.ds(0, CAP), part(k)]

    each = range(CHUNKS)
    c4a = [copy(column(0, k), column(2, k), dev_xa) for k in each]
    c4b = [copy(column(0, k), column(1, k), dev_xb) for k in each]
    c5 = [copy(column(1, k), column(3, k), dev_xa) for k in each]
    r4a = [copy(line_of(0, k), line_of(2, k), dev_za) for k in each]
    r4b = [copy(line_of(0, k), line_of(1, k), dev_zb) for k in each]
    r5 = [copy(line_of(1, k), line_of(3, k), dev_za) for k in each]
    f = [[copy(line_of(role, k), line_of(4 + role, k), dev_core) for k in each] for role in range(4)]

    def blocks3_column(k):
        landed(c3[k])
        for j in range(CAP):
            columns_panel[j, part(k), :] = C.third[k][table[IX_C3 + j]]
        start(c4b[k], c4a[k])

    def blocks3_row(k):
        landed(r3[k])
        for j in range(CAP):
            rows[0][j, part(k), :] = R.third[k][table[IX_R3 + j]]
        start(r4b[k], r4a[k], f[0][k])

    def squares(ref):
        total = jnp.zeros((8, BS), jnp.float32)
        for i in range(2 * CAP):
            block = ref[i].astype(jnp.float32)
            total = total + jnp.sum((block * block).reshape(PART // 8, 8, BS), axis=0)
        return total

    trace_devices = (dev_core, dev_xa, dev_za, dev_xb, dev_zb, dev_yh, dev_yl)
    trace = [copy(tacc.at[i], trecv.at[i], trace_devices[i]) for i in range(7)]

    def trace_step(i):
        landed(trace[i])
        tacc[i + 1] = tacc[i] + trecv[i]
        if i < 6:
            start(trace[i + 1])

    for k in each:
        pack_row(ranked_rows[0], k, R.first[k], 0)
        pack_row(ranked_rows[1], k, R.first[k], CAP)
    total = jnp.zeros((8, BS), jnp.float32)
    for k in each:
        total = total + squares(C.send[k])
        total = total + squares(C.first[k])
    tacc[0] = total
    start(trace[0])

    def match(row_role, carry):
        have = [R.l_final[row_role * LIST + 1 + i] for i in range(CAP)]
        for t in range(4 * CAP):
            wanted = C.l_final[(t // CAP) * LIST + 1 + t % CAP]
            slot = jnp.int32(CAP)
            for i in range(CAP):
                slot = jnp.where(have[i] == wanted, i, slot)
            table[IX_MATCH + row_role * 4 * CAP + t] = slot
        return carry

    def match_rows(first_role):
        lax.fori_loop(first_role, first_role + 4, match, 0)

    row_lag = 0.75
    steps = []
    for k in each:
        steps += [
            (1 + k, lambda k=k: blocks1(C, c1, c2, IX_C1B, IX_C1O, k)),
            (2 + k, lambda k=k: blocks2(C, c2, c3, IX_C2, k)),
            (3 + k, lambda k=k: blocks3_column(k)),
            (4 + k, lambda k=k: (landed(c4b[k]), start(c5[k]))),
            (1 + k + row_lag, lambda k=k: blocks1(R, r1, r2, IX_R1B, IX_R1O, k)),
            (2 + k + row_lag, lambda k=k: blocks2(R, r2, r3, IX_R2, k)),
            (3 + k + row_lag, lambda k=k: blocks3_row(k)),
            (4 + k + row_lag, lambda k=k: (landed(r4b[k]), start(r5[k], f[1][k]))),
            (4.2 + k + row_lag, lambda k=k: (landed(r4a[k]), start(f[2][k]))),
            (5 + k + row_lag, lambda k=k: (landed(r5[k]), start(f[3][k]))),
        ]
    steps += [
        (0.9, lambda: lists1(C, c1m, c2m, IX_C1B, IX_C1O)),
        (1.1, lambda: lists1(R, r1m, r2m, IX_R1B, IX_R1O)),
        (1.3, lambda: lists2(C, c2m, c3m, IX_C2)),
        (1.8, lambda: trace_step(0)),
        (2.1, lambda: lists2(R, r2m, r3m, IX_R2)),
        (2.2, lambda: lists3(C, c3m, (c4bm, c4am), IX_C3)),
        (2.9, lambda: lists3(R, r3m, (r4bm, r4am), IX_R3)),
        (3.1, lambda: trace_step(1)),
        (3.2, lambda: (landed(c4bm), start(c5m))),
        (3.8, lambda: (landed(r4bm), start(r5m))),
        (3.85, lambda: trace_step(2)),
        (4.05, lambda: (landed(r4am, r5m), start(fm))),
        (4.1, lambda: (landed(c4am, c5m), match_rows(0))),
        (4.3, lambda: trace_step(3)),
        (5.05, lambda: (landed(fm), match_rows(4))),
        (5.1, lambda: trace_step(4)),
        (5.85, lambda: trace_step(5)),
    ]
    for _, step in sorted(steps, key=lambda one: one[0]):
        step()

    for k in each:
        landed(c4a[k], c5[k])

    column_of = (x, xb, xa, xd)
    line_by_role = (
        [core * 4 + position for position in (z, zb, za, zd)]
        + [(1 - core) * 4 + position for position in (z, za, zb, zd)]
    )

    leaving = [
        pltpu.make_async_copy(finished.at[role], out.at[line_by_role[role]], out_sem.at[role])
        for role in range(8)
    ]

    def product(row_roles):
        for c in range(4):
            left = []
            for role in row_roles:
                base = IX_MATCH + (role * 4 + c) * CAP
                left.append(jnp.concatenate([rows[role][table[base + j]] for j in range(CAP)], axis=1))
            right = columns_panel[c * CAP:(c + 1) * CAP].reshape(CAP * BS, BS)
            total = jnp.dot(
                jnp.concatenate(left, axis=0), right, preferred_element_type=jnp.float32
            )
            q = column_of[c]
            for i, role in enumerate(row_roles):
                line = line_by_role[role]
                kept = jnp.where(filter_mask[q, line] != 0, total[i * BS:(i + 1) * BS], 0.0)
                finished[role, :, pl.ds(pl.multiple_of(q * BS, BS), BS)] = kept.astype(jnp.bfloat16)
        start(*[leaving[role] for role in row_roles])

    product((0, 1))
    product((2, 3))
    for role in (0, 1):
        landed(*f[role])
    product((4, 5))
    for role in (2, 3):
        landed(*f[role])
    product((6, 7))

    trace_step(6)
    occupation[0, 0] = jnp.sum(tacc[7])
    for one in remote:
        one.wait_send()
    for one in leaving:
        one.wait()


def on_device(values, pattern, filter_mask, assignment):
    hbm = pl.BlockSpec(memory_space=pltpu.HBM)
    parts = lambda count: [pltpu.VMEM((count, PART, BS), jnp.bfloat16)] * CHUNKS
    lists = lambda *counts: [pltpu.SMEM((count * LIST,), jnp.int32) for count in counts]

    def path(final):
        return [
            *parts(4 * CAP + 1), *parts(2 * CAP), *parts(CAP), *parts(2 * CAP + 1),
            *parts(2 * CAP + 1), *lists(4, 2, 1, 1, 1, 1, 1, final),
        ]

    product, occupation = pl.pallas_call(
        kernel,
        out_shape=(
            jax.ShapeDtypeStruct((8, BS, 4 * BS), jnp.bfloat16),
            jax.ShapeDtypeStruct((1, 1), jnp.float32),
        ),
        in_specs=[hbm] * 4,
        out_specs=(hbm, pl.BlockSpec(memory_space=pltpu.SMEM)),
        scratch_shapes=[
            pltpu.VMEM((4, 8, BS, BS), jnp.bfloat16),
            pltpu.SMEM((4, 8), jnp.int32),
            pltpu.SMEM((4, 8), jnp.int32),
            pltpu.SMEM((4, 8), jnp.int32),
            pltpu.SMEM((64,), jnp.int32),
            *[pltpu.VMEM((4, 4, PART, BS), jnp.bfloat16)] * CHUNKS,
            *path(4),
            *path(8),
            pltpu.VMEM((4 * CAP, BS, BS), jnp.bfloat16),
            *[pltpu.VMEM((CAP + 1, BS, BS), jnp.bfloat16)] * 8,
            pltpu.VMEM((8, 8, BS), jnp.float32),
            pltpu.VMEM((7, 8, BS), jnp.float32),
            pltpu.VMEM((8, BS, 4 * BS), jnp.bfloat16),
            pltpu.SMEM((IX_MATCH + 8 * 4 * CAP,), jnp.int32),
            pltpu.SemaphoreType.DMA((7,)),
            pltpu.SemaphoreType.DMA((8,)),
            pltpu.SemaphoreType.DMA((COPIES,)),
            pltpu.SemaphoreType.DMA((COPIES,)),
        ],
        compiler_params=pltpu.CompilerParams(
            collective_id=0, has_side_effects=True, vmem_limit_bytes=63 * 1024 * 1024
        ),
        cost_estimate=pl.CostEstimate(
            flops=2 * 192 * BS**3, bytes_accessed=4 * 1024 * 1024, transcendentals=0
        ),
    )(values.reshape(8, BS, 4 * BS), pattern.T, filter_mask.T, assignment)
    return product.reshape(values.shape), occupation[0, 0]


def solution(mesh):
    in_specs = (P("row", "col"), P("row", "col"), P("row", "col"), P())
    out_specs = (P("row", "col"), P())
    return jax.shard_map(
        on_device, mesh=mesh, in_specs=in_specs, out_specs=out_specs, check_vma=False
    )
```

```python
import jax
import jax.numpy as jnp
from jax import lax
from jax.experimental import pallas as pl
from jax.experimental.pallas import tpu as pltpu
from jax.sharding import PartitionSpec as P

BS = 128
CAP = 6
LIST = 128
CHUNKS = 2
PART = BS // CHUNKS
COPIES = 96
IX_C1B, IX_C1O, IX_C2, IX_C3, IX_R1B, IX_R1O, IX_R2, IX_R3 = range(0, 64, 8)
IX_MATCH = 64
MESH = pl.DeviceIdType.MESH


class Path:
    def __init__(self, refs):
        refs = list(refs)
        take = lambda: [refs.pop(0) for _ in range(CHUNKS)]
        self.first, self.send, self.send2 = take(), take(), take()
        self.second, self.third = take(), take()
        (self.l_own, self.l_in1, self.l_send2, self.l_own2, self.l_in2,
         self.l_send3, self.l_in3, self.l_final) = refs


def kernel(values, pattern_in, filter_in, assignment_in, out, occupation, *refs):
    refs = list(refs)
    take = lambda count: [refs.pop(0) for _ in range(count)]
    own, pattern, other_pattern, filter_mask, assignment = take(5)
    other = take(CHUNKS)
    C, R = Path(take(5 * CHUNKS + 8)), Path(take(5 * CHUNKS + 8))
    columns_panel, = take(1)
    rows = take(8)
    tacc, trecv, table, load_sem, send_sem, recv_sem = take(6)

    row, col = lax.axis_index("row"), lax.axis_index("col")
    x, y_hi = row // 2, row % 2
    y_lo, z, core = col // 8, (col // 2) % 4, col % 2

    def partners(position):
        even, odd = position + 1 - 2 * (position % 2), 3 - position
        a = even * (1 - core) + odd * core
        b = odd * (1 - core) + even * core
        return a, b, (position + 2) % 4

    xa, xb, xd = partners(x)
    za, zb, zd = partners(z)
    dev_xa, dev_xb = (xa * 2 + y_hi, col), (xb * 2 + y_hi, col)
    dev_yh = (x * 2 + 1 - y_hi, col)
    dev_za = (row, y_lo * 8 + za * 2 + core)
    dev_zb = (row, y_lo * 8 + zb * 2 + core)
    dev_yl = (row, (1 - y_lo) * 8 + z * 2 + core)
    other_col = col + 1 - 2 * core
    dev_core = (row, other_col)

    remote = []

    def copy(src, dst, device):
        index = len(remote)
        remote.append(pltpu.make_async_remote_copy(
            src_ref=src, dst_ref=dst, send_sem=send_sem.at[index],
            recv_sem=recv_sem.at[index], device_id=device, device_id_type=MESH,
        ))
        return remote[-1]

    def start(*copies):
        for one in copies:
            one.start()

    def landed(*copies):
        for one in copies:
            one.wait_recv()

    small = [
        pltpu.make_async_copy(src, dst, load_sem.at[4 + i])
        for i, (src, dst) in enumerate(
            ((pattern_in, pattern), (assignment_in, assignment), (filter_in, filter_mask))
        )
    ]
    loads = [
        pltpu.make_async_copy(values.at[:, :, q * BS:(q + 1) * BS], own.at[q], load_sem.at[q])
        for q in range(4)
    ]
    start(*small, *loads)
    barrier = pltpu.get_barrier_semaphore()
    for device in (dev_xa, dev_xb, dev_yh, dev_za, dev_zb, dev_yl, dev_core):
        pl.semaphore_signal(barrier, inc=1, device_id=device, device_id_type=MESH)

    zero = jnp.zeros((PART, BS), jnp.bfloat16)
    for path in (C, R):
        for k in range(CHUNKS):
            path.first[k][4 * CAP] = zero
            path.second[k][2 * CAP] = zero
            path.third[k][2 * CAP] = zero
    for ref in rows:
        ref[CAP] = jnp.zeros((BS, BS), jnp.bfloat16)

    def part(k):
        return slice(k * PART, (k + 1) * PART)

    def rank(flags):
        count = jnp.int32(0)
        places = [jnp.int32(0)] * CAP
        for t, flag in enumerate(flags):
            for j in range(min(CAP, t + 1)):
                places[j] = jnp.where((flag != 0) & (count == j), t, places[j])
            count = count + flag
        return places, count

    def rank_column(role, q):
        places, count = rank([pattern[q, t] for t in range(8)])
        C.l_own[role * LIST] = count
        for j in range(CAP):
            name = assignment[row * 8 + places[j]]
            C.l_own[role * LIST + 1 + j] = jnp.where(j < count, name, -1)
        return q, places, count

    def pack_column(ranked, k, dst, first):
        q, places, count = ranked
        for j in range(CAP):
            block = own[q, places[j], part(k), :]
            dst[first + j] = jnp.where(j < count, block, zero)

    for one in small:
        one.wait()
    ranked_columns = [rank_column(role, q) for role, q in enumerate((x, xb, xa, xd))]
    for one in loads:
        one.wait()
    for k in range(CHUNKS):
        pack_column(ranked_columns[2], k, C.send[k], 0)
        pack_column(ranked_columns[3], k, C.send[k], CAP)

    half = (1 - core) * 4
    r0m = copy(pattern, other_pattern, dev_core)
    r0 = [copy(own.at[:, pl.ds(half, 4), part(k)], other[k], dev_core) for k in range(CHUNKS)]

    def first_copies(path, device):
        return (
            copy(path.l_own.at[pl.ds(2 * LIST, 2 * LIST)], path.l_in1, device),
            [copy(path.send[k], path.first[k].at[pl.ds(2 * CAP, 2 * CAP)], device) for k in range(CHUNKS)],
        )

    c1m, c1 = first_copies(C, dev_xa)
    r1m, r1 = first_copies(R, dev_za)

    pl.semaphore_wait(barrier, 7)
    start(r0m, c1m)
    for k in range(CHUNKS):
        start(r0[k], c1[k])
    for k in range(CHUNKS):
        pack_column(ranked_columns[0], k, C.first[k], 0)
        pack_column(ranked_columns[1], k, C.first[k], CAP)

    def rank_row(role, q):
        line = core * 4 + q
        places, count = rank(
            [pattern[t, line] for t in range(4)] + [other_pattern[t, line] for t in range(4)]
        )
        R.l_own[role * LIST] = count
        for j in range(CAP):
            name = jnp.where(places[j] < 4, col * 4, other_col * 4 - 4) + places[j]
            R.l_own[role * LIST + 1 + j] = jnp.where(j < count, name, -1)
        return line, q, places, count

    def pack_row(ranked, k, dst, first):
        line, q, places, count = ranked
        for j in range(CAP):
            mine = places[j] < 4
            place = jnp.where(mine, places[j], places[j] - 4)
            block = jnp.where(mine, own[place, line, part(k), :], other[k][place, q])
            dst[first + j] = jnp.where(j < count, block, zero)

    landed(r0m)
    ranked_rows = [rank_row(role, q) for role, q in enumerate((z, zb, za, zd))]
    start(r1m)
    for k in range(CHUNKS):
        landed(r0[k])
        pack_row(ranked_rows[2], k, R.send[k], 0)
        pack_row(ranked_rows[3], k, R.send[k], CAP)
        start(r1[k])

    def merge(l1, at1, l2, at2, lout, ix, base1, base2, zero_slot):
        n1, n2 = l1[at1], l2[at2]
        lout[0] = n1 + n2
        for j in range(CAP):
            rest = jnp.clip(j - n1, 0, CAP - 1)
            in1, in2 = j < n1, j - n1 < n2
            lout[1 + j] = jnp.where(in1, l1[at1 + 1 + j], jnp.where(in2, l2[at2 + 1 + rest], -1))
            table[ix + j] = jnp.where(in1, base1 + j, jnp.where(in2, base2 + rest, zero_slot))

    def move(src, ix, dst):
        for j in range(CAP):
            dst[j] = src[table[ix + j]]

    def six(ref, k, first=0):
        return ref[k].at[pl.ds(first, CAP)]

    def later_copies(path, device2, device3):
        return (
            copy(path.l_send2, path.l_in2, device2),
            [copy(path.send2[k], six(path.second, k, CAP), device2) for k in range(CHUNKS)],
            copy(path.l_send3, path.l_in3, device3),
            [copy(six(path.third, k), six(path.third, k, CAP), device3) for k in range(CHUNKS)],
        )

    c2m, c2, c3m, c3 = later_copies(C, dev_xb, dev_yh)
    r2m, r2, r3m, r3 = later_copies(R, dev_zb, dev_yl)

    def lists1(path, in_copy, out_copy, ix_b, ix_o):
        landed(in_copy)
        merge(path.l_own, LIST, path.l_in1, LIST, path.l_send2, ix_b, CAP, 3 * CAP, 4 * CAP)
        start(out_copy)
        merge(path.l_own, 0, path.l_in1, 0, path.l_own2, ix_o, 0, 2 * CAP, 4 * CAP)

    def lists2(path, in_copy, out_copy, ix):
        landed(in_copy)
        merge(path.l_own2, 0, path.l_in2, 0, path.l_send3, ix, 0, CAP, 2 * CAP)
        start(out_copy)

    def lists3(path, in_copy, out_copies, ix):
        landed(in_copy)
        merge(path.l_send3, 0, path.l_in3, 0, path.l_final, ix, 0, CAP, 2 * CAP)
        start(*out_copies)

    def blocks1(path, in_copies, out_copies, ix_b, ix_o, k):
        landed(in_copies[k])
        move(path.first[k], ix_b, path.send2[k])
        start(out_copies[k])
        move(path.first[k], ix_o, path.second[k])

    def blocks2(path, in_copies, out_copies, ix, k):
        landed(in_copies[k])
        move(path.second[k], ix, path.third[k])
        start(out_copies[k])

    def names(path, role):
        return path.l_final.at[pl.ds(role * LIST, LIST)]

    c4am, c4bm = copy(names(C, 0), names(C, 2), dev_xa), copy(names(C, 0), names(C, 1), dev_xb)
    c5m = copy(names(C, 1), names(C, 3), dev_xa)
    r4am, r4bm = copy(names(R, 0), names(R, 2), dev_za), copy(names(R, 0), names(R, 1), dev_zb)
    r5m = copy(names(R, 1), names(R, 3), dev_za)
    fm = copy(R.l_final.at[pl.ds(0, 4 * LIST)], R.l_final.at[pl.ds(4 * LIST, 4 * LIST)], dev_core)

    def column(role, k):
        return columns_panel.at[pl.ds(role * CAP, CAP), part(k)]

    def line_of(role, k):
        return rows[role].at[pl.ds(0, CAP), part(k)]

    each = range(CHUNKS)
    c4a = [copy(column(0, k), column(2, k), dev_xa) for k in each]
    c4b = [copy(column(0, k), column(1, k), dev_xb) for k in each]
    c5 = [copy(column(1, k), column(3, k), dev_xa) for k in each]
    r4a = [copy(line_of(0, k), line_of(2, k), dev_za) for k in each]
    r4b = [copy(line_of(0, k), line_of(1, k), dev_zb) for k in each]
    r5 = [copy(line_of(1, k), line_of(3, k), dev_za) for k in each]
    f = [[copy(line_of(role, k), line_of(4 + role, k), dev_core) for k in each] for role in range(4)]

    def blocks3_column(k):
        landed(c3[k])
        for j in range(CAP):
            columns_panel[j, part(k), :] = C.third[k][table[IX_C3 + j]]
        start(c4b[k], c4a[k])

    def blocks3_row(k):
        landed(r3[k])
        for j in range(CAP):
            rows[0][j, part(k), :] = R.third[k][table[IX_R3 + j]]
        start(r4b[k], r4a[k], f[0][k])

    def squares(ref):
        total = jnp.zeros((8, BS), jnp.float32)
        for i in range(2 * CAP):
            block = ref[i].astype(jnp.float32)
            total = total + jnp.sum((block * block).reshape(PART // 8, 8, BS), axis=0)
        return total

    trace_devices = (dev_core, dev_xa, dev_za, dev_xb, dev_zb, dev_yh, dev_yl)
    trace = [copy(tacc.at[i], trecv.at[i], trace_devices[i]) for i in range(7)]

    def trace_step(i):
        landed(trace[i])
        tacc[i + 1] = tacc[i] + trecv[i]
        if i < 6:
            start(trace[i + 1])

    for k in each:
        pack_row(ranked_rows[0], k, R.first[k], 0)
        pack_row(ranked_rows[1], k, R.first[k], CAP)
    total = jnp.zeros((8, BS), jnp.float32)
    for k in each:
        total = total + squares(C.send[k])
        total = total + squares(C.first[k])
    tacc[0] = total
    start(trace[0])

    def match(row_role, carry):
        have = [R.l_final[row_role * LIST + 1 + i] for i in range(CAP)]
        for t in range(4 * CAP):
            wanted = C.l_final[(t // CAP) * LIST + 1 + t % CAP]
            slot = jnp.int32(CAP)
            for i in range(CAP):
                slot = jnp.where(have[i] == wanted, i, slot)
            table[IX_MATCH + row_role * 4 * CAP + t] = slot
        return carry

    def match_rows(first_role):
        lax.fori_loop(first_role, first_role + 4, match, 0)

    row_lag = 0.75
    steps = []
    for k in each:
        steps += [
            (1 + k, lambda k=k: blocks1(C, c1, c2, IX_C1B, IX_C1O, k)),
            (2 + k, lambda k=k: blocks2(C, c2, c3, IX_C2, k)),
            (3 + k, lambda k=k: blocks3_column(k)),
            (4 + k, lambda k=k: (landed(c4b[k]), start(c5[k]))),
            (1 + k + row_lag, lambda k=k: blocks1(R, r1, r2, IX_R1B, IX_R1O, k)),
            (2 + k + row_lag, lambda k=k: blocks2(R, r2, r3, IX_R2, k)),
            (3 + k + row_lag, lambda k=k: blocks3_row(k)),
            (4 + k + row_lag, lambda k=k: (landed(r4b[k]), start(r5[k], f[1][k]))),
            (4.2 + k + row_lag, lambda k=k: (landed(r4a[k]), start(f[2][k]))),
            (5 + k + row_lag, lambda k=k: (landed(r5[k]), start(f[3][k]))),
        ]
    steps += [
        (0.9, lambda: lists1(C, c1m, c2m, IX_C1B, IX_C1O)),
        (1.1, lambda: lists1(R, r1m, r2m, IX_R1B, IX_R1O)),
        (1.3, lambda: lists2(C, c2m, c3m, IX_C2)),
        (1.8, lambda: trace_step(0)),
        (2.1, lambda: lists2(R, r2m, r3m, IX_R2)),
        (2.2, lambda: lists3(C, c3m, (c4bm, c4am), IX_C3)),
        (2.9, lambda: lists3(R, r3m, (r4bm, r4am), IX_R3)),
        (3.1, lambda: trace_step(1)),
        (3.2, lambda: (landed(c4bm), start(c5m))),
        (3.8, lambda: (landed(r4bm), start(r5m))),
        (3.85, lambda: trace_step(2)),
        (4.05, lambda: (landed(r4am, r5m), start(fm))),
        (4.1, lambda: (landed(c4am, c5m), match_rows(0))),
        (4.3, lambda: trace_step(3)),
        (5.05, lambda: (landed(fm), match_rows(4))),
        (5.1, lambda: trace_step(4)),
        (5.85, lambda: trace_step(5)),
    ]
    for _, step in sorted(steps, key=lambda one: one[0]):
        step()

    for k in each:
        landed(c4a[k], c5[k])

    column_of = (x, xb, xa, xd)
    line_by_role = (
        [core * 4 + position for position in (z, zb, za, zd)]
        + [(1 - core) * 4 + position for position in (z, za, zb, zd)]
    )

    def product(row_roles):
        for c in range(4):
            left = []
            for role in row_roles:
                base = IX_MATCH + (role * 4 + c) * CAP
                left.append(jnp.concatenate([rows[role][table[base + j]] for j in range(CAP)], axis=1))
            right = columns_panel[c * CAP:(c + 1) * CAP].reshape(CAP * BS, BS)
            total = jnp.dot(
                jnp.concatenate(left, axis=0), right, preferred_element_type=jnp.float32
            )
            q = column_of[c]
            for i, role in enumerate(row_roles):
                line = line_by_role[role]
                kept = jnp.where(filter_mask[q, line] != 0, total[i * BS:(i + 1) * BS], 0.0)
                out[line, :, pl.ds(pl.multiple_of(q * BS, BS), BS)] = kept.astype(jnp.bfloat16)

    product((0, 1))
    product((2, 3))
    for role in (0, 1):
        landed(*f[role])
    product((4, 5))
    for role in (2, 3):
        landed(*f[role])
    product((6, 7))

    trace_step(6)
    occupation[0, 0] = jnp.sum(tacc[7])
    for one in remote:
        one.wait_send()


def on_device(values, pattern, filter_mask, assignment):
    hbm = pl.BlockSpec(memory_space=pltpu.HBM)
    parts = lambda count: [pltpu.VMEM((count, PART, BS), jnp.bfloat16)] * CHUNKS
    lists = lambda *counts: [pltpu.SMEM((count * LIST,), jnp.int32) for count in counts]

    def path(final):
        return [
            *parts(4 * CAP + 1), *parts(2 * CAP), *parts(CAP), *parts(2 * CAP + 1),
            *parts(2 * CAP + 1), *lists(4, 2, 1, 1, 1, 1, 1, final),
        ]

    product, occupation = pl.pallas_call(
        kernel,
        out_shape=(
            jax.ShapeDtypeStruct((8, BS, 4 * BS), jnp.bfloat16),
            jax.ShapeDtypeStruct((1, 1), jnp.float32),
        ),
        in_specs=[hbm] * 4,
        out_specs=(pl.BlockSpec(memory_space=pltpu.VMEM), pl.BlockSpec(memory_space=pltpu.SMEM)),
        scratch_shapes=[
            pltpu.VMEM((4, 8, BS, BS), jnp.bfloat16),
            pltpu.SMEM((4, 8), jnp.int32),
            pltpu.SMEM((4, 8), jnp.int32),
            pltpu.SMEM((4, 8), jnp.int32),
            pltpu.SMEM((64,), jnp.int32),
            *[pltpu.VMEM((4, 4, PART, BS), jnp.bfloat16)] * CHUNKS,
            *path(4),
            *path(8),
            pltpu.VMEM((4 * CAP, BS, BS), jnp.bfloat16),
            *[pltpu.VMEM((CAP + 1, BS, BS), jnp.bfloat16)] * 8,
            pltpu.VMEM((8, 8, BS), jnp.float32),
            pltpu.VMEM((7, 8, BS), jnp.float32),
            pltpu.SMEM((IX_MATCH + 8 * 4 * CAP,), jnp.int32),
            pltpu.SemaphoreType.DMA((7,)),
            pltpu.SemaphoreType.DMA((COPIES,)),
            pltpu.SemaphoreType.DMA((COPIES,)),
        ],
        compiler_params=pltpu.CompilerParams(
            collective_id=0, has_side_effects=True, vmem_limit_bytes=52 * 1024 * 1024
        ),
        cost_estimate=pl.CostEstimate(
            flops=2 * 192 * BS**3, bytes_accessed=4 * 1024 * 1024, transcendentals=0
        ),
    )(values.reshape(8, BS, 4 * BS), pattern.T, filter_mask.T, assignment)
    return product.reshape(values.shape), occupation[0, 0]


def solution(mesh):
    in_specs = (P("row", "col"), P("row", "col"), P("row", "col"), P())
    out_specs = (P("row", "col"), P())
    return jax.shard_map(
        on_device, mesh=mesh, in_specs=in_specs, out_specs=out_specs, check_vma=False
    )
```

```python
import jax
import jax.numpy as jnp
from jax import lax
from jax.experimental import pallas as pl
from jax.experimental.pallas import tpu as pltpu
from jax.sharding import PartitionSpec as P

BS = 128
CAP = 6
LIST = 128
CHUNKS = 2
PART = BS // CHUNKS
COPIES = 96
IX_C1B, IX_C1O, IX_C2, IX_C3, IX_R1B, IX_R1O, IX_R2, IX_R3 = range(0, 64, 8)
IX_MATCH = 64
MESH = pl.DeviceIdType.MESH


class Path:
    def __init__(self, refs):
        refs = list(refs)
        take = lambda: [refs.pop(0) for _ in range(CHUNKS)]
        self.first, self.send, self.send2 = take(), take(), take()
        self.second, self.third = take(), take()
        (self.l_own, self.l_in1, self.l_send2, self.l_own2, self.l_in2,
         self.l_send3, self.l_in3, self.l_final) = refs


def kernel(values, pattern_in, filter_in, assignment_in, out, occupation, *refs):
    refs = list(refs)
    take = lambda count: [refs.pop(0) for _ in range(count)]
    own, pattern, other_pattern, filter_mask, assignment = take(5)
    other = take(CHUNKS)
    C, R = Path(take(5 * CHUNKS + 8)), Path(take(5 * CHUNKS + 8))
    columns_panel, = take(1)
    rows = take(8)
    tacc, trecv, table, load_sem, send_sem, recv_sem = take(6)

    row, col = lax.axis_index("row"), lax.axis_index("col")
    x, y_hi = row // 2, row % 2
    y_lo, z, core = col // 8, (col // 2) % 4, col % 2

    def partners(position):
        even, odd = position + 1 - 2 * (position % 2), 3 - position
        a = even * (1 - core) + odd * core
        b = odd * (1 - core) + even * core
        return a, b, (position + 2) % 4

    xa, xb, xd = partners(x)
    za, zb, zd = partners(z)
    dev_xa, dev_xb = (xa * 2 + y_hi, col), (xb * 2 + y_hi, col)
    dev_yh = (x * 2 + 1 - y_hi, col)
    dev_za = (row, y_lo * 8 + za * 2 + core)
    dev_zb = (row, y_lo * 8 + zb * 2 + core)
    dev_yl = (row, (1 - y_lo) * 8 + z * 2 + core)
    other_col = col + 1 - 2 * core
    dev_core = (row, other_col)

    remote = []

    def copy(src, dst, device):
        index = len(remote)
        remote.append(pltpu.make_async_remote_copy(
            src_ref=src, dst_ref=dst, send_sem=send_sem.at[index],
            recv_sem=recv_sem.at[index], device_id=device, device_id_type=MESH,
        ))
        return remote[-1]

    def start(*copies):
        for one in copies:
            one.start()

    def landed(*copies):
        for one in copies:
            one.wait_recv()

    small = [
        pltpu.make_async_copy(src, dst, load_sem.at[4 + i])
        for i, (src, dst) in enumerate(
            ((pattern_in, pattern), (assignment_in, assignment), (filter_in, filter_mask))
        )
    ]
    loads = [
        pltpu.make_async_copy(values.at[:, :, q * BS:(q + 1) * BS], own.at[q], load_sem.at[q])
        for q in range(4)
    ]
    start(*small, *loads)
    barrier = pltpu.get_barrier_semaphore()
    for device in (dev_xa, dev_xb, dev_yh, dev_za, dev_zb, dev_yl, dev_core):
        pl.semaphore_signal(barrier, inc=1, device_id=device, device_id_type=MESH)

    zero = jnp.zeros((PART, BS), jnp.bfloat16)
    for path in (C, R):
        for k in range(CHUNKS):
            path.first[k][4 * CAP] = zero
            path.second[k][2 * CAP] = zero
            path.third[k][2 * CAP] = zero
    for ref in rows:
        ref[CAP] = jnp.zeros((BS, BS), jnp.bfloat16)

    def part(k):
        return slice(k * PART, (k + 1) * PART)

    def rank(flags):
        count = jnp.int32(0)
        places = [jnp.int32(0)] * CAP
        for t, flag in enumerate(flags):
            for j in range(min(CAP, t + 1)):
                places[j] = jnp.where((flag != 0) & (count == j), t, places[j])
            count = count + flag
        return places, count

    def rank_column(role, q):
        places, count = rank([pattern[q, t] for t in range(8)])
        C.l_own[role * LIST] = count
        for j in range(CAP):
            name = assignment[row * 8 + places[j]]
            C.l_own[role * LIST + 1 + j] = jnp.where(j < count, name, -1)
        return q, places, count

    def pack_column(ranked, k, dst, first):
        q, places, count = ranked
        for j in range(CAP):
            block = own[q, places[j], part(k), :]
            dst[first + j] = jnp.where(j < count, block, zero)

    for one in small:
        one.wait()
    ranked_columns = [rank_column(role, q) for role, q in enumerate((x, xb, xa, xd))]
    for one in loads:
        one.wait()
    for k in range(CHUNKS):
        pack_column(ranked_columns[2], k, C.send[k], 0)
        pack_column(ranked_columns[3], k, C.send[k], CAP)

    half = (1 - core) * 4
    r0m = copy(pattern, other_pattern, dev_core)
    r0 = [copy(own.at[:, pl.ds(half, 4), part(k)], other[k], dev_core) for k in range(CHUNKS)]

    def first_copies(path, device):
        return (
            copy(path.l_own.at[pl.ds(2 * LIST, 2 * LIST)], path.l_in1, device),
            [copy(path.send[k], path.first[k].at[pl.ds(2 * CAP, 2 * CAP)], device) for k in range(CHUNKS)],
        )

    c1m, c1 = first_copies(C, dev_xa)
    r1m, r1 = first_copies(R, dev_za)

    pl.semaphore_wait(barrier, 7)
    start(r0m, c1m)
    for k in range(CHUNKS):
        start(r0[k], c1[k])
    for k in range(CHUNKS):
        pack_column(ranked_columns[0], k, C.first[k], 0)
        pack_column(ranked_columns[1], k, C.first[k], CAP)

    def rank_row(role, q):
        line = core * 4 + q
        places, count = rank(
            [pattern[t, line] for t in range(4)] + [other_pattern[t, line] for t in range(4)]
        )
        R.l_own[role * LIST] = count
        for j in range(CAP):
            name = jnp.where(places[j] < 4, col * 4, other_col * 4 - 4) + places[j]
            R.l_own[role * LIST + 1 + j] = jnp.where(j < count, name, -1)
        return line, q, places, count

    def pack_row(ranked, k, dst, first):
        line, q, places, count = ranked
        for j in range(CAP):
            mine = places[j] < 4
            place = jnp.where(mine, places[j], places[j] - 4)
            block = jnp.where(mine, own[place, line, part(k), :], other[k][place, q])
            dst[first + j] = jnp.where(j < count, block, zero)

    landed(r0m)
    ranked_rows = [rank_row(role, q) for role, q in enumerate((z, zb, za, zd))]
    start(r1m)
    for k in range(CHUNKS):
        landed(r0[k])
        pack_row(ranked_rows[2], k, R.send[k], 0)
        pack_row(ranked_rows[3], k, R.send[k], CAP)
        start(r1[k])

    def merge(l1, at1, l2, at2, lout, ix, base1, base2, zero_slot):
        n1, n2 = l1[at1], l2[at2]
        lout[0] = n1 + n2
        for j in range(CAP):
            rest = jnp.clip(j - n1, 0, CAP - 1)
            in1, in2 = j < n1, j - n1 < n2
            lout[1 + j] = jnp.where(in1, l1[at1 + 1 + j], jnp.where(in2, l2[at2 + 1 + rest], -1))
            table[ix + j] = jnp.where(in1, base1 + j, jnp.where(in2, base2 + rest, zero_slot))

    def move(src, ix, dst):
        for j in range(CAP):
            dst[j] = src[table[ix + j]]

    def six(ref, k, first=0):
        return ref[k].at[pl.ds(first, CAP)]

    def later_copies(path, device2, device3):
        return (
            copy(path.l_send2, path.l_in2, device2),
            [copy(path.send2[k], six(path.second, k, CAP), device2) for k in range(CHUNKS)],
            copy(path.l_send3, path.l_in3, device3),
            [copy(six(path.third, k), six(path.third, k, CAP), device3) for k in range(CHUNKS)],
        )

    c2m, c2, c3m, c3 = later_copies(C, dev_xb, dev_yh)
    r2m, r2, r3m, r3 = later_copies(R, dev_zb, dev_yl)

    def lists1(path, in_copy, out_copy, ix_b, ix_o):
        landed(in_copy)
        merge(path.l_own, LIST, path.l_in1, LIST, path.l_send2, ix_b, CAP, 3 * CAP, 4 * CAP)
        start(out_copy)
        merge(path.l_own, 0, path.l_in1, 0, path.l_own2, ix_o, 0, 2 * CAP, 4 * CAP)

    def lists2(path, in_copy, out_copy, ix):
        landed(in_copy)
        merge(path.l_own2, 0, path.l_in2, 0, path.l_send3, ix, 0, CAP, 2 * CAP)
        start(out_copy)

    def lists3(path, in_copy, out_copies, ix):
        landed(in_copy)
        merge(path.l_send3, 0, path.l_in3, 0, path.l_final, ix, 0, CAP, 2 * CAP)
        start(*out_copies)

    def blocks1(path, in_copies, out_copies, ix_b, ix_o, k):
        landed(in_copies[k])
        move(path.first[k], ix_b, path.send2[k])
        start(out_copies[k])
        move(path.first[k], ix_o, path.second[k])

    def blocks2(path, in_copies, out_copies, ix, k):
        landed(in_copies[k])
        move(path.second[k], ix, path.third[k])
        start(out_copies[k])

    def names(path, role):
        return path.l_final.at[pl.ds(role * LIST, LIST)]

    c4am, c4bm = copy(names(C, 0), names(C, 2), dev_xa), copy(names(C, 0), names(C, 1), dev_xb)
    c5m = copy(names(C, 1), names(C, 3), dev_xa)
    r4am, r4bm = copy(names(R, 0), names(R, 2), dev_za), copy(names(R, 0), names(R, 1), dev_zb)
    r5m = copy(names(R, 1), names(R, 3), dev_za)
    fm = copy(R.l_final.at[pl.ds(0, 4 * LIST)], R.l_final.at[pl.ds(4 * LIST, 4 * LIST)], dev_core)

    def column(role, k):
        return columns_panel.at[pl.ds(role * CAP, CAP), part(k)]

    def line_of(role, k):
        return rows[role].at[pl.ds(0, CAP), part(k)]

    each = range(CHUNKS)
    c4a = [copy(column(0, k), column(2, k), dev_xa) for k in each]
    c4b = [copy(column(0, k), column(1, k), dev_xb) for k in each]
    c5 = [copy(column(1, k), column(3, k), dev_xa) for k in each]
    r4a = [copy(line_of(0, k), line_of(2, k), dev_za) for k in each]
    r4b = [copy(line_of(0, k), line_of(1, k), dev_zb) for k in each]
    r5 = [copy(line_of(1, k), line_of(3, k), dev_za) for k in each]
    f = [[copy(line_of(role, k), line_of(4 + role, k), dev_core) for k in each] for role in range(4)]

    def blocks3_column(k):
        landed(c3[k])
        for j in range(CAP):
            columns_panel[j, part(k), :] = C.third[k][table[IX_C3 + j]]
        start(c4b[k], c4a[k])

    def blocks3_row(k):
        landed(r3[k])
        for j in range(CAP):
            rows[0][j, part(k), :] = R.third[k][table[IX_R3 + j]]
        start(r4b[k], r4a[k], f[0][k])

    def squares(ref):
        total = jnp.zeros((8, BS), jnp.float32)
        for i in range(2 * CAP):
            block = ref[i].astype(jnp.float32)
            total = total + jnp.sum((block * block).reshape(PART // 8, 8, BS), axis=0)
        return total

    trace_devices = (dev_core, dev_xa, dev_za, dev_xb, dev_zb, dev_yh, dev_yl)
    trace = [copy(tacc.at[i], trecv.at[i], trace_devices[i]) for i in range(7)]

    def trace_step(i):
        landed(trace[i])
        tacc[i + 1] = tacc[i] + trecv[i]
        if i < 6:
            start(trace[i + 1])

    for k in each:
        pack_row(ranked_rows[0], k, R.first[k], 0)
        pack_row(ranked_rows[1], k, R.first[k], CAP)
    total = jnp.zeros((8, BS), jnp.float32)
    for k in each:
        total = total + squares(C.send[k])
        total = total + squares(C.first[k])
    tacc[0] = total
    start(trace[0])

    def match(row_role, carry):
        have = [R.l_final[row_role * LIST + 1 + i] for i in range(CAP)]
        for t in range(4 * CAP):
            wanted = C.l_final[(t // CAP) * LIST + 1 + t % CAP]
            slot = jnp.int32(CAP)
            for i in range(CAP):
                slot = jnp.where(have[i] == wanted, i, slot)
            table[IX_MATCH + row_role * 4 * CAP + t] = slot
        return carry

    def match_rows(first_role):
        lax.fori_loop(first_role, first_role + 4, match, 0)

    done = []

    def sent(*copies):
        for one in copies:
            one.wait_send()
            done.append(one)

    row_lag = 0.75
    steps = []
    for k in each:
        steps += [
            (1 + k, lambda k=k: blocks1(C, c1, c2, IX_C1B, IX_C1O, k)),
            (2 + k, lambda k=k: blocks2(C, c2, c3, IX_C2, k)),
            (3 + k, lambda k=k: blocks3_column(k)),
            (4 + k, lambda k=k: (landed(c4b[k]), start(c5[k]))),
            (1 + k + row_lag, lambda k=k: blocks1(R, r1, r2, IX_R1B, IX_R1O, k)),
            (2 + k + row_lag, lambda k=k: blocks2(R, r2, r3, IX_R2, k)),
            (3 + k + row_lag, lambda k=k: blocks3_row(k)),
            (4 + k + row_lag, lambda k=k: (landed(r4b[k]), start(r5[k], f[1][k]))),
            (4.2 + k + row_lag, lambda k=k: (landed(r4a[k]), start(f[2][k]))),
            (5 + k + row_lag, lambda k=k: (landed(r5[k]), start(f[3][k]))),
        ]
    steps += [
        (0.9, lambda: lists1(C, c1m, c2m, IX_C1B, IX_C1O)),
        (1.1, lambda: lists1(R, r1m, r2m, IX_R1B, IX_R1O)),
        (1.3, lambda: lists2(C, c2m, c3m, IX_C2)),
        (1.8, lambda: trace_step(0)),
        (2.1, lambda: lists2(R, r2m, r3m, IX_R2)),
        (2.2, lambda: lists3(C, c3m, (c4bm, c4am), IX_C3)),
        (2.9, lambda: lists3(R, r3m, (r4bm, r4am), IX_R3)),
        (3.1, lambda: trace_step(1)),
        (3.2, lambda: (landed(c4bm), start(c5m))),
        (3.8, lambda: (landed(r4bm), start(r5m))),
        (3.85, lambda: trace_step(2)),
        (4.05, lambda: (landed(r4am, r5m), start(fm))),
        (4.1, lambda: (landed(c4am, c5m), match_rows(0))),
        (4.3, lambda: trace_step(3)),
        (5.05, lambda: (landed(fm), match_rows(4))),
        (5.1, lambda: trace_step(4)),
        (5.5, lambda: sent(c1m, *c1, r0m, *r0, r1m, *r1, c2m, *c2, r2m, *r2)),
        (5.85, lambda: trace_step(5)),
    ]
    for _, step in sorted(steps, key=lambda one: one[0]):
        step()

    for k in each:
        landed(c4a[k], c5[k])

    column_of = (x, xb, xa, xd)
    line_by_role = (
        [core * 4 + position for position in (z, zb, za, zd)]
        + [(1 - core) * 4 + position for position in (z, za, zb, zd)]
    )

    def product(row_roles):
        for c in range(4):
            left = []
            for role in row_roles:
                base = IX_MATCH + (role * 4 + c) * CAP
                left.append(jnp.concatenate([rows[role][table[base + j]] for j in range(CAP)], axis=1))
            right = columns_panel[c * CAP:(c + 1) * CAP].reshape(CAP * BS, BS)
            total = jnp.dot(
                jnp.concatenate(left, axis=0), right, preferred_element_type=jnp.float32
            )
            q = column_of[c]
            for i, role in enumerate(row_roles):
                line = line_by_role[role]
                kept = jnp.where(filter_mask[q, line] != 0, total[i * BS:(i + 1) * BS], 0.0)
                out[line, :, pl.ds(pl.multiple_of(q * BS, BS), BS)] = kept.astype(jnp.bfloat16)

    product((0, 1))
    product((2, 3))
    for role in (0, 1):
        landed(*f[role])
    product((4, 5))
    sent(c3m, *c3, r3m, *r3, c4am, c4bm, r4am, r4bm, c5m, r5m, fm, *c4b, *trace[:5])
    for role in (2, 3):
        landed(*f[role])
    product((6, 7))

    trace_step(6)
    occupation[0, 0] = jnp.sum(tacc[7])
    for one in remote:
        if not any(one is other_one for other_one in done):
            one.wait_send()


def on_device(values, pattern, filter_mask, assignment):
    hbm = pl.BlockSpec(memory_space=pltpu.HBM)
    parts = lambda count: [pltpu.VMEM((count, PART, BS), jnp.bfloat16)] * CHUNKS
    lists = lambda *counts: [pltpu.SMEM((count * LIST,), jnp.int32) for count in counts]

    def path(final):
        return [
            *parts(4 * CAP + 1), *parts(2 * CAP), *parts(CAP), *parts(2 * CAP + 1),
            *parts(2 * CAP + 1), *lists(4, 2, 1, 1, 1, 1, 1, final),
        ]

    product, occupation = pl.pallas_call(
        kernel,
        out_shape=(
            jax.ShapeDtypeStruct((8, BS, 4 * BS), jnp.bfloat16),
            jax.ShapeDtypeStruct((1, 1), jnp.float32),
        ),
        in_specs=[hbm] * 4,
        out_specs=(pl.BlockSpec(memory_space=pltpu.VMEM), pl.BlockSpec(memory_space=pltpu.SMEM)),
        scratch_shapes=[
            pltpu.VMEM((4, 8, BS, BS), jnp.bfloat16),
            pltpu.SMEM((4, 8), jnp.int32),
            pltpu.SMEM((4, 8), jnp.int32),
            pltpu.SMEM((4, 8), jnp.int32),
            pltpu.SMEM((64,), jnp.int32),
            *[pltpu.VMEM((4, 4, PART, BS), jnp.bfloat16)] * CHUNKS,
            *path(4),
            *path(8),
            pltpu.VMEM((4 * CAP, BS, BS), jnp.bfloat16),
            *[pltpu.VMEM((CAP + 1, BS, BS), jnp.bfloat16)] * 8,
            pltpu.VMEM((8, 8, BS), jnp.float32),
            pltpu.VMEM((7, 8, BS), jnp.float32),
            pltpu.SMEM((IX_MATCH + 8 * 4 * CAP,), jnp.int32),
            pltpu.SemaphoreType.DMA((7,)),
            pltpu.SemaphoreType.DMA((COPIES,)),
            pltpu.SemaphoreType.DMA((COPIES,)),
        ],
        compiler_params=pltpu.CompilerParams(
            collective_id=0, has_side_effects=True, vmem_limit_bytes=52 * 1024 * 1024
        ),
        cost_estimate=pl.CostEstimate(
            flops=2 * 192 * BS**3, bytes_accessed=4 * 1024 * 1024, transcendentals=0
        ),
    )(values.reshape(8, BS, 4 * BS), pattern.T, filter_mask.T, assignment)
    return product.reshape(values.shape), occupation[0, 0]


def solution(mesh):
    in_specs = (P("row", "col"), P("row", "col"), P("row", "col"), P())
    out_specs = (P("row", "col"), P())
    return jax.shard_map(
        on_device, mesh=mesh, in_specs=in_specs, out_specs=out_specs, check_vma=False
    )
```

```python
import jax
import jax.numpy as jnp
from jax import lax
from jax.experimental import pallas as pl
from jax.experimental.pallas import tpu as pltpu
from jax.sharding import PartitionSpec as P

BS = 128
CAP = 6
LIST = 128
CHUNKS = 2
PART = BS // CHUNKS
COPIES = 96
IX_C1B, IX_C1O, IX_C2, IX_C3, IX_R1B, IX_R1O, IX_R2, IX_R3 = range(0, 64, 8)
IX_MATCH = 64
MESH = pl.DeviceIdType.MESH


class Path:
    def __init__(self, refs):
        refs = list(refs)
        take = lambda: [refs.pop(0) for _ in range(CHUNKS)]
        self.first, self.send, self.send2 = take(), take(), take()
        self.second, self.third = take(), take()
        (self.l_own, self.l_in1, self.l_send2, self.l_own2, self.l_in2,
         self.l_send3, self.l_in3, self.l_final) = refs


def kernel(values, pattern_in, filter_in, assignment_in, out, occupation, *refs):
    refs = list(refs)
    take = lambda count: [refs.pop(0) for _ in range(count)]
    own, pattern, other_pattern, filter_mask, assignment = take(5)
    other = take(CHUNKS)
    C, R = Path(take(5 * CHUNKS + 8)), Path(take(5 * CHUNKS + 8))
    columns_panel, = take(1)
    rows = take(8)
    tacc, trecv, table, load_sem, send_sem, recv_sem = take(6)

    row, col = lax.axis_index("row"), lax.axis_index("col")
    x, y_hi = row // 2, row % 2
    y_lo, z, core = col // 8, (col // 2) % 4, col % 2

    def partners(position):
        even, odd = position + 1 - 2 * (position % 2), 3 - position
        a = even * (1 - core) + odd * core
        b = odd * (1 - core) + even * core
        return a, b, (position + 2) % 4

    xa, xb, xd = partners(x)
    za, zb, zd = partners(z)
    dev_xa, dev_xb = (xa * 2 + y_hi, col), (xb * 2 + y_hi, col)
    dev_yh = (x * 2 + 1 - y_hi, col)
    dev_za = (row, y_lo * 8 + za * 2 + core)
    dev_zb = (row, y_lo * 8 + zb * 2 + core)
    dev_yl = (row, (1 - y_lo) * 8 + z * 2 + core)
    other_col = col + 1 - 2 * core
    dev_core = (row, other_col)

    remote = []

    def copy(src, dst, device):
        index = len(remote)
        remote.append(pltpu.make_async_remote_copy(
            src_ref=src, dst_ref=dst, send_sem=send_sem.at[index],
            recv_sem=recv_sem.at[index], device_id=device, device_id_type=MESH,
        ))
        return remote[-1]

    def start(*copies):
        for one in copies:
            one.start()

    def landed(*copies):
        for one in copies:
            one.wait_recv()

    small = [
        pltpu.make_async_copy(src, dst, load_sem.at[4 + i])
        for i, (src, dst) in enumerate(
            ((pattern_in, pattern), (assignment_in, assignment), (filter_in, filter_mask))
        )
    ]
    loads = [
        pltpu.make_async_copy(values.at[:, :, q * BS:(q + 1) * BS], own.at[q], load_sem.at[q])
        for q in range(4)
    ]
    start(*small, *loads)
    barrier = pltpu.get_barrier_semaphore()
    for device in (dev_xa, dev_xb, dev_yh, dev_za, dev_zb, dev_yl, dev_core):
        pl.semaphore_signal(barrier, inc=1, device_id=device, device_id_type=MESH)

    zero = jnp.zeros((PART, BS), jnp.bfloat16)
    for path in (C, R):
        for k in range(CHUNKS):
            path.first[k][4 * CAP] = zero
            path.second[k][2 * CAP] = zero
            path.third[k][2 * CAP] = zero
    for ref in rows:
        ref[CAP] = jnp.zeros((BS, BS), jnp.bfloat16)

    def part(k):
        return slice(k * PART, (k + 1) * PART)

    def rank(flags):
        count = jnp.int32(0)
        places = [jnp.int32(0)] * CAP
        for t, flag in enumerate(flags):
            for j in range(min(CAP, t + 1)):
                places[j] = jnp.where((flag != 0) & (count == j), t, places[j])
            count = count + flag
        return places, count

    def rank_column(role, q):
        places, count = rank([pattern[q, t] for t in range(8)])
        C.l_own[role * LIST] = count
        for j in range(CAP):
            name = assignment[row * 8 + places[j]]
            C.l_own[role * LIST + 1 + j] = jnp.where(j < count, name, -1)
        return q, places, count

    def pack_column(ranked, k, dst, first):
        q, places, count = ranked
        for j in range(CAP):
            block = own[q, places[j], part(k), :]
            dst[first + j] = jnp.where(j < count, block, zero)

    for one in small:
        one.wait()
    ranked_columns = [rank_column(role, q) for role, q in enumerate((x, xb, xa, xd))]
    for one in loads:
        one.wait()
    half = (1 - core) * 4
    r0m = copy(pattern, other_pattern, dev_core)
    r0 = [copy(own.at[:, pl.ds(half, 4), part(k)], other[k], dev_core) for k in range(CHUNKS)]

    def first_copies(path, device):
        return (
            copy(path.l_own.at[pl.ds(2 * LIST, 2 * LIST)], path.l_in1, device),
            [copy(path.send[k], path.first[k].at[pl.ds(2 * CAP, 2 * CAP)], device) for k in range(CHUNKS)],
        )

    c1m, c1 = first_copies(C, dev_xa)
    r1m, r1 = first_copies(R, dev_za)

    pl.semaphore_wait(barrier, 7)
    start(r0m, *r0, c1m)
    for k in range(CHUNKS):
        pack_column(ranked_columns[2], k, C.send[k], 0)
        pack_column(ranked_columns[3], k, C.send[k], CAP)
        start(c1[k])
    for k in range(CHUNKS):
        pack_column(ranked_columns[0], k, C.first[k], 0)
        pack_column(ranked_columns[1], k, C.first[k], CAP)

    def rank_row(role, q):
        line = core * 4 + q
        places, count = rank(
            [pattern[t, line] for t in range(4)] + [other_pattern[t, line] for t in range(4)]
        )
        R.l_own[role * LIST] = count
        for j in range(CAP):
            name = jnp.where(places[j] < 4, col * 4, other_col * 4 - 4) + places[j]
            R.l_own[role * LIST + 1 + j] = jnp.where(j < count, name, -1)
        return line, q, places, count

    def pack_row(ranked, k, dst, first):
        line, q, places, count = ranked
        for j in range(CAP):
            mine = places[j] < 4
            place = jnp.where(mine, places[j], places[j] - 4)
            block = jnp.where(mine, own[place, line, part(k), :], other[k][place, q])
            dst[first + j] = jnp.where(j < count, block, zero)

    landed(r0m)
    ranked_rows = {role: rank_row(role, q) for role, q in ((2, za), (3, zd))}
    start(r1m)
    for k in range(CHUNKS):
        landed(r0[k])
        pack_row(ranked_rows[2], k, R.send[k], 0)
        pack_row(ranked_rows[3], k, R.send[k], CAP)
        start(r1[k])

    def merge(l1, at1, l2, at2, lout, ix, base1, base2, zero_slot):
        n1, n2 = l1[at1], l2[at2]
        lout[0] = n1 + n2
        for j in range(CAP):
            rest = jnp.clip(j - n1, 0, CAP - 1)
            in1, in2 = j < n1, j - n1 < n2
            lout[1 + j] = jnp.where(in1, l1[at1 + 1 + j], jnp.where(in2, l2[at2 + 1 + rest], -1))
            table[ix + j] = jnp.where(in1, base1 + j, jnp.where(in2, base2 + rest, zero_slot))

    def move(src, ix, dst):
        for j in range(CAP):
            dst[j] = src[table[ix + j]]

    def six(ref, k, first=0):
        return ref[k].at[pl.ds(first, CAP)]

    def later_copies(path, device2, device3):
        return (
            copy(path.l_send2, path.l_in2, device2),
            [copy(path.send2[k], six(path.second, k, CAP), device2) for k in range(CHUNKS)],
            copy(path.l_send3, path.l_in3, device3),
            [copy(six(path.third, k), six(path.third, k, CAP), device3) for k in range(CHUNKS)],
        )

    c2m, c2, c3m, c3 = later_copies(C, dev_xb, dev_yh)
    r2m, r2, r3m, r3 = later_copies(R, dev_zb, dev_yl)

    def lists1(path, in_copy, out_copy, ix_b, ix_o):
        landed(in_copy)
        merge(path.l_own, LIST, path.l_in1, LIST, path.l_send2, ix_b, CAP, 3 * CAP, 4 * CAP)
        start(out_copy)
        merge(path.l_own, 0, path.l_in1, 0, path.l_own2, ix_o, 0, 2 * CAP, 4 * CAP)

    def lists2(path, in_copy, out_copy, ix):
        landed(in_copy)
        merge(path.l_own2, 0, path.l_in2, 0, path.l_send3, ix, 0, CAP, 2 * CAP)
        start(out_copy)

    def lists3(path, in_copy, out_copies, ix):
        landed(in_copy)
        merge(path.l_send3, 0, path.l_in3, 0, path.l_final, ix, 0, CAP, 2 * CAP)
        start(*out_copies)

    def blocks1(path, in_copies, out_copies, ix_b, ix_o, k):
        landed(in_copies[k])
        move(path.first[k], ix_b, path.send2[k])
        start(out_copies[k])
        move(path.first[k], ix_o, path.second[k])

    def blocks2(path, in_copies, out_copies, ix, k):
        landed(in_copies[k])
        move(path.second[k], ix, path.third[k])
        start(out_copies[k])

    def names(path, role):
        return path.l_final.at[pl.ds(role * LIST, LIST)]

    c4am, c4bm = copy(names(C, 0), names(C, 2), dev_xa), copy(names(C, 0), names(C, 1), dev_xb)
    c5m = copy(names(C, 1), names(C, 3), dev_xa)
    r4am, r4bm = copy(names(R, 0), names(R, 2), dev_za), copy(names(R, 0), names(R, 1), dev_zb)
    r5m = copy(names(R, 1), names(R, 3), dev_za)
    fm = copy(R.l_final.at[pl.ds(0, 4 * LIST)], R.l_final.at[pl.ds(4 * LIST, 4 * LIST)], dev_core)

    def column(role, k):
        return columns_panel.at[pl.ds(role * CAP, CAP), part(k)]

    def line_of(role, k):
        return rows[role].at[pl.ds(0, CAP), part(k)]

    each = range(CHUNKS)
    c4a = [copy(column(0, k), column(2, k), dev_xa) for k in each]
    c4b = [copy(column(0, k), column(1, k), dev_xb) for k in each]
    c5 = [copy(column(1, k), column(3, k), dev_xa) for k in each]
    r4a = [copy(line_of(0, k), line_of(2, k), dev_za) for k in each]
    r4b = [copy(line_of(0, k), line_of(1, k), dev_zb) for k in each]
    r5 = [copy(line_of(1, k), line_of(3, k), dev_za) for k in each]
    f = [[copy(line_of(role, k), line_of(4 + role, k), dev_core) for k in each] for role in range(4)]

    def blocks3_column(k):
        landed(c3[k])
        for j in range(CAP):
            columns_panel[j, part(k), :] = C.third[k][table[IX_C3 + j]]
        start(c4b[k], c4a[k])

    def blocks3_row(k):
        landed(r3[k])
        for j in range(CAP):
            rows[0][j, part(k), :] = R.third[k][table[IX_R3 + j]]
        start(r4b[k], r4a[k], f[0][k])

    def squares(ref):
        total = jnp.zeros((8, BS), jnp.float32)
        for i in range(2 * CAP):
            block = ref[i].astype(jnp.float32)
            total = total + jnp.sum((block * block).reshape(PART // 8, 8, BS), axis=0)
        return total

    trace_devices = (dev_core, dev_xa, dev_za, dev_xb, dev_zb, dev_yh, dev_yl)
    trace = [copy(tacc.at[i], trecv.at[i], trace_devices[i]) for i in range(7)]

    def trace_step(i):
        landed(trace[i])
        tacc[i + 1] = tacc[i] + trecv[i]
        if i < 6:
            start(trace[i + 1])

    def own_rows():
        ranked_rows.update({role: rank_row(role, q) for role, q in ((0, z), (1, zb))})
        for k in each:
            pack_row(ranked_rows[0], k, R.first[k], 0)
            pack_row(ranked_rows[1], k, R.first[k], CAP)

    def begin_trace():
        total = jnp.zeros((8, BS), jnp.float32)
        for k in each:
            total = total + squares(C.send[k])
            total = total + squares(C.first[k])
        tacc[0] = total
        start(trace[0])

    def match(row_role, carry):
        have = [R.l_final[row_role * LIST + 1 + i] for i in range(CAP)]
        for t in range(4 * CAP):
            wanted = C.l_final[(t // CAP) * LIST + 1 + t % CAP]
            slot = jnp.int32(CAP)
            for i in range(CAP):
                slot = jnp.where(have[i] == wanted, i, slot)
            table[IX_MATCH + row_role * 4 * CAP + t] = slot
        return carry

    def match_rows(first_role):
        lax.fori_loop(first_role, first_role + 4, match, 0)

    done = []

    def sent(*copies):
        for one in copies:
            one.wait_send()
            done.append(one)

    row_lag = 0.75
    steps = []
    for k in each:
        steps += [
            (1 + k, lambda k=k: blocks1(C, c1, c2, IX_C1B, IX_C1O, k)),
            (2 + k, lambda k=k: blocks2(C, c2, c3, IX_C2, k)),
            (3 + k, lambda k=k: blocks3_column(k)),
            (4 + k, lambda k=k: (landed(c4b[k]), start(c5[k]))),
            (1 + k + row_lag, lambda k=k: blocks1(R, r1, r2, IX_R1B, IX_R1O, k)),
            (2 + k + row_lag, lambda k=k: blocks2(R, r2, r3, IX_R2, k)),
            (3 + k + row_lag, lambda k=k: blocks3_row(k)),
            (4 + k + row_lag, lambda k=k: (landed(r4b[k]), start(r5[k], f[1][k]))),
            (4.2 + k + row_lag, lambda k=k: (landed(r4a[k]), start(f[2][k]))),
            (5 + k + row_lag, lambda k=k: (landed(r5[k]), start(f[3][k]))),
        ]
    steps += [
        (0.9, lambda: lists1(C, c1m, c2m, IX_C1B, IX_C1O)),
        (1.05, lambda: own_rows()),
        (1.1, lambda: lists1(R, r1m, r2m, IX_R1B, IX_R1O)),
        (1.76, lambda: begin_trace()),
        (1.3, lambda: lists2(C, c2m, c3m, IX_C2)),
        (2.05, lambda: trace_step(0)),
        (2.1, lambda: lists2(R, r2m, r3m, IX_R2)),
        (2.2, lambda: lists3(C, c3m, (c4bm, c4am), IX_C3)),
        (2.9, lambda: lists3(R, r3m, (r4bm, r4am), IX_R3)),
        (3.1, lambda: trace_step(1)),
        (3.2, lambda: (landed(c4bm), start(c5m))),
        (3.8, lambda: (landed(r4bm), start(r5m))),
        (3.85, lambda: trace_step(2)),
        (4.05, lambda: (landed(r4am, r5m), start(fm))),
        (4.1, lambda: (landed(c4am, c5m), match_rows(0))),
        (4.3, lambda: trace_step(3)),
        (5.05, lambda: (landed(fm), match_rows(4))),
        (5.1, lambda: trace_step(4)),
        (5.5, lambda: sent(c1m, *c1, r0m, *r0, r1m, *r1, c2m, *c2, r2m, *r2)),
        (5.85, lambda: trace_step(5)),
    ]
    for _, step in sorted(steps, key=lambda one: one[0]):
        step()

    for k in each:
        landed(c4a[k], c5[k])

    column_of = (x, xb, xa, xd)
    line_by_role = (
        [core * 4 + position for position in (z, zb, za, zd)]
        + [(1 - core) * 4 + position for position in (z, za, zb, zd)]
    )

    def product(row_roles):
        for c in range(4):
            left = []
            for role in row_roles:
                base = IX_MATCH + (role * 4 + c) * CAP
                left.append(jnp.concatenate([rows[role][table[base + j]] for j in range(CAP)], axis=1))
            right = columns_panel[c * CAP:(c + 1) * CAP].reshape(CAP * BS, BS)
            total = jnp.dot(
                jnp.concatenate(left, axis=0), right, preferred_element_type=jnp.float32
            )
            q = column_of[c]
            for i, role in enumerate(row_roles):
                line = line_by_role[role]
                kept = jnp.where(filter_mask[q, line] != 0, total[i * BS:(i + 1) * BS], 0.0)
                out[line, :, pl.ds(pl.multiple_of(q * BS, BS), BS)] = kept.astype(jnp.bfloat16)

    product((0, 1))
    product((2, 3))
    for role in (0, 1):
        landed(*f[role])
    product((4, 5))
    sent(c3m, *c3, r3m, *r3, c4am, c4bm, r4am, r4bm, c5m, r5m, fm, *c4b, *trace[:5])
    for role in (2, 3):
        landed(*f[role])
    product((6, 7))

    trace_step(6)
    occupation[0, 0] = jnp.sum(tacc[7])
    for one in remote:
        if not any(one is other_one for other_one in done):
            one.wait_send()


def on_device(values, pattern, filter_mask, assignment):
    hbm = pl.BlockSpec(memory_space=pltpu.HBM)
    parts = lambda count: [pltpu.VMEM((count, PART, BS), jnp.bfloat16)] * CHUNKS
    lists = lambda *counts: [pltpu.SMEM((count * LIST,), jnp.int32) for count in counts]

    def path(final):
        return [
            *parts(4 * CAP + 1), *parts(2 * CAP), *parts(CAP), *parts(2 * CAP + 1),
            *parts(2 * CAP + 1), *lists(4, 2, 1, 1, 1, 1, 1, final),
        ]

    product, occupation = pl.pallas_call(
        kernel,
        out_shape=(
            jax.ShapeDtypeStruct((8, BS, 4 * BS), jnp.bfloat16),
            jax.ShapeDtypeStruct((1, 1), jnp.float32),
        ),
        in_specs=[hbm] * 4,
        out_specs=(pl.BlockSpec(memory_space=pltpu.VMEM), pl.BlockSpec(memory_space=pltpu.SMEM)),
        scratch_shapes=[
            pltpu.VMEM((4, 8, BS, BS), jnp.bfloat16),
            pltpu.SMEM((4, 8), jnp.int32),
            pltpu.SMEM((4, 8), jnp.int32),
            pltpu.SMEM((4, 8), jnp.int32),
            pltpu.SMEM((64,), jnp.int32),
            *[pltpu.VMEM((4, 4, PART, BS), jnp.bfloat16)] * CHUNKS,
            *path(4),
            *path(8),
            pltpu.VMEM((4 * CAP, BS, BS), jnp.bfloat16),
            *[pltpu.VMEM((CAP + 1, BS, BS), jnp.bfloat16)] * 8,
            pltpu.VMEM((8, 8, BS), jnp.float32),
            pltpu.VMEM((7, 8, BS), jnp.float32),
            pltpu.SMEM((IX_MATCH + 8 * 4 * CAP,), jnp.int32),
            pltpu.SemaphoreType.DMA((7,)),
            pltpu.SemaphoreType.DMA((COPIES,)),
            pltpu.SemaphoreType.DMA((COPIES,)),
        ],
        compiler_params=pltpu.CompilerParams(
            collective_id=0, has_side_effects=True, vmem_limit_bytes=52 * 1024 * 1024
        ),
        cost_estimate=pl.CostEstimate(
            flops=2 * 192 * BS**3, bytes_accessed=4 * 1024 * 1024, transcendentals=0
        ),
    )(values.reshape(8, BS, 4 * BS), pattern.T, filter_mask.T, assignment)
    return product.reshape(values.shape), occupation[0, 0]


def solution(mesh):
    in_specs = (P("row", "col"), P("row", "col"), P("row", "col"), P())
    out_specs = (P("row", "col"), P())
    return jax.shard_map(
        on_device, mesh=mesh, in_specs=in_specs, out_specs=out_specs, check_vma=False
    )
```

```python
import jax
import jax.numpy as jnp
from jax import lax
from jax.experimental import pallas as pl
from jax.experimental.pallas import tpu as pltpu
from jax.sharding import PartitionSpec as P

BS = 128
CAP = 6
LIST = 128
CHUNKS = 2
PART = BS // CHUNKS
COPIES = 96
IX_C1B, IX_C1O, IX_C2, IX_C3, IX_R1B, IX_R1O, IX_R2, IX_R3 = range(0, 64, 8)
IX_MATCH = 64
MESH = pl.DeviceIdType.MESH


class Path:
    def __init__(self, refs):
        refs = list(refs)
        take = lambda: [refs.pop(0) for _ in range(CHUNKS)]
        self.first, self.send, self.send2 = take(), take(), take()
        self.second, self.third = take(), take()
        (self.l_own, self.l_in1, self.l_send2, self.l_own2, self.l_in2,
         self.l_send3, self.l_in3, self.l_final) = refs


def kernel(values, pattern_in, filter_in, assignment_in, out, occupation, *refs):
    refs = list(refs)
    take = lambda count: [refs.pop(0) for _ in range(count)]
    own, pattern, other_pattern, filter_mask, assignment = take(5)
    other = take(CHUNKS)
    C, R = Path(take(5 * CHUNKS + 8)), Path(take(5 * CHUNKS + 8))
    columns_panel, = take(1)
    rows = take(8)
    tacc, trecv, table, load_sem, send_sem, recv_sem = take(6)

    row, col = lax.axis_index("row"), lax.axis_index("col")
    x, y_hi = row // 2, row % 2
    y_lo, z, core = col // 8, (col // 2) % 4, col % 2

    def partners(position):
        even, odd = position + 1 - 2 * (position % 2), 3 - position
        a = even * (1 - core) + odd * core
        b = odd * (1 - core) + even * core
        return a, b, (position + 2) % 4

    xa, xb, xd = partners(x)
    za, zb, zd = partners(z)
    dev_xa, dev_xb = (xa * 2 + y_hi, col), (xb * 2 + y_hi, col)
    dev_yh = (x * 2 + 1 - y_hi, col)
    dev_za = (row, y_lo * 8 + za * 2 + core)
    dev_zb = (row, y_lo * 8 + zb * 2 + core)
    dev_yl = (row, (1 - y_lo) * 8 + z * 2 + core)
    other_col = col + 1 - 2 * core
    dev_core = (row, other_col)

    remote = []

    def copy(src, dst, device):
        index = len(remote)
        remote.append(pltpu.make_async_remote_copy(
            src_ref=src, dst_ref=dst, send_sem=send_sem.at[index],
            recv_sem=recv_sem.at[index], device_id=device, device_id_type=MESH,
        ))
        return remote[-1]

    def start(*copies):
        for one in copies:
            one.start()

    def landed(*copies):
        for one in copies:
            one.wait_recv()

    small = [
        pltpu.make_async_copy(src, dst, load_sem.at[4 + i])
        for i, (src, dst) in enumerate(
            ((pattern_in, pattern), (assignment_in, assignment), (filter_in, filter_mask))
        )
    ]
    loads = [
        pltpu.make_async_copy(values.at[:, :, q * BS:(q + 1) * BS], own.at[q], load_sem.at[q])
        for q in range(4)
    ]
    start(*small, *loads)
    barrier = pltpu.get_barrier_semaphore()
    for device in (dev_xa, dev_xb, dev_yh, dev_za, dev_zb, dev_yl, dev_core):
        pl.semaphore_signal(barrier, inc=1, device_id=device, device_id_type=MESH)

    zero = jnp.zeros((PART, BS), jnp.bfloat16)
    for path in (C, R):
        for k in range(CHUNKS):
            path.first[k][4 * CAP] = zero
            path.second[k][2 * CAP] = zero
            path.third[k][2 * CAP] = zero
    for ref in rows:
        ref[CAP] = jnp.zeros((BS, BS), jnp.bfloat16)

    def part(k):
        return slice(k * PART, (k + 1) * PART)

    def rank(flags):
        count = jnp.int32(0)
        places = [jnp.int32(0)] * CAP
        for t, flag in enumerate(flags):
            for j in range(min(CAP, t + 1)):
                places[j] = jnp.where((flag != 0) & (count == j), t, places[j])
            count = count + flag
        return places, count

    def rank_column(role, q):
        places, count = rank([pattern[q, t] for t in range(8)])
        C.l_own[role * LIST] = count
        for j in range(CAP):
            name = assignment[row * 8 + places[j]]
            C.l_own[role * LIST + 1 + j] = jnp.where(j < count, name, -1)
        return q, places, count

    def pack_column(ranked, k, dst, first):
        q, places, count = ranked
        for j in range(CAP):
            block = own[q, places[j], part(k), :]
            dst[first + j] = jnp.where(j < count, block, zero)

    for one in small:
        one.wait()
    ranked_columns = [rank_column(role, q) for role, q in enumerate((x, xb, xa, xd))]
    for one in loads:
        one.wait()
    for k in range(CHUNKS):
        pack_column(ranked_columns[2], k, C.send[k], 0)
        pack_column(ranked_columns[3], k, C.send[k], CAP)

    half = (1 - core) * 4
    r0m = copy(pattern, other_pattern, dev_core)
    r0 = [copy(own.at[:, pl.ds(half, 4), part(k)], other[k], dev_core) for k in range(CHUNKS)]

    def first_copies(path, device):
        return (
            copy(path.l_own.at[pl.ds(2 * LIST, 2 * LIST)], path.l_in1, device),
            [copy(path.send[k], path.first[k].at[pl.ds(2 * CAP, 2 * CAP)], device) for k in range(CHUNKS)],
        )

    c1m, c1 = first_copies(C, dev_xa)
    r1m, r1 = first_copies(R, dev_za)

    pl.semaphore_wait(barrier, 7)
    start(r0m, c1m)
    for k in range(CHUNKS):
        start(r0[k], c1[k])
    for k in range(CHUNKS):
        pack_column(ranked_columns[0], k, C.first[k], 0)
        pack_column(ranked_columns[1], k, C.first[k], CAP)

    def rank_row(role, q):
        line = core * 4 + q
        places, count = rank(
            [pattern[t, line] for t in range(4)] + [other_pattern[t, line] for t in range(4)]
        )
        R.l_own[role * LIST] = count
        for j in range(CAP):
            name = jnp.where(places[j] < 4, col * 4, other_col * 4 - 4) + places[j]
            R.l_own[role * LIST + 1 + j] = jnp.where(j < count, name, -1)
        return line, q, places, count

    def pack_row(ranked, k, dst, first):
        line, q, places, count = ranked
        for j in range(CAP):
            mine = places[j] < 4
            place = jnp.where(mine, places[j], places[j] - 4)
            block = jnp.where(mine, own[place, line, part(k), :], other[k][place, q])
            dst[first + j] = jnp.where(j < count, block, zero)

    landed(r0m)
    ranked_rows = [rank_row(role, q) for role, q in enumerate((z, zb, za, zd))]
    start(r1m)
    for k in range(CHUNKS):
        landed(r0[k])
        pack_row(ranked_rows[2], k, R.send[k], 0)
        pack_row(ranked_rows[3], k, R.send[k], CAP)
        start(r1[k])

    def merge(l1, at1, l2, at2, lout, ix, base1, base2, zero_slot):
        n1, n2 = l1[at1], l2[at2]
        lout[0] = n1 + n2
        for j in range(CAP):
            rest = jnp.clip(j - n1, 0, CAP - 1)
            in1, in2 = j < n1, j - n1 < n2
            lout[1 + j] = jnp.where(in1, l1[at1 + 1 + j], jnp.where(in2, l2[at2 + 1 + rest], -1))
            table[ix + j] = jnp.where(in1, base1 + j, jnp.where(in2, base2 + rest, zero_slot))

    def move(src, ix, dst):
        for j in range(CAP):
            dst[j] = src[table[ix + j]]

    def six(ref, k, first=0):
        return ref[k].at[pl.ds(first, CAP)]

    def later_copies(path, device2, device3):
        return (
            copy(path.l_send2, path.l_in2, device2),
            [copy(path.send2[k], six(path.second, k, CAP), device2) for k in range(CHUNKS)],
            copy(path.l_send3, path.l_in3, device3),
            [copy(six(path.third, k), six(path.third, k, CAP), device3) for k in range(CHUNKS)],
        )

    c2m, c2, c3m, c3 = later_copies(C, dev_xb, dev_yh)
    r2m, r2, r3m, r3 = later_copies(R, dev_zb, dev_yl)

    def lists1(path, in_copy, out_copy, ix_b, ix_o):
        landed(in_copy)
        merge(path.l_own, LIST, path.l_in1, LIST, path.l_send2, ix_b, CAP, 3 * CAP, 4 * CAP)
        start(out_copy)
        merge(path.l_own, 0, path.l_in1, 0, path.l_own2, ix_o, 0, 2 * CAP, 4 * CAP)

    def lists2(path, in_copy, out_copy, ix):
        landed(in_copy)
        merge(path.l_own2, 0, path.l_in2, 0, path.l_send3, ix, 0, CAP, 2 * CAP)
        start(out_copy)

    def lists3(path, in_copy, out_copies, ix):
        landed(in_copy)
        merge(path.l_send3, 0, path.l_in3, 0, path.l_final, ix, 0, CAP, 2 * CAP)
        start(*out_copies)

    def blocks1(path, in_copies, out_copies, ix_b, ix_o, k):
        landed(in_copies[k])
        move(path.first[k], ix_b, path.send2[k])
        start(out_copies[k])
        move(path.first[k], ix_o, path.second[k])

    def blocks2(path, in_copies, out_copies, ix, k):
        landed(in_copies[k])
        move(path.second[k], ix, path.third[k])
        start(out_copies[k])

    def names(path, role):
        return path.l_final.at[pl.ds(role * LIST, LIST)]

    c4am, c4bm = copy(names(C, 0), names(C, 2), dev_xa), copy(names(C, 0), names(C, 1), dev_xb)
    c5m = copy(names(C, 1), names(C, 3), dev_xa)
    r4am, r4bm = copy(names(R, 0), names(R, 2), dev_za), copy(names(R, 0), names(R, 1), dev_zb)
    r5m = copy(names(R, 1), names(R, 3), dev_za)
    fm = copy(R.l_final.at[pl.ds(0, 4 * LIST)], R.l_final.at[pl.ds(4 * LIST, 4 * LIST)], dev_core)

    def column(role, k):
        return columns_panel.at[pl.ds(role * CAP, CAP), part(k)]

    def line_of(role, k):
        return rows[role].at[pl.ds(0, CAP), part(k)]

    each = range(CHUNKS)
    c4a = [copy(column(0, k), column(2, k), dev_xa) for k in each]
    c4b = [copy(column(0, k), column(1, k), dev_xb) for k in each]
    c5 = [copy(column(1, k), column(3, k), dev_xa) for k in each]
    r4a = [copy(line_of(0, k), line_of(2, k), dev_za) for k in each]
    r4b = [copy(line_of(0, k), line_of(1, k), dev_zb) for k in each]
    r5 = [copy(line_of(1, k), line_of(3, k), dev_za) for k in each]
    f = [[copy(line_of(role, k), line_of(4 + role, k), dev_core) for k in each] for role in range(4)]

    def blocks3_column(k):
        landed(c3[k])
        for j in range(CAP):
            columns_panel[j, part(k), :] = C.third[k][table[IX_C3 + j]]
        start(c4b[k], c4a[k])

    def blocks3_row(k):
        landed(r3[k])
        for j in range(CAP):
            rows[0][j, part(k), :] = R.third[k][table[IX_R3 + j]]
        start(r4b[k], r4a[k], f[0][k])

    def squares(ref):
        total = jnp.zeros((8, BS), jnp.float32)
        for i in range(2 * CAP):
            block = ref[i].astype(jnp.float32)
            total = total + jnp.sum((block * block).reshape(PART // 8, 8, BS), axis=0)
        return total

    trace_devices = (dev_core, dev_xa, dev_za, dev_xb, dev_zb, dev_yh, dev_yl)
    trace = [copy(tacc.at[i], trecv.at[i], trace_devices[i]) for i in range(7)]

    def trace_step(i):
        landed(trace[i])
        tacc[i + 1] = tacc[i] + trecv[i]
        if i < 6:
            start(trace[i + 1])

    for k in each:
        pack_row(ranked_rows[0], k, R.first[k], 0)
        pack_row(ranked_rows[1], k, R.first[k], CAP)
    total = jnp.zeros((8, BS), jnp.float32)
    for k in each:
        total = total + squares(C.send[k])
        total = total + squares(C.first[k])
    tacc[0] = total
    start(trace[0])

    def match(row_role, carry):
        have = [R.l_final[row_role * LIST + 1 + i] for i in range(CAP)]
        for t in range(4 * CAP):
            wanted = C.l_final[(t // CAP) * LIST + 1 + t % CAP]
            slot = jnp.int32(CAP)
            for i in range(CAP):
                slot = jnp.where(have[i] == wanted, i, slot)
            table[IX_MATCH + row_role * 4 * CAP + t] = slot
        return carry

    def match_rows(first_role):
        lax.fori_loop(first_role, first_role + 4, match, 0)

    done = []

    def sent(*copies):
        for one in copies:
            one.wait_send()
            done.append(one)

    column_of = (x, xb, xa, xd)
    line_by_role = (
        [core * 4 + position for position in (z, zb, za, zd)]
        + [(1 - core) * 4 + position for position in (z, za, zb, zd)]
    )

    def product(row_roles):
        for c in range(4):
            left = []
            for role in row_roles:
                base = IX_MATCH + (role * 4 + c) * CAP
                left.append(jnp.concatenate([rows[role][table[base + j]] for j in range(CAP)], axis=1))
            right = columns_panel[c * CAP:(c + 1) * CAP].reshape(CAP * BS, BS)
            total = jnp.dot(
                jnp.concatenate(left, axis=0), right, preferred_element_type=jnp.float32
            )
            q = column_of[c]
            for i, role in enumerate(row_roles):
                line = line_by_role[role]
                kept = jnp.where(filter_mask[q, line] != 0, total[i * BS:(i + 1) * BS], 0.0)
                out[line, :, pl.ds(pl.multiple_of(q * BS, BS), BS)] = kept.astype(jnp.bfloat16)

    row_lag = 0.75
    steps = []
    for k in each:
        steps += [
            (1 + k, lambda k=k: blocks1(C, c1, c2, IX_C1B, IX_C1O, k)),
            (2 + k, lambda k=k: blocks2(C, c2, c3, IX_C2, k)),
            (3 + k, lambda k=k: blocks3_column(k)),
            (4 + k, lambda k=k: (landed(c4b[k]), start(c5[k]))),
            (1 + k + row_lag, lambda k=k: blocks1(R, r1, r2, IX_R1B, IX_R1O, k)),
            (2 + k + row_lag, lambda k=k: blocks2(R, r2, r3, IX_R2, k)),
            (3 + k + row_lag, lambda k=k: blocks3_row(k)),
            (4 + k + row_lag, lambda k=k: (landed(r4b[k]), start(r5[k], f[1][k]))),
            (4.2 + k + row_lag, lambda k=k: (landed(r4a[k]), start(f[2][k]))),
            (5 + k + row_lag, lambda k=k: (landed(r5[k]), start(f[3][k]))),
        ]
    steps += [
        (0.9, lambda: lists1(C, c1m, c2m, IX_C1B, IX_C1O)),
        (1.1, lambda: lists1(R, r1m, r2m, IX_R1B, IX_R1O)),
        (1.3, lambda: lists2(C, c2m, c3m, IX_C2)),
        (1.8, lambda: trace_step(0)),
        (2.1, lambda: lists2(R, r2m, r3m, IX_R2)),
        (2.2, lambda: lists3(C, c3m, (c4bm, c4am), IX_C3)),
        (2.9, lambda: lists3(R, r3m, (r4bm, r4am), IX_R3)),
        (3.1, lambda: trace_step(1)),
        (3.2, lambda: (landed(c4bm), start(c5m))),
        (3.8, lambda: (landed(r4bm), start(r5m))),
        (3.85, lambda: trace_step(2)),
        (4.05, lambda: (landed(r4am, r5m), start(fm))),
        (4.1, lambda: (landed(c4am, c5m), match_rows(0))),
        (4.3, lambda: trace_step(3)),
        (5.05, lambda: (landed(fm), match_rows(4))),
        (5.1, lambda: trace_step(4)),
        (5.5, lambda: sent(c1m, *c1, r0m, *r0, r1m, *r1, c2m, *c2, r2m, *r2)),
        (5.85, lambda: trace_step(5)),
        (6.3, lambda: (landed(*c4a, *c5), product((0, 1)))),
        (6.4, lambda: (landed(*f[0], *f[1]), product((4, 5)))),
    ]
    for _, step in sorted(steps, key=lambda one: one[0]):
        step()

    product((2, 3))
    sent(c3m, *c3, r3m, *r3, c4am, c4bm, r4am, r4bm, c5m, r5m, fm, *c4b, *trace[:5])
    for role in (2, 3):
        landed(*f[role])
    product((6, 7))

    trace_step(6)
    occupation[0, 0] = jnp.sum(tacc[7])
    for one in remote:
        if not any(one is other_one for other_one in done):
            one.wait_send()


def on_device(values, pattern, filter_mask, assignment):
    hbm = pl.BlockSpec(memory_space=pltpu.HBM)
    parts = lambda count: [pltpu.VMEM((count, PART, BS), jnp.bfloat16)] * CHUNKS
    lists = lambda *counts: [pltpu.SMEM((count * LIST,), jnp.int32) for count in counts]

    def path(final):
        return [
            *parts(4 * CAP + 1), *parts(2 * CAP), *parts(CAP), *parts(2 * CAP + 1),
            *parts(2 * CAP + 1), *lists(4, 2, 1, 1, 1, 1, 1, final),
        ]

    product, occupation = pl.pallas_call(
        kernel,
        out_shape=(
            jax.ShapeDtypeStruct((8, BS, 4 * BS), jnp.bfloat16),
            jax.ShapeDtypeStruct((1, 1), jnp.float32),
        ),
        in_specs=[hbm] * 4,
        out_specs=(pl.BlockSpec(memory_space=pltpu.VMEM), pl.BlockSpec(memory_space=pltpu.SMEM)),
        scratch_shapes=[
            pltpu.VMEM((4, 8, BS, BS), jnp.bfloat16),
            pltpu.SMEM((4, 8), jnp.int32),
            pltpu.SMEM((4, 8), jnp.int32),
            pltpu.SMEM((4, 8), jnp.int32),
            pltpu.SMEM((64,), jnp.int32),
            *[pltpu.VMEM((4, 4, PART, BS), jnp.bfloat16)] * CHUNKS,
            *path(4),
            *path(8),
            pltpu.VMEM((4 * CAP, BS, BS), jnp.bfloat16),
            *[pltpu.VMEM((CAP + 1, BS, BS), jnp.bfloat16)] * 8,
            pltpu.VMEM((8, 8, BS), jnp.float32),
            pltpu.VMEM((7, 8, BS), jnp.float32),
            pltpu.SMEM((IX_MATCH + 8 * 4 * CAP,), jnp.int32),
            pltpu.SemaphoreType.DMA((7,)),
            pltpu.SemaphoreType.DMA((COPIES,)),
            pltpu.SemaphoreType.DMA((COPIES,)),
        ],
        compiler_params=pltpu.CompilerParams(
            collective_id=0, has_side_effects=True, vmem_limit_bytes=52 * 1024 * 1024
        ),
        cost_estimate=pl.CostEstimate(
            flops=2 * 192 * BS**3, bytes_accessed=4 * 1024 * 1024, transcendentals=0
        ),
    )(values.reshape(8, BS, 4 * BS), pattern.T, filter_mask.T, assignment)
    return product.reshape(values.shape), occupation[0, 0]


def solution(mesh):
    in_specs = (P("row", "col"), P("row", "col"), P("row", "col"), P())
    out_specs = (P("row", "col"), P())
    return jax.shard_map(
        on_device, mesh=mesh, in_specs=in_specs, out_specs=out_specs, check_vma=False
    )
```

```python
import jax
import jax.numpy as jnp
from jax import lax
from jax.experimental import pallas as pl
from jax.experimental.pallas import tpu as pltpu
from jax.sharding import PartitionSpec as P

BS = 128
CAP = 6
LIST = 128
CHUNKS = 2
PART = BS // CHUNKS
COPIES = 96
IX_C1B, IX_C1O, IX_C2, IX_C3, IX_R1B, IX_R1O, IX_R2, IX_R3 = range(0, 64, 8)
IX_MATCH = 64
MESH = pl.DeviceIdType.MESH


class Path:
    def __init__(self, refs):
        refs = list(refs)
        take = lambda: [refs.pop(0) for _ in range(CHUNKS)]
        self.first, self.send, self.send2 = take(), take(), take()
        self.second, self.third = take(), take()
        (self.l_own, self.l_in1, self.l_send2, self.l_own2, self.l_in2,
         self.l_send3, self.l_in3, self.l_final) = refs


def kernel(values, pattern_in, filter_in, assignment_in, out, occupation, *refs):
    refs = list(refs)
    take = lambda count: [refs.pop(0) for _ in range(count)]
    own, pattern, other_pattern, filter_mask, assignment = take(5)
    other = take(CHUNKS)
    C, R = Path(take(5 * CHUNKS + 8)), Path(take(5 * CHUNKS + 8))
    columns_panel, = take(1)
    rows = take(8)
    tacc, trecv, table, load_sem, send_sem, recv_sem = take(6)

    row, col = lax.axis_index("row"), lax.axis_index("col")
    x, y_hi = row // 2, row % 2
    y_lo, z, core = col // 8, (col // 2) % 4, col % 2

    def partners(position):
        even, odd = position + 1 - 2 * (position % 2), 3 - position
        a = even * (1 - core) + odd * core
        b = odd * (1 - core) + even * core
        return a, b, (position + 2) % 4

    xa, xb, xd = partners(x)
    za, zb, zd = partners(z)
    dev_xa, dev_xb = (xa * 2 + y_hi, col), (xb * 2 + y_hi, col)
    dev_yh = (x * 2 + 1 - y_hi, col)
    dev_za = (row, y_lo * 8 + za * 2 + core)
    dev_zb = (row, y_lo * 8 + zb * 2 + core)
    dev_yl = (row, (1 - y_lo) * 8 + z * 2 + core)
    other_col = col + 1 - 2 * core
    dev_core = (row, other_col)

    remote = []

    def copy(src, dst, device):
        index = len(remote)
        remote.append(pltpu.make_async_remote_copy(
            src_ref=src, dst_ref=dst, send_sem=send_sem.at[index],
            recv_sem=recv_sem.at[index], device_id=device, device_id_type=MESH,
        ))
        return remote[-1]

    def start(*copies):
        for one in copies:
            one.start()

    def landed(*copies):
        for one in copies:
            one.wait_recv()

    small = [
        pltpu.make_async_copy(src, dst, load_sem.at[4 + i])
        for i, (src, dst) in enumerate(
            ((pattern_in, pattern), (assignment_in, assignment), (filter_in, filter_mask))
        )
    ]
    loads = [
        pltpu.make_async_copy(values.at[:, :, q * BS:(q + 1) * BS], own.at[q], load_sem.at[q])
        for q in range(4)
    ]
    start(*small, *loads)
    barrier = pltpu.get_barrier_semaphore()
    for device in (dev_xa, dev_xb, dev_yh, dev_za, dev_zb, dev_yl, dev_core):
        pl.semaphore_signal(barrier, inc=1, device_id=device, device_id_type=MESH)

    zero = jnp.zeros((PART, BS), jnp.bfloat16)
    for path in (C, R):
        for k in range(CHUNKS):
            path.first[k][4 * CAP] = zero
            path.second[k][2 * CAP] = zero
            path.third[k][2 * CAP] = zero
    for ref in rows:
        ref[CAP] = jnp.zeros((BS, BS), jnp.bfloat16)

    def part(k):
        return slice(k * PART, (k + 1) * PART)

    def rank(flags):
        count = jnp.int32(0)
        places = [jnp.int32(0)] * CAP
        for t, flag in enumerate(flags):
            for j in range(min(CAP, t + 1)):
                places[j] = jnp.where((flag != 0) & (count == j), t, places[j])
            count = count + flag
        return places, count

    def rank_column(role, q):
        places, count = rank([pattern[q, t] for t in range(8)])
        C.l_own[role * LIST] = count
        for j in range(CAP):
            name = assignment[row * 8 + places[j]]
            C.l_own[role * LIST + 1 + j] = jnp.where(j < count, name, -1)
        return q, places, count

    def pack_column(ranked, k, dst, first):
        q, places, count = ranked
        for j in range(CAP):
            block = own[q, places[j], part(k), :]
            dst[first + j] = jnp.where(j < count, block, zero)

    for one in small:
        one.wait()
    ranked_columns = [rank_column(role, q) for role, q in enumerate((x, xb, xa, xd))]
    for one in loads:
        one.wait()
    for k in range(CHUNKS):
        pack_column(ranked_columns[2], k, C.send[k], 0)
        pack_column(ranked_columns[3], k, C.send[k], CAP)

    half = (1 - core) * 4
    r0m = copy(pattern, other_pattern, dev_core)
    r0 = [copy(own.at[:, pl.ds(half, 4), part(k)], other[k], dev_core) for k in range(CHUNKS)]

    def first_copies(path, device):
        return (
            copy(path.l_own.at[pl.ds(2 * LIST, 2 * LIST)], path.l_in1, device),
            [copy(path.send[k], path.first[k].at[pl.ds(2 * CAP, 2 * CAP)], device) for k in range(CHUNKS)],
        )

    c1m, c1 = first_copies(C, dev_xa)
    r1m, r1 = first_copies(R, dev_za)

    pl.semaphore_wait(barrier, 7)
    start(r0m, c1m)
    for k in range(CHUNKS):
        start(r0[k], c1[k])
    for k in range(CHUNKS):
        pack_column(ranked_columns[0], k, C.first[k], 0)
        pack_column(ranked_columns[1], k, C.first[k], CAP)

    def rank_row(role, q):
        line = core * 4 + q
        places, count = rank(
            [pattern[t, line] for t in range(4)] + [other_pattern[t, line] for t in range(4)]
        )
        R.l_own[role * LIST] = count
        for j in range(CAP):
            name = jnp.where(places[j] < 4, col * 4, other_col * 4 - 4) + places[j]
            R.l_own[role * LIST + 1 + j] = jnp.where(j < count, name, -1)
        return line, q, places, count

    def pack_row(ranked, k, dst, first):
        line, q, places, count = ranked
        for j in range(CAP):
            mine = places[j] < 4
            place = jnp.where(mine, places[j], places[j] - 4)
            block = jnp.where(mine, own[place, line, part(k), :], other[k][place, q])
            dst[first + j] = jnp.where(j < count, block, zero)

    landed(r0m)
    ranked_rows = [rank_row(role, q) for role, q in enumerate((z, zb, za, zd))]
    start(r1m)
    for k in range(CHUNKS):
        landed(r0[k])
        pack_row(ranked_rows[2], k, R.send[k], 0)
        pack_row(ranked_rows[3], k, R.send[k], CAP)
        start(r1[k])

    def merge(l1, at1, l2, at2, lout, ix, base1, base2, zero_slot):
        n1, n2 = l1[at1], l2[at2]
        lout[0] = n1 + n2
        for j in range(CAP):
            rest = jnp.clip(j - n1, 0, CAP - 1)
            in1, in2 = j < n1, j - n1 < n2
            lout[1 + j] = jnp.where(in1, l1[at1 + 1 + j], jnp.where(in2, l2[at2 + 1 + rest], -1))
            table[ix + j] = jnp.where(in1, base1 + j, jnp.where(in2, base2 + rest, zero_slot))

    def move(src, ix, dst):
        for j in range(CAP):
            dst[j] = src[table[ix + j]]

    def six(ref, k, first=0):
        return ref[k].at[pl.ds(first, CAP)]

    def later_copies(path, device2, device3):
        return (
            copy(path.l_send2, path.l_in2, device2),
            [copy(path.send2[k], six(path.second, k, CAP), device2) for k in range(CHUNKS)],
            copy(path.l_send3, path.l_in3, device3),
            [copy(six(path.third, k), six(path.third, k, CAP), device3) for k in range(CHUNKS)],
        )

    c2m, c2, c3m, c3 = later_copies(C, dev_xb, dev_yh)
    r2m, r2, r3m, r3 = later_copies(R, dev_zb, dev_yl)

    def lists1(path, in_copy, out_copy, ix_b, ix_o):
        landed(in_copy)
        merge(path.l_own, LIST, path.l_in1, LIST, path.l_send2, ix_b, CAP, 3 * CAP, 4 * CAP)
        start(out_copy)
        merge(path.l_own, 0, path.l_in1, 0, path.l_own2, ix_o, 0, 2 * CAP, 4 * CAP)

    def lists2(path, in_copy, out_copy, ix):
        landed(in_copy)
        merge(path.l_own2, 0, path.l_in2, 0, path.l_send3, ix, 0, CAP, 2 * CAP)
        start(out_copy)

    def lists3(path, in_copy, out_copies, ix):
        landed(in_copy)
        merge(path.l_send3, 0, path.l_in3, 0, path.l_final, ix, 0, CAP, 2 * CAP)
        start(*out_copies)

    def blocks1(path, in_copies, out_copies, ix_b, ix_o, k):
        landed(in_copies[k])
        move(path.first[k], ix_b, path.send2[k])
        start(out_copies[k])
        move(path.first[k], ix_o, path.second[k])

    def blocks2(path, in_copies, out_copies, ix, k):
        landed(in_copies[k])
        move(path.second[k], ix, path.third[k])
        start(out_copies[k])

    def names(path, role):
        return path.l_final.at[pl.ds(role * LIST, LIST)]

    c4am, c4bm = copy(names(C, 0), names(C, 2), dev_xa), copy(names(C, 0), names(C, 1), dev_xb)
    c5m = copy(names(C, 1), names(C, 3), dev_xa)
    r4am, r4bm = copy(names(R, 0), names(R, 2), dev_za), copy(names(R, 0), names(R, 1), dev_zb)
    r5m = copy(names(R, 1), names(R, 3), dev_za)
    fm = copy(R.l_final.at[pl.ds(0, 4 * LIST)], R.l_final.at[pl.ds(4 * LIST, 4 * LIST)], dev_core)

    def column(role, k):
        return columns_panel.at[pl.ds(role * CAP, CAP), part(k)]

    def line_of(role, k):
        return rows[role].at[pl.ds(0, CAP), part(k)]

    each = range(CHUNKS)
    c4a = [copy(column(0, k), column(2, k), dev_xa) for k in each]
    c4b = [copy(column(0, k), column(1, k), dev_xb) for k in each]
    c5 = [copy(column(1, k), column(3, k), dev_xa) for k in each]
    r4a = [copy(line_of(0, k), line_of(2, k), dev_za) for k in each]
    r4b = [copy(line_of(0, k), line_of(1, k), dev_zb) for k in each]
    r5 = [copy(line_of(1, k), line_of(3, k), dev_za) for k in each]
    f = [[copy(line_of(role, k), line_of(4 + role, k), dev_core) for k in each] for role in range(4)]

    def blocks3_column(k):
        landed(c3[k])
        for j in range(CAP):
            columns_panel[j, part(k), :] = C.third[k][table[IX_C3 + j]]
        start(c4b[k], c4a[k])

    def blocks3_row(k):
        landed(r3[k])
        for j in range(CAP):
            rows[0][j, part(k), :] = R.third[k][table[IX_R3 + j]]
        start(r4b[k], r4a[k], f[0][k])

    def squares(ref):
        total = jnp.zeros((8, BS), jnp.float32)
        for i in range(2 * CAP):
            block = ref[i].astype(jnp.float32)
            total = total + jnp.sum((block * block).reshape(PART // 8, 8, BS), axis=0)
        return total

    trace_devices = (dev_core, dev_xa, dev_za, dev_xb, dev_zb, dev_yh, dev_yl)
    trace = [copy(tacc.at[i], trecv.at[i], trace_devices[i]) for i in range(7)]

    def trace_step(i):
        landed(trace[i])
        tacc[i + 1] = tacc[i] + trecv[i]
        if i < 6:
            start(trace[i + 1])

    for k in each:
        pack_row(ranked_rows[0], k, R.first[k], 0)
        pack_row(ranked_rows[1], k, R.first[k], CAP)
    total = jnp.zeros((8, BS), jnp.float32)
    for k in each:
        total = total + squares(C.send[k])
        total = total + squares(C.first[k])
    tacc[0] = total
    start(trace[0])

    def match(row_role, carry):
        have = [R.l_final[row_role * LIST + 1 + i] for i in range(CAP)]
        for t in range(4 * CAP):
            wanted = C.l_final[(t // CAP) * LIST + 1 + t % CAP]
            slot = jnp.int32(CAP)
            for i in range(CAP):
                slot = jnp.where(have[i] == wanted, i, slot)
            table[IX_MATCH + row_role * 4 * CAP + t] = slot
        return carry

    def match_rows(first_role):
        lax.fori_loop(first_role, first_role + 4, match, 0)

    done = []

    def sent(*copies):
        for one in copies:
            one.wait_send()
            done.append(one)

    row_lag = 0.75
    steps = []
    for k in each:
        steps += [
            (1 + k, lambda k=k: blocks1(C, c1, c2, IX_C1B, IX_C1O, k)),
            (2 + k, lambda k=k: blocks2(C, c2, c3, IX_C2, k)),
            (3 + k, lambda k=k: blocks3_column(k)),
            (4 + k, lambda k=k: (landed(c4b[k]), start(c5[k]))),
            (1 + k + row_lag, lambda k=k: blocks1(R, r1, r2, IX_R1B, IX_R1O, k)),
            (2 + k + row_lag, lambda k=k: blocks2(R, r2, r3, IX_R2, k)),
            (3 + k + row_lag, lambda k=k: blocks3_row(k)),
            (4 + k + row_lag, lambda k=k: (landed(r4b[k]), start(r5[k], f[1][k]))),
            (4.2 + k + row_lag, lambda k=k: (landed(r4a[k]), start(f[2][k]))),
            (5 + k + row_lag, lambda k=k: (landed(r5[k]), start(f[3][k]))),
        ]
    steps += [
        (0.9, lambda: lists1(C, c1m, c2m, IX_C1B, IX_C1O)),
        (1.1, lambda: lists1(R, r1m, r2m, IX_R1B, IX_R1O)),
        (1.3, lambda: lists2(C, c2m, c3m, IX_C2)),
        (1.8, lambda: trace_step(0)),
        (2.1, lambda: lists2(R, r2m, r3m, IX_R2)),
        (2.2, lambda: lists3(C, c3m, (c4bm, c4am), IX_C3)),
        (2.9, lambda: lists3(R, r3m, (r4bm, r4am), IX_R3)),
        (3.1, lambda: trace_step(1)),
        (3.2, lambda: (landed(c4bm), start(c5m))),
        (3.8, lambda: (landed(r4bm), start(r5m))),
        (3.85, lambda: trace_step(2)),
        (4.05, lambda: (landed(r4am, r5m), start(fm))),
        (4.1, lambda: (landed(c4am, c5m), match_rows(0))),
        (4.3, lambda: trace_step(3)),
        (5.05, lambda: (landed(fm), match_rows(4))),
        (5.1, lambda: trace_step(4)),
        (5.5, lambda: sent(c1m, *c1, r0m, *r0, r1m, *r1, c2m, *c2, r2m, *r2)),
        (5.85, lambda: trace_step(5)),
    ]
    for _, step in sorted(steps, key=lambda one: one[0]):
        step()

    column_of = (x, xb, xa, xd)
    line_by_role = (
        [core * 4 + position for position in (z, zb, za, zd)]
        + [(1 - core) * 4 + position for position in (z, za, zb, zd)]
    )

    def product(row_roles, column_roles):
        for c in column_roles:
            left = []
            for role in row_roles:
                base = IX_MATCH + (role * 4 + c) * CAP
                left.append(jnp.concatenate([rows[role][table[base + j]] for j in range(CAP)], axis=1))
            right = columns_panel[c * CAP:(c + 1) * CAP].reshape(CAP * BS, BS)
            total = jnp.dot(
                jnp.concatenate(left, axis=0), right, preferred_element_type=jnp.float32
            )
            q = column_of[c]
            for i, role in enumerate(row_roles):
                line = line_by_role[role]
                kept = jnp.where(filter_mask[q, line] != 0, total[i * BS:(i + 1) * BS], 0.0)
                out[line, :, pl.ds(pl.multiple_of(q * BS, BS), BS)] = kept.astype(jnp.bfloat16)

    first_three = (0, 1, 2)
    landed(*c4a)
    product((0, 1), first_three)
    product((2, 3), first_three)
    landed(*f[0], *f[1])
    product((4, 5), first_three)
    sent(c3m, *c3, r3m, *r3, c4am, c4bm, r4am, r4bm, c5m, r5m, fm, *c4b, *trace[:5])
    landed(*f[2], *f[3])
    product((6, 7), first_three)
    trace_step(6)
    occupation[0, 0] = jnp.sum(tacc[7])
    landed(*c5)
    product((0, 1, 2, 3), (3,))
    product((4, 5, 6, 7), (3,))

    for one in remote:
        if not any(one is other_one for other_one in done):
            one.wait_send()


def on_device(values, pattern, filter_mask, assignment):
    hbm = pl.BlockSpec(memory_space=pltpu.HBM)
    parts = lambda count: [pltpu.VMEM((count, PART, BS), jnp.bfloat16)] * CHUNKS
    lists = lambda *counts: [pltpu.SMEM((count * LIST,), jnp.int32) for count in counts]

    def path(final):
        return [
            *parts(4 * CAP + 1), *parts(2 * CAP), *parts(CAP), *parts(2 * CAP + 1),
            *parts(2 * CAP + 1), *lists(4, 2, 1, 1, 1, 1, 1, final),
        ]

    product, occupation = pl.pallas_call(
        kernel,
        out_shape=(
            jax.ShapeDtypeStruct((8, BS, 4 * BS), jnp.bfloat16),
            jax.ShapeDtypeStruct((1, 1), jnp.float32),
        ),
        in_specs=[hbm] * 4,
        out_specs=(pl.BlockSpec(memory_space=pltpu.VMEM), pl.BlockSpec(memory_space=pltpu.SMEM)),
        scratch_shapes=[
            pltpu.VMEM((4, 8, BS, BS), jnp.bfloat16),
            pltpu.SMEM((4, 8), jnp.int32),
            pltpu.SMEM((4, 8), jnp.int32),
            pltpu.SMEM((4, 8), jnp.int32),
            pltpu.SMEM((64,), jnp.int32),
            *[pltpu.VMEM((4, 4, PART, BS), jnp.bfloat16)] * CHUNKS,
            *path(4),
            *path(8),
            pltpu.VMEM((4 * CAP, BS, BS), jnp.bfloat16),
            *[pltpu.VMEM((CAP + 1, BS, BS), jnp.bfloat16)] * 8,
            pltpu.VMEM((8, 8, BS), jnp.float32),
            pltpu.VMEM((7, 8, BS), jnp.float32),
            pltpu.SMEM((IX_MATCH + 8 * 4 * CAP,), jnp.int32),
            pltpu.SemaphoreType.DMA((7,)),
            pltpu.SemaphoreType.DMA((COPIES,)),
            pltpu.SemaphoreType.DMA((COPIES,)),
        ],
        compiler_params=pltpu.CompilerParams(
            collective_id=0, has_side_effects=True, vmem_limit_bytes=52 * 1024 * 1024
        ),
        cost_estimate=pl.CostEstimate(
            flops=2 * 192 * BS**3, bytes_accessed=4 * 1024 * 1024, transcendentals=0
        ),
    )(values.reshape(8, BS, 4 * BS), pattern.T, filter_mask.T, assignment)
    return product.reshape(values.shape), occupation[0, 0]


def solution(mesh):
    in_specs = (P("row", "col"), P("row", "col"), P("row", "col"), P())
    out_specs = (P("row", "col"), P())
    return jax.shard_map(
        on_device, mesh=mesh, in_specs=in_specs, out_specs=out_specs, check_vma=False
    )
```

```python
import jax
import jax.numpy as jnp
from jax import lax
from jax.experimental import pallas as pl
from jax.experimental.pallas import tpu as pltpu
from jax.sharding import PartitionSpec as P

BS = 128
CAP = 6
LIST = 128
CHUNKS = 2
PART = BS // CHUNKS
COPIES = 96
IX_C1B, IX_C1O, IX_C2, IX_C3, IX_R1B, IX_R1O, IX_R2, IX_R3 = range(0, 64, 8)
IX_MATCH = 64
MESH = pl.DeviceIdType.MESH


class Path:
    def __init__(self, refs):
        refs = list(refs)
        take = lambda: [refs.pop(0) for _ in range(CHUNKS)]
        self.first, self.send, self.send2 = take(), take(), take()
        self.second, self.third = take(), take()
        (self.l_own, self.l_in1, self.l_send2, self.l_own2, self.l_in2,
         self.l_send3, self.l_in3, self.l_final) = refs


def kernel(values, pattern_in, filter_in, assignment_in, out, occupation, *refs):
    refs = list(refs)
    take = lambda count: [refs.pop(0) for _ in range(count)]
    own, pattern, other_pattern, filter_mask, assignment = take(5)
    other = take(CHUNKS)
    C, R = Path(take(5 * CHUNKS + 8)), Path(take(5 * CHUNKS + 8))
    columns_panel, = take(1)
    rows = take(8)
    tacc, trecv, table, load_sem, send_sem, recv_sem = take(6)

    row, col = lax.axis_index("row"), lax.axis_index("col")
    x, y_hi = row // 2, row % 2
    y_lo, z, core = col // 8, (col // 2) % 4, col % 2

    def partners(position):
        even, odd = position + 1 - 2 * (position % 2), 3 - position
        a = even * (1 - core) + odd * core
        b = odd * (1 - core) + even * core
        return a, b, (position + 2) % 4

    xa, xb, xd = partners(x)
    za, zb, zd = partners(z)
    dev_xa, dev_xb = (xa * 2 + y_hi, col), (xb * 2 + y_hi, col)
    dev_yh = (x * 2 + 1 - y_hi, col)
    dev_za = (row, y_lo * 8 + za * 2 + core)
    dev_zb = (row, y_lo * 8 + zb * 2 + core)
    dev_yl = (row, (1 - y_lo) * 8 + z * 2 + core)
    other_col = col + 1 - 2 * core
    dev_core = (row, other_col)

    remote = []

    def copy(src, dst, device):
        index = len(remote)
        remote.append(pltpu.make_async_remote_copy(
            src_ref=src, dst_ref=dst, send_sem=send_sem.at[index],
            recv_sem=recv_sem.at[index], device_id=device, device_id_type=MESH,
        ))
        return remote[-1]

    def start(*copies):
        for one in copies:
            one.start()

    def landed(*copies):
        for one in copies:
            one.wait_recv()

    small = [
        pltpu.make_async_copy(src, dst, load_sem.at[4 + i])
        for i, (src, dst) in enumerate(
            ((pattern_in, pattern), (assignment_in, assignment), (filter_in, filter_mask))
        )
    ]
    loads = [
        pltpu.make_async_copy(values.at[:, :, q * BS:(q + 1) * BS], own.at[q], load_sem.at[q])
        for q in range(4)
    ]
    start(*small, *loads)
    barrier = pltpu.get_barrier_semaphore()
    for device in (dev_xa, dev_xb, dev_yh, dev_za, dev_zb, dev_yl, dev_core):
        pl.semaphore_signal(barrier, inc=1, device_id=device, device_id_type=MESH)

    zero = jnp.zeros((PART, BS), jnp.bfloat16)
    for path in (C, R):
        for k in range(CHUNKS):
            path.first[k][4 * CAP] = zero
            path.second[k][2 * CAP] = zero
            path.third[k][2 * CAP] = zero
    for ref in rows:
        ref[CAP] = jnp.zeros((BS, BS), jnp.bfloat16)

    def part(k):
        return slice(k * PART, (k + 1) * PART)

    def rank(flags):
        count = jnp.int32(0)
        places = [jnp.int32(0)] * CAP
        for t, flag in enumerate(flags):
            for j in range(min(CAP, t + 1)):
                places[j] = jnp.where((flag != 0) & (count == j), t, places[j])
            count = count + flag
        return places, count

    def rank_column(role, q):
        places, count = rank([pattern[q, t] for t in range(8)])
        C.l_own[role * LIST] = count
        for j in range(CAP):
            name = assignment[row * 8 + places[j]]
            C.l_own[role * LIST + 1 + j] = jnp.where(j < count, name, -1)
        return q, places, count

    def pack_column(ranked, k, dst, first):
        q, places, count = ranked
        for j in range(CAP):
            block = own[q, places[j], part(k), :]
            dst[first + j] = jnp.where(j < count, block, zero)

    for one in small:
        one.wait()
    ranked_columns = [rank_column(role, q) for role, q in enumerate((x, xb, xa, xd))]
    for one in loads:
        one.wait()
    for k in range(CHUNKS):
        pack_column(ranked_columns[2], k, C.send[k], 0)
        pack_column(ranked_columns[3], k, C.send[k], CAP)

    half = (1 - core) * 4
    r0m = copy(pattern, other_pattern, dev_core)
    r0 = [copy(own.at[:, pl.ds(half, 4), part(k)], other[k], dev_core) for k in range(CHUNKS)]

    def first_copies(path, device):
        return (
            copy(path.l_own.at[pl.ds(2 * LIST, 2 * LIST)], path.l_in1, device),
            [copy(path.send[k], path.first[k].at[pl.ds(2 * CAP, 2 * CAP)], device) for k in range(CHUNKS)],
        )

    c1m, c1 = first_copies(C, dev_xa)
    r1m, r1 = first_copies(R, dev_za)

    pl.semaphore_wait(barrier, 7)
    start(r0m, c1m)
    for k in range(CHUNKS):
        start(r0[k], c1[k])
    for k in range(CHUNKS):
        pack_column(ranked_columns[0], k, C.first[k], 0)
        pack_column(ranked_columns[1], k, C.first[k], CAP)

    def rank_row(role, q):
        line = core * 4 + q
        places, count = rank(
            [pattern[t, line] for t in range(4)] + [other_pattern[t, line] for t in range(4)]
        )
        R.l_own[role * LIST] = count
        for j in range(CAP):
            name = jnp.where(places[j] < 4, col * 4, other_col * 4 - 4) + places[j]
            R.l_own[role * LIST + 1 + j] = jnp.where(j < count, name, -1)
        return line, q, places, count

    def pack_row(ranked, k, dst, first):
        line, q, places, count = ranked
        for j in range(CAP):
            mine = places[j] < 4
            place = jnp.where(mine, places[j], places[j] - 4)
            block = jnp.where(mine, own[place, line, part(k), :], other[k][place, q])
            dst[first + j] = jnp.where(j < count, block, zero)

    landed(r0m)
    ranked_rows = [rank_row(role, q) for role, q in enumerate((z, zb, za, zd))]
    start(r1m)
    for k in range(CHUNKS):
        landed(r0[k])
        pack_row(ranked_rows[2], k, R.send[k], 0)
        pack_row(ranked_rows[3], k, R.send[k], CAP)
        start(r1[k])

    def merge(l1, at1, l2, at2, lout, ix, base1, base2, zero_slot):
        n1, n2 = l1[at1], l2[at2]
        lout[0] = n1 + n2
        for j in range(CAP):
            rest = jnp.clip(j - n1, 0, CAP - 1)
            in1, in2 = j < n1, j - n1 < n2
            lout[1 + j] = jnp.where(in1, l1[at1 + 1 + j], jnp.where(in2, l2[at2 + 1 + rest], -1))
            table[ix + j] = jnp.where(in1, base1 + j, jnp.where(in2, base2 + rest, zero_slot))

    def move(src, ix, dst):
        for j in range(CAP):
            dst[j] = src[table[ix + j]]

    def six(ref, k, first=0):
        return ref[k].at[pl.ds(first, CAP)]

    def later_copies(path, device2, device3):
        return (
            copy(path.l_send2, path.l_in2, device2),
            [copy(path.send2[k], six(path.second, k, CAP), device2) for k in range(CHUNKS)],
            copy(path.l_send3, path.l_in3, device3),
            [copy(six(path.third, k), six(path.third, k, CAP), device3) for k in range(CHUNKS)],
        )

    c2m, c2, c3m, c3 = later_copies(C, dev_xb, dev_yh)
    r2m, r2, r3m, r3 = later_copies(R, dev_zb, dev_yl)

    def lists1(path, in_copy, out_copy, ix_b, ix_o):
        landed(in_copy)
        merge(path.l_own, LIST, path.l_in1, LIST, path.l_send2, ix_b, CAP, 3 * CAP, 4 * CAP)
        start(out_copy)
        merge(path.l_own, 0, path.l_in1, 0, path.l_own2, ix_o, 0, 2 * CAP, 4 * CAP)

    def lists2(path, in_copy, out_copy, ix):
        landed(in_copy)
        merge(path.l_own2, 0, path.l_in2, 0, path.l_send3, ix, 0, CAP, 2 * CAP)
        start(out_copy)

    def lists3(path, in_copy, out_copies, ix):
        landed(in_copy)
        merge(path.l_send3, 0, path.l_in3, 0, path.l_final, ix, 0, CAP, 2 * CAP)
        start(*out_copies)

    def blocks1(path, in_copies, out_copies, ix_b, ix_o, k):
        landed(in_copies[k])
        move(path.first[k], ix_b, path.send2[k])
        start(out_copies[k])
        move(path.first[k], ix_o, path.second[k])

    def blocks2(path, in_copies, out_copies, ix, k):
        landed(in_copies[k])
        move(path.second[k], ix, path.third[k])
        start(out_copies[k])

    def names(path, role):
        return path.l_final.at[pl.ds(role * LIST, LIST)]

    c4am, c4bm = copy(names(C, 0), names(C, 2), dev_xa), copy(names(C, 0), names(C, 1), dev_xb)
    c5m = copy(names(C, 1), names(C, 3), dev_xa)
    r4am, r4bm = copy(names(R, 0), names(R, 2), dev_za), copy(names(R, 0), names(R, 1), dev_zb)
    r5m = copy(names(R, 1), names(R, 3), dev_za)
    fm = copy(R.l_final.at[pl.ds(0, 4 * LIST)], R.l_final.at[pl.ds(4 * LIST, 4 * LIST)], dev_core)

    def column(role, k):
        return columns_panel.at[pl.ds(role * CAP, CAP), part(k)]

    def line_of(role, k):
        return rows[role].at[pl.ds(0, CAP), part(k)]

    each = range(CHUNKS)
    c4a = [copy(column(0, k), column(2, k), dev_xa) for k in each]
    c4b = [copy(column(0, k), column(1, k), dev_xb) for k in each]
    c5 = [copy(column(1, k), column(3, k), dev_xa) for k in each]
    r4a = [copy(line_of(0, k), line_of(2, k), dev_za) for k in each]
    r4b = [copy(line_of(0, k), line_of(1, k), dev_zb) for k in each]
    r5 = [copy(line_of(1, k), line_of(3, k), dev_za) for k in each]
    f = [[copy(line_of(role, k), line_of(4 + role, k), dev_core) for k in each] for role in range(4)]

    def blocks3_column(k):
        landed(c3[k])
        for j in range(CAP):
            columns_panel[j, part(k), :] = C.third[k][table[IX_C3 + j]]
        start(c4b[k], c4a[k])

    def blocks3_row(k):
        landed(r3[k])
        for j in range(CAP):
            rows[0][j, part(k), :] = R.third[k][table[IX_R3 + j]]
        start(r4b[k], r4a[k], f[0][k])

    def squares(ref):
        total = jnp.zeros((8, BS), jnp.float32)
        for i in range(2 * CAP):
            block = ref[i].astype(jnp.float32)
            total = total + jnp.sum((block * block).reshape(PART // 8, 8, BS), axis=0)
        return total

    trace_devices = (dev_core, dev_xa, dev_za, dev_xb, dev_zb, dev_yh, dev_yl)
    trace = [copy(tacc.at[i], trecv.at[i], trace_devices[i]) for i in range(7)]

    def trace_step(i):
        landed(trace[i])
        tacc[i + 1] = tacc[i] + trecv[i]
        if i < 6:
            start(trace[i + 1])

    for k in each:
        pack_row(ranked_rows[0], k, R.first[k], 0)
        pack_row(ranked_rows[1], k, R.first[k], CAP)
    total = jnp.zeros((8, BS), jnp.float32)
    for k in each:
        total = total + squares(C.send[k])
        total = total + squares(C.first[k])
    tacc[0] = total
    start(trace[0])

    def match(row_role, carry):
        have = [R.l_final[row_role * LIST + 1 + i] for i in range(CAP)]
        for t in range(4 * CAP):
            wanted = C.l_final[(t // CAP) * LIST + 1 + t % CAP]
            slot = jnp.int32(CAP)
            for i in range(CAP):
                slot = jnp.where(have[i] == wanted, i, slot)
            table[IX_MATCH + row_role * 4 * CAP + t] = slot
        return carry

    def match_rows(first_role):
        lax.fori_loop(first_role, first_role + 4, match, 0)

    done = []

    def sent(*copies):
        for one in copies:
            one.wait_send()
            done.append(one)

    row_lag, gap = 0.75, 0.9
    steps = []
    for k in each:
        steps += [
            (1 + gap * k, lambda k=k: blocks1(C, c1, c2, IX_C1B, IX_C1O, k)),
            (2 + gap * k, lambda k=k: blocks2(C, c2, c3, IX_C2, k)),
            (3 + gap * k, lambda k=k: blocks3_column(k)),
            (4 + gap * k, lambda k=k: (landed(c4b[k]), start(c5[k]))),
            (1 + gap * k + row_lag, lambda k=k: blocks1(R, r1, r2, IX_R1B, IX_R1O, k)),
            (2 + gap * k + row_lag, lambda k=k: blocks2(R, r2, r3, IX_R2, k)),
            (3 + gap * k + row_lag, lambda k=k: blocks3_row(k)),
            (4 + gap * k + row_lag, lambda k=k: (landed(r4b[k]), start(r5[k], f[1][k]))),
            (4.2 + gap * k + row_lag, lambda k=k: (landed(r4a[k]), start(f[2][k]))),
            (5 + gap * k + row_lag, lambda k=k: (landed(r5[k]), start(f[3][k]))),
        ]
    steps += [
        (0.9, lambda: lists1(C, c1m, c2m, IX_C1B, IX_C1O)),
        (1.1, lambda: lists1(R, r1m, r2m, IX_R1B, IX_R1O)),
        (1.3, lambda: lists2(C, c2m, c3m, IX_C2)),
        (1.8, lambda: trace_step(0)),
        (2.1, lambda: lists2(R, r2m, r3m, IX_R2)),
        (2.2, lambda: lists3(C, c3m, (c4bm, c4am), IX_C3)),
        (2.9, lambda: lists3(R, r3m, (r4bm, r4am), IX_R3)),
        (3.1, lambda: trace_step(1)),
        (3.2, lambda: (landed(c4bm), start(c5m))),
        (3.8, lambda: (landed(r4bm), start(r5m))),
        (3.85, lambda: trace_step(2)),
        (4.05, lambda: (landed(r4am, r5m), start(fm))),
        (4.1, lambda: (landed(c4am, c5m), match_rows(0))),
        (4.3, lambda: trace_step(3)),
        (5.05, lambda: (landed(fm), match_rows(4))),
        (5.1, lambda: trace_step(4)),
        (5.5, lambda: sent(c1m, *c1, r0m, *r0, r1m, *r1, c2m, *c2, r2m, *r2)),
        (5.85, lambda: trace_step(5)),
    ]
    for _, step in sorted(steps, key=lambda one: one[0]):
        step()

    for k in each:
        landed(c4a[k], c5[k])

    column_of = (x, xb, xa, xd)
    line_by_role = (
        [core * 4 + position for position in (z, zb, za, zd)]
        + [(1 - core) * 4 + position for position in (z, za, zb, zd)]
    )

    def product(row_roles):
        for c in range(4):
            left = []
            for role in row_roles:
                base = IX_MATCH + (role * 4 + c) * CAP
                left.append(jnp.concatenate([rows[role][table[base + j]] for j in range(CAP)], axis=1))
            right = columns_panel[c * CAP:(c + 1) * CAP].reshape(CAP * BS, BS)
            total = jnp.dot(
                jnp.concatenate(left, axis=0), right, preferred_element_type=jnp.float32
            )
            q = column_of[c]
            for i, role in enumerate(row_roles):
                line = line_by_role[role]
                kept = jnp.where(filter_mask[q, line] != 0, total[i * BS:(i + 1) * BS], 0.0)
                out[line, :, pl.ds(pl.multiple_of(q * BS, BS), BS)] = kept.astype(jnp.bfloat16)

    product((0, 1))
    product((2, 3))
    for role in (0, 1):
        landed(*f[role])
    product((4, 5))
    sent(c3m, *c3, r3m, *r3, c4am, c4bm, r4am, r4bm, c5m, r5m, fm, *c4b, *trace[:5])
    for role in (2, 3):
        landed(*f[role])
    product((6, 7))

    trace_step(6)
    occupation[0, 0] = jnp.sum(tacc[7])
    for one in remote:
        if not any(one is other_one for other_one in done):
            one.wait_send()


def on_device(values, pattern, filter_mask, assignment):
    hbm = pl.BlockSpec(memory_space=pltpu.HBM)
    parts = lambda count: [pltpu.VMEM((count, PART, BS), jnp.bfloat16)] * CHUNKS
    lists = lambda *counts: [pltpu.SMEM((count * LIST,), jnp.int32) for count in counts]

    def path(final):
        return [
            *parts(4 * CAP + 1), *parts(2 * CAP), *parts(CAP), *parts(2 * CAP + 1),
            *parts(2 * CAP + 1), *lists(4, 2, 1, 1, 1, 1, 1, final),
        ]

    product, occupation = pl.pallas_call(
        kernel,
        out_shape=(
            jax.ShapeDtypeStruct((8, BS, 4 * BS), jnp.bfloat16),
            jax.ShapeDtypeStruct((1, 1), jnp.float32),
        ),
        in_specs=[hbm] * 4,
        out_specs=(pl.BlockSpec(memory_space=pltpu.VMEM), pl.BlockSpec(memory_space=pltpu.SMEM)),
        scratch_shapes=[
            pltpu.VMEM((4, 8, BS, BS), jnp.bfloat16),
            pltpu.SMEM((4, 8), jnp.int32),
            pltpu.SMEM((4, 8), jnp.int32),
            pltpu.SMEM((4, 8), jnp.int32),
            pltpu.SMEM((64,), jnp.int32),
            *[pltpu.VMEM((4, 4, PART, BS), jnp.bfloat16)] * CHUNKS,
            *path(4),
            *path(8),
            pltpu.VMEM((4 * CAP, BS, BS), jnp.bfloat16),
            *[pltpu.VMEM((CAP + 1, BS, BS), jnp.bfloat16)] * 8,
            pltpu.VMEM((8, 8, BS), jnp.float32),
            pltpu.VMEM((7, 8, BS), jnp.float32),
            pltpu.SMEM((IX_MATCH + 8 * 4 * CAP,), jnp.int32),
            pltpu.SemaphoreType.DMA((7,)),
            pltpu.SemaphoreType.DMA((COPIES,)),
            pltpu.SemaphoreType.DMA((COPIES,)),
        ],
        compiler_params=pltpu.CompilerParams(
            collective_id=0, has_side_effects=True, vmem_limit_bytes=52 * 1024 * 1024
        ),
        cost_estimate=pl.CostEstimate(
            flops=2 * 192 * BS**3, bytes_accessed=4 * 1024 * 1024, transcendentals=0
        ),
    )(values.reshape(8, BS, 4 * BS), pattern.T, filter_mask.T, assignment)
    return product.reshape(values.shape), occupation[0, 0]


def solution(mesh):
    in_specs = (P("row", "col"), P("row", "col"), P("row", "col"), P())
    out_specs = (P("row", "col"), P())
    return jax.shard_map(
        on_device, mesh=mesh, in_specs=in_specs, out_specs=out_specs, check_vma=False
    )
```

```python
import jax
import jax.numpy as jnp
from jax import lax
from jax.experimental import pallas as pl
from jax.experimental.pallas import tpu as pltpu
from jax.sharding import PartitionSpec as P

BS = 128
CAP = 6
LIST = 128
CHUNKS = 2
PART = BS // CHUNKS
COPIES = 96
IX_C1B, IX_C1O, IX_C2, IX_C3, IX_R1B, IX_R1O, IX_R2, IX_R3 = range(0, 64, 8)
IX_MATCH = 64
MESH = pl.DeviceIdType.MESH


class Path:
    def __init__(self, refs):
        refs = list(refs)
        take = lambda: [refs.pop(0) for _ in range(CHUNKS)]
        self.first, self.send, self.send2 = take(), take(), take()
        self.second, self.third = take(), take()
        (self.l_own, self.l_in1, self.l_send2, self.l_own2, self.l_in2,
         self.l_send3, self.l_in3, self.l_final) = refs


def kernel(values, pattern_in, filter_in, assignment_in, out, occupation, *refs):
    refs = list(refs)
    take = lambda count: [refs.pop(0) for _ in range(count)]
    own, pattern, other_pattern, filter_mask, assignment = take(5)
    other = take(CHUNKS)
    C, R = Path(take(5 * CHUNKS + 8)), Path(take(5 * CHUNKS + 8))
    columns_panel, = take(1)
    rows = take(8)
    tacc, trecv, table, load_sem, send_sem, recv_sem = take(6)

    row, col = lax.axis_index("row"), lax.axis_index("col")
    x, y_hi = row // 2, row % 2
    y_lo, z, core = col // 8, (col // 2) % 4, col % 2

    def partners(position, core):
        even, odd = position + 1 - 2 * (position % 2), 3 - position
        a = even * (1 - core) + odd * core
        b = odd * (1 - core) + even * core
        return a, b, (position + 2) % 4

    xa, xb, xd = partners(x, core)
    za, zb, zd = partners(z, 1 - core)
    dev_xa, dev_xb = (xa * 2 + y_hi, col), (xb * 2 + y_hi, col)
    dev_yh = (x * 2 + 1 - y_hi, col)
    dev_za = (row, y_lo * 8 + za * 2 + core)
    dev_zb = (row, y_lo * 8 + zb * 2 + core)
    dev_yl = (row, (1 - y_lo) * 8 + z * 2 + core)
    other_col = col + 1 - 2 * core
    dev_core = (row, other_col)

    remote = []

    def copy(src, dst, device):
        index = len(remote)
        remote.append(pltpu.make_async_remote_copy(
            src_ref=src, dst_ref=dst, send_sem=send_sem.at[index],
            recv_sem=recv_sem.at[index], device_id=device, device_id_type=MESH,
        ))
        return remote[-1]

    def start(*copies):
        for one in copies:
            one.start()

    def landed(*copies):
        for one in copies:
            one.wait_recv()

    small = [
        pltpu.make_async_copy(src, dst, load_sem.at[4 + i])
        for i, (src, dst) in enumerate(
            ((pattern_in, pattern), (assignment_in, assignment), (filter_in, filter_mask))
        )
    ]
    loads = [
        pltpu.make_async_copy(values.at[:, :, q * BS:(q + 1) * BS], own.at[q], load_sem.at[q])
        for q in range(4)
    ]
    start(*small, *loads)
    barrier = pltpu.get_barrier_semaphore()
    for device in (dev_xa, dev_xb, dev_yh, dev_za, dev_zb, dev_yl, dev_core):
        pl.semaphore_signal(barrier, inc=1, device_id=device, device_id_type=MESH)

    zero = jnp.zeros((PART, BS), jnp.bfloat16)
    for path in (C, R):
        for k in range(CHUNKS):
            path.first[k][4 * CAP] = zero
            path.second[k][2 * CAP] = zero
            path.third[k][2 * CAP] = zero
    for ref in rows:
        ref[CAP] = jnp.zeros((BS, BS), jnp.bfloat16)

    def part(k):
        return slice(k * PART, (k + 1) * PART)

    def rank(flags):
        count = jnp.int32(0)
        places = [jnp.int32(0)] * CAP
        for t, flag in enumerate(flags):
            for j in range(min(CAP, t + 1)):
                places[j] = jnp.where((flag != 0) & (count == j), t, places[j])
            count = count + flag
        return places, count

    def rank_column(role, q):
        places, count = rank([pattern[q, t] for t in range(8)])
        C.l_own[role * LIST] = count
        for j in range(CAP):
            name = assignment[row * 8 + places[j]]
            C.l_own[role * LIST + 1 + j] = jnp.where(j < count, name, -1)
        return q, places, count

    def pack_column(ranked, k, dst, first):
        q, places, count = ranked
        for j in range(CAP):
            block = own[q, places[j], part(k), :]
            dst[first + j] = jnp.where(j < count, block, zero)

    for one in small:
        one.wait()
    ranked_columns = [rank_column(role, q) for role, q in enumerate((x, xb, xa, xd))]
    for one in loads:
        one.wait()
    for k in range(CHUNKS):
        pack_column(ranked_columns[2], k, C.send[k], 0)
        pack_column(ranked_columns[3], k, C.send[k], CAP)

    half = (1 - core) * 4
    r0m = copy(pattern, other_pattern, dev_core)
    r0 = [copy(own.at[:, pl.ds(half, 4), part(k)], other[k], dev_core) for k in range(CHUNKS)]

    def first_copies(path, device):
        return (
            copy(path.l_own.at[pl.ds(2 * LIST, 2 * LIST)], path.l_in1, device),
            [copy(path.send[k], path.first[k].at[pl.ds(2 * CAP, 2 * CAP)], device) for k in range(CHUNKS)],
        )

    c1m, c1 = first_copies(C, dev_xa)
    r1m, r1 = first_copies(R, dev_za)

    pl.semaphore_wait(barrier, 7)
    start(r0m, c1m)
    for k in range(CHUNKS):
        start(r0[k], c1[k])
    for k in range(CHUNKS):
        pack_column(ranked_columns[0], k, C.first[k], 0)
        pack_column(ranked_columns[1], k, C.first[k], CAP)

    def rank_row(role, q):
        line = core * 4 + q
        places, count = rank(
            [pattern[t, line] for t in range(4)] + [other_pattern[t, line] for t in range(4)]
        )
        R.l_own[role * LIST] = count
        for j in range(CAP):
            name = jnp.where(places[j] < 4, col * 4, other_col * 4 - 4) + places[j]
            R.l_own[role * LIST + 1 + j] = jnp.where(j < count, name, -1)
        return line, q, places, count

    def pack_row(ranked, k, dst, first):
        line, q, places, count = ranked
        for j in range(CAP):
            mine = places[j] < 4
            place = jnp.where(mine, places[j], places[j] - 4)
            block = jnp.where(mine, own[place, line, part(k), :], other[k][place, q])
            dst[first + j] = jnp.where(j < count, block, zero)

    landed(r0m)
    ranked_rows = [rank_row(role, q) for role, q in enumerate((z, zb, za, zd))]
    start(r1m)
    for k in range(CHUNKS):
        landed(r0[k])
        pack_row(ranked_rows[2], k, R.send[k], 0)
        pack_row(ranked_rows[3], k, R.send[k], CAP)
        start(r1[k])

    def merge(l1, at1, l2, at2, lout, ix, base1, base2, zero_slot):
        n1, n2 = l1[at1], l2[at2]
        lout[0] = n1 + n2
        for j in range(CAP):
            rest = jnp.clip(j - n1, 0, CAP - 1)
            in1, in2 = j < n1, j - n1 < n2
            lout[1 + j] = jnp.where(in1, l1[at1 + 1 + j], jnp.where(in2, l2[at2 + 1 + rest], -1))
            table[ix + j] = jnp.where(in1, base1 + j, jnp.where(in2, base2 + rest, zero_slot))

    def move(src, ix, dst):
        for j in range(CAP):
            dst[j] = src[table[ix + j]]

    def six(ref, k, first=0):
        return ref[k].at[pl.ds(first, CAP)]

    def later_copies(path, device2, device3):
        return (
            copy(path.l_send2, path.l_in2, device2),
            [copy(path.send2[k], six(path.second, k, CAP), device2) for k in range(CHUNKS)],
            copy(path.l_send3, path.l_in3, device3),
            [copy(six(path.third, k), six(path.third, k, CAP), device3) for k in range(CHUNKS)],
        )

    c2m, c2, c3m, c3 = later_copies(C, dev_xb, dev_yh)
    r2m, r2, r3m, r3 = later_copies(R, dev_zb, dev_yl)

    def lists1(path, in_copy, out_copy, ix_b, ix_o):
        landed(in_copy)
        merge(path.l_own, LIST, path.l_in1, LIST, path.l_send2, ix_b, CAP, 3 * CAP, 4 * CAP)
        start(out_copy)
        merge(path.l_own, 0, path.l_in1, 0, path.l_own2, ix_o, 0, 2 * CAP, 4 * CAP)

    def lists2(path, in_copy, out_copy, ix):
        landed(in_copy)
        merge(path.l_own2, 0, path.l_in2, 0, path.l_send3, ix, 0, CAP, 2 * CAP)
        start(out_copy)

    def lists3(path, in_copy, out_copies, ix):
        landed(in_copy)
        merge(path.l_send3, 0, path.l_in3, 0, path.l_final, ix, 0, CAP, 2 * CAP)
        start(*out_copies)

    def blocks1(path, in_copies, out_copies, ix_b, ix_o, k):
        landed(in_copies[k])
        move(path.first[k], ix_b, path.send2[k])
        start(out_copies[k])
        move(path.first[k], ix_o, path.second[k])

    def blocks2(path, in_copies, out_copies, ix, k):
        landed(in_copies[k])
        move(path.second[k], ix, path.third[k])
        start(out_copies[k])

    def names(path, role):
        return path.l_final.at[pl.ds(role * LIST, LIST)]

    c4am, c4bm = copy(names(C, 0), names(C, 2), dev_xa), copy(names(C, 0), names(C, 1), dev_xb)
    c5m = copy(names(C, 1), names(C, 3), dev_xa)
    r4am, r4bm = copy(names(R, 0), names(R, 2), dev_za), copy(names(R, 0), names(R, 1), dev_zb)
    r5m = copy(names(R, 1), names(R, 3), dev_za)
    fm = copy(R.l_final.at[pl.ds(0, 4 * LIST)], R.l_final.at[pl.ds(4 * LIST, 4 * LIST)], dev_core)

    def column(role, k):
        return columns_panel.at[pl.ds(role * CAP, CAP), part(k)]

    def line_of(role, k):
        return rows[role].at[pl.ds(0, CAP), part(k)]

    each = range(CHUNKS)
    c4a = [copy(column(0, k), column(2, k), dev_xa) for k in each]
    c4b = [copy(column(0, k), column(1, k), dev_xb) for k in each]
    c5 = [copy(column(1, k), column(3, k), dev_xa) for k in each]
    r4a = [copy(line_of(0, k), line_of(2, k), dev_za) for k in each]
    r4b = [copy(line_of(0, k), line_of(1, k), dev_zb) for k in each]
    r5 = [copy(line_of(1, k), line_of(3, k), dev_za) for k in each]
    f = [[copy(line_of(role, k), line_of(4 + role, k), dev_core) for k in each] for role in range(4)]

    def blocks3_column(k):
        landed(c3[k])
        for j in range(CAP):
            columns_panel[j, part(k), :] = C.third[k][table[IX_C3 + j]]
        start(c4b[k], c4a[k])

    def blocks3_row(k):
        landed(r3[k])
        for j in range(CAP):
            rows[0][j, part(k), :] = R.third[k][table[IX_R3 + j]]
        start(r4b[k], r4a[k], f[0][k])

    def squares(ref):
        total = jnp.zeros((8, BS), jnp.float32)
        for i in range(2 * CAP):
            block = ref[i].astype(jnp.float32)
            total = total + jnp.sum((block * block).reshape(PART // 8, 8, BS), axis=0)
        return total

    trace_devices = (dev_core, dev_xa, dev_za, dev_xb, dev_zb, dev_yh, dev_yl)
    trace = [copy(tacc.at[i], trecv.at[i], trace_devices[i]) for i in range(7)]

    def trace_step(i):
        landed(trace[i])
        tacc[i + 1] = tacc[i] + trecv[i]
        if i < 6:
            start(trace[i + 1])

    for k in each:
        pack_row(ranked_rows[0], k, R.first[k], 0)
        pack_row(ranked_rows[1], k, R.first[k], CAP)
    total = jnp.zeros((8, BS), jnp.float32)
    for k in each:
        total = total + squares(C.send[k])
        total = total + squares(C.first[k])
    tacc[0] = total
    start(trace[0])

    def match(row_role, carry):
        have = [R.l_final[row_role * LIST + 1 + i] for i in range(CAP)]
        for t in range(4 * CAP):
            wanted = C.l_final[(t // CAP) * LIST + 1 + t % CAP]
            slot = jnp.int32(CAP)
            for i in range(CAP):
                slot = jnp.where(have[i] == wanted, i, slot)
            table[IX_MATCH + row_role * 4 * CAP + t] = slot
        return carry

    def match_rows(first_role):
        lax.fori_loop(first_role, first_role + 4, match, 0)

    done = []

    def sent(*copies):
        for one in copies:
            one.wait_send()
            done.append(one)

    row_lag = 0.75
    steps = []
    for k in each:
        steps += [
            (1 + k, lambda k=k: blocks1(C, c1, c2, IX_C1B, IX_C1O, k)),
            (2 + k, lambda k=k: blocks2(C, c2, c3, IX_C2, k)),
            (3 + k, lambda k=k: blocks3_column(k)),
            (4 + k, lambda k=k: (landed(c4b[k]), start(c5[k]))),
            (1 + k + row_lag, lambda k=k: blocks1(R, r1, r2, IX_R1B, IX_R1O, k)),
            (2 + k + row_lag, lambda k=k: blocks2(R, r2, r3, IX_R2, k)),
            (3 + k + row_lag, lambda k=k: blocks3_row(k)),
            (4 + k + row_lag, lambda k=k: (landed(r4b[k]), start(r5[k], f[1][k]))),
            (4.2 + k + row_lag, lambda k=k: (landed(r4a[k]), start(f[2][k]))),
            (5 + k + row_lag, lambda k=k: (landed(r5[k]), start(f[3][k]))),
        ]
    steps += [
        (0.9, lambda: lists1(C, c1m, c2m, IX_C1B, IX_C1O)),
        (1.1, lambda: lists1(R, r1m, r2m, IX_R1B, IX_R1O)),
        (1.3, lambda: lists2(C, c2m, c3m, IX_C2)),
        (1.8, lambda: trace_step(0)),
        (2.1, lambda: lists2(R, r2m, r3m, IX_R2)),
        (2.2, lambda: lists3(C, c3m, (c4bm, c4am), IX_C3)),
        (2.9, lambda: lists3(R, r3m, (r4bm, r4am), IX_R3)),
        (3.1, lambda: trace_step(1)),
        (3.2, lambda: (landed(c4bm), start(c5m))),
        (3.8, lambda: (landed(r4bm), start(r5m))),
        (3.85, lambda: trace_step(2)),
        (4.05, lambda: (landed(r4am, r5m), start(fm))),
        (4.1, lambda: (landed(c4am, c5m), match_rows(0))),
        (4.3, lambda: trace_step(3)),
        (5.05, lambda: (landed(fm), match_rows(4))),
        (5.1, lambda: trace_step(4)),
        (5.5, lambda: sent(c1m, *c1, r0m, *r0, r1m, *r1, c2m, *c2, r2m, *r2)),
        (5.85, lambda: trace_step(5)),
    ]
    for _, step in sorted(steps, key=lambda one: one[0]):
        step()

    for k in each:
        landed(c4a[k], c5[k])

    column_of = (x, xb, xa, xd)
    line_by_role = (
        [core * 4 + position for position in (z, zb, za, zd)]
        + [(1 - core) * 4 + position for position in (z, za, zb, zd)]
    )

    def product(row_roles):
        for c in range(4):
            left = []
            for role in row_roles:
                base = IX_MATCH + (role * 4 + c) * CAP
                left.append(jnp.concatenate([rows[role][table[base + j]] for j in range(CAP)], axis=1))
            right = columns_panel[c * CAP:(c + 1) * CAP].reshape(CAP * BS, BS)
            total = jnp.dot(
                jnp.concatenate(left, axis=0), right, preferred_element_type=jnp.float32
            )
            q = column_of[c]
            for i, role in enumerate(row_roles):
                line = line_by_role[role]
                kept = jnp.where(filter_mask[q, line] != 0, total[i * BS:(i + 1) * BS], 0.0)
                out[line, :, pl.ds(pl.multiple_of(q * BS, BS), BS)] = kept.astype(jnp.bfloat16)

    product((0, 1))
    product((2, 3))
    for role in (0, 1):
        landed(*f[role])
    product((4, 5))
    sent(c3m, *c3, r3m, *r3, c4am, c4bm, r4am, r4bm, c5m, r5m, fm, *c4b, *trace[:5])
    for role in (2, 3):
        landed(*f[role])
    product((6, 7))

    trace_step(6)
    occupation[0, 0] = jnp.sum(tacc[7])
    for one in remote:
        if not any(one is other_one for other_one in done):
            one.wait_send()


def on_device(values, pattern, filter_mask, assignment):
    hbm = pl.BlockSpec(memory_space=pltpu.HBM)
    parts = lambda count: [pltpu.VMEM((count, PART, BS), jnp.bfloat16)] * CHUNKS
    lists = lambda *counts: [pltpu.SMEM((count * LIST,), jnp.int32) for count in counts]

    def path(final):
        return [
            *parts(4 * CAP + 1), *parts(2 * CAP), *parts(CAP), *parts(2 * CAP + 1),
            *parts(2 * CAP + 1), *lists(4, 2, 1, 1, 1, 1, 1, final),
        ]

    product, occupation = pl.pallas_call(
        kernel,
        out_shape=(
            jax.ShapeDtypeStruct((8, BS, 4 * BS), jnp.bfloat16),
            jax.ShapeDtypeStruct((1, 1), jnp.float32),
        ),
        in_specs=[hbm] * 4,
        out_specs=(pl.BlockSpec(memory_space=pltpu.VMEM), pl.BlockSpec(memory_space=pltpu.SMEM)),
        scratch_shapes=[
            pltpu.VMEM((4, 8, BS, BS), jnp.bfloat16),
            pltpu.SMEM((4, 8), jnp.int32),
            pltpu.SMEM((4, 8), jnp.int32),
            pltpu.SMEM((4, 8), jnp.int32),
            pltpu.SMEM((64,), jnp.int32),
            *[pltpu.VMEM((4, 4, PART, BS), jnp.bfloat16)] * CHUNKS,
            *path(4),
            *path(8),
            pltpu.VMEM((4 * CAP, BS, BS), jnp.bfloat16),
            *[pltpu.VMEM((CAP + 1, BS, BS), jnp.bfloat16)] * 8,
            pltpu.VMEM((8, 8, BS), jnp.float32),
            pltpu.VMEM((7, 8, BS), jnp.float32),
            pltpu.SMEM((IX_MATCH + 8 * 4 * CAP,), jnp.int32),
            pltpu.SemaphoreType.DMA((7,)),
            pltpu.SemaphoreType.DMA((COPIES,)),
            pltpu.SemaphoreType.DMA((COPIES,)),
        ],
        compiler_params=pltpu.CompilerParams(
            collective_id=0, has_side_effects=True, vmem_limit_bytes=52 * 1024 * 1024
        ),
        cost_estimate=pl.CostEstimate(
            flops=2 * 192 * BS**3, bytes_accessed=4 * 1024 * 1024, transcendentals=0
        ),
    )(values.reshape(8, BS, 4 * BS), pattern.T, filter_mask.T, assignment)
    return product.reshape(values.shape), occupation[0, 0]


def solution(mesh):
    in_specs = (P("row", "col"), P("row", "col"), P("row", "col"), P())
    out_specs = (P("row", "col"), P())
    return jax.shard_map(
        on_device, mesh=mesh, in_specs=in_specs, out_specs=out_specs, check_vma=False
    )
```

```python
import jax
import jax.numpy as jnp
from jax import lax
from jax.experimental import pallas as pl
from jax.experimental.pallas import tpu as pltpu
from jax.sharding import PartitionSpec as P

BS = 128
CAP = 6
LIST = 128
CHUNKS = 2
PART = BS // CHUNKS
COPIES = 96
IX_C1B, IX_C1O, IX_C2, IX_C3, IX_R1B, IX_R1O, IX_R2, IX_R3 = range(0, 64, 8)
IX_MATCH = 64
MESH = pl.DeviceIdType.MESH


class Path:
    def __init__(self, refs):
        refs = list(refs)
        take = lambda: [refs.pop(0) for _ in range(CHUNKS)]
        self.first, self.send, self.send2 = take(), take(), take()
        self.second, self.third = take(), take()
        (self.l_own, self.l_in1, self.l_send2, self.l_own2, self.l_in2,
         self.l_send3, self.l_in3, self.l_final) = refs


def kernel(values, pattern_in, filter_in, assignment_in, out, occupation, *refs):
    refs = list(refs)
    take = lambda count: [refs.pop(0) for _ in range(count)]
    own, pattern, other_pattern, filter_mask, assignment = take(5)
    other = take(CHUNKS)
    C, R = Path(take(5 * CHUNKS + 8)), Path(take(5 * CHUNKS + 8))
    columns_panel, = take(1)
    rows = take(8)
    tacc, trecv, table, load_sem, send_sem, recv_sem = take(6)

    row, col = lax.axis_index("row"), lax.axis_index("col")
    x, y_hi = row // 2, row % 2
    y_lo, z, core = col // 8, (col // 2) % 4, col % 2

    def partners(position):
        even, odd = position + 1 - 2 * (position % 2), 3 - position
        a = even * (1 - core) + odd * core
        b = odd * (1 - core) + even * core
        return a, b, (position + 2) % 4

    xa, xb, xd = partners(x)
    za, zb, zd = partners(z)
    dev_xa, dev_xb = (xa * 2 + y_hi, col), (xb * 2 + y_hi, col)
    dev_yh = (x * 2 + 1 - y_hi, col)
    dev_za = (row, y_lo * 8 + za * 2 + core)
    dev_zb = (row, y_lo * 8 + zb * 2 + core)
    dev_yl = (row, (1 - y_lo) * 8 + z * 2 + core)
    other_col = col + 1 - 2 * core
    dev_core = (row, other_col)

    remote = []

    def copy(src, dst, device):
        index = len(remote)
        remote.append(pltpu.make_async_remote_copy(
            src_ref=src, dst_ref=dst, send_sem=send_sem.at[index],
            recv_sem=recv_sem.at[index], device_id=device, device_id_type=MESH,
        ))
        return remote[-1]

    def start(*copies):
        for one in copies:
            one.start()

    def landed(*copies):
        for one in copies:
            one.wait_recv()

    small = [
        pltpu.make_async_copy(src, dst, load_sem.at[4 + i])
        for i, (src, dst) in enumerate(
            ((pattern_in, pattern), (assignment_in, assignment), (filter_in, filter_mask))
        )
    ]
    loads = [
        pltpu.make_async_copy(values.at[:, :, q * BS:(q + 1) * BS], own.at[q], load_sem.at[q])
        for q in range(4)
    ]
    start(*small, *loads)
    barrier = pltpu.get_barrier_semaphore()
    for device in (dev_xa, dev_xb, dev_yh, dev_za, dev_zb, dev_yl, dev_core):
        pl.semaphore_signal(barrier, inc=1, device_id=device, device_id_type=MESH)

    zero = jnp.zeros((PART, BS), jnp.bfloat16)
    for path in (C, R):
        for k in range(CHUNKS):
            path.first[k][4 * CAP] = zero
            path.second[k][2 * CAP] = zero
            path.third[k][2 * CAP] = zero
    for ref in rows:
        ref[CAP] = jnp.zeros((BS, BS), jnp.bfloat16)

    def part(k):
        return slice(k * PART, (k + 1) * PART)

    def rank(flags):
        count = jnp.int32(0)
        places = [jnp.int32(0)] * CAP
        for t, flag in enumerate(flags):
            for j in range(min(CAP, t + 1)):
                places[j] = jnp.where((flag != 0) & (count == j), t, places[j])
            count = count + flag
        return places, count

    def rank_column(role, q):
        places, count = rank([pattern[q, t] for t in range(8)])
        C.l_own[role * LIST] = count
        for j in range(CAP):
            name = assignment[row * 8 + places[j]]
            C.l_own[role * LIST + 1 + j] = jnp.where(j < count, name, -1)
        return q, places, count

    def pack_column(ranked, k, dst, first):
        q, places, count = ranked
        for j in range(CAP):
            block = own[q, places[j], part(k), :]
            dst[first + j] = jnp.where(j < count, block, zero)

    for one in small:
        one.wait()
    ranked_columns = [rank_column(role, q) for role, q in enumerate((x, xb, xa, xd))]
    for one in loads:
        one.wait()
    for k in range(CHUNKS):
        pack_column(ranked_columns[2], k, C.send[k], 0)
        pack_column(ranked_columns[3], k, C.send[k], CAP)

    half = (1 - core) * 4
    r0m = copy(pattern, other_pattern, dev_core)
    r0 = [copy(own.at[:, pl.ds(half, 4), part(k)], other[k], dev_core) for k in range(CHUNKS)]

    def first_copies(path, device):
        return (
            copy(path.l_own.at[pl.ds(2 * LIST, 2 * LIST)], path.l_in1, device),
            [copy(path.send[k], path.first[k].at[pl.ds(2 * CAP, 2 * CAP)], device) for k in range(CHUNKS)],
        )

    c1m, c1 = first_copies(C, dev_xa)
    r1m, r1 = first_copies(R, dev_za)

    pl.semaphore_wait(barrier, 7)
    start(r0m, c1m)
    for k in range(CHUNKS):
        start(c1[k], r0[k])
    for k in range(CHUNKS):
        pack_column(ranked_columns[0], k, C.first[k], 0)
        pack_column(ranked_columns[1], k, C.first[k], CAP)

    def rank_row(role, q):
        line = core * 4 + q
        places, count = rank(
            [pattern[t, line] for t in range(4)] + [other_pattern[t, line] for t in range(4)]
        )
        R.l_own[role * LIST] = count
        for j in range(CAP):
            name = jnp.where(places[j] < 4, col * 4, other_col * 4 - 4) + places[j]
            R.l_own[role * LIST + 1 + j] = jnp.where(j < count, name, -1)
        return line, q, places, count

    def pack_row(ranked, k, dst, first):
        line, q, places, count = ranked
        for j in range(CAP):
            mine = places[j] < 4
            place = jnp.where(mine, places[j], places[j] - 4)
            block = jnp.where(mine, own[place, line, part(k), :], other[k][place, q])
            dst[first + j] = jnp.where(j < count, block, zero)

    landed(r0m)
    ranked_rows = [rank_row(role, q) for role, q in enumerate((z, zb, za, zd))]
    start(r1m)
    for k in range(CHUNKS):
        landed(r0[k])
        pack_row(ranked_rows[2], k, R.send[k], 0)
        pack_row(ranked_rows[3], k, R.send[k], CAP)
        start(r1[k])

    def merge(l1, at1, l2, at2, lout, ix, base1, base2, zero_slot):
        n1, n2 = l1[at1], l2[at2]
        lout[0] = n1 + n2
        for j in range(CAP):
            rest = jnp.clip(j - n1, 0, CAP - 1)
            in1, in2 = j < n1, j - n1 < n2
            lout[1 + j] = jnp.where(in1, l1[at1 + 1 + j], jnp.where(in2, l2[at2 + 1 + rest], -1))
            table[ix + j] = jnp.where(in1, base1 + j, jnp.where(in2, base2 + rest, zero_slot))

    def move(src, ix, dst):
        for j in range(CAP):
            dst[j] = src[table[ix + j]]

    def six(ref, k, first=0):
        return ref[k].at[pl.ds(first, CAP)]

    def later_copies(path, device2, device3):
        return (
            copy(path.l_send2, path.l_in2, device2),
            [copy(path.send2[k], six(path.second, k, CAP), device2) for k in range(CHUNKS)],
            copy(path.l_send3, path.l_in3, device3),
            [copy(six(path.third, k), six(path.third, k, CAP), device3) for k in range(CHUNKS)],
        )

    c2m, c2, c3m, c3 = later_copies(C, dev_xb, dev_yh)
    r2m, r2, r3m, r3 = later_copies(R, dev_zb, dev_yl)

    def lists1(path, in_copy, out_copy, ix_b, ix_o):
        landed(in_copy)
        merge(path.l_own, LIST, path.l_in1, LIST, path.l_send2, ix_b, CAP, 3 * CAP, 4 * CAP)
        start(out_copy)
        merge(path.l_own, 0, path.l_in1, 0, path.l_own2, ix_o, 0, 2 * CAP, 4 * CAP)

    def lists2(path, in_copy, out_copy, ix):
        landed(in_copy)
        merge(path.l_own2, 0, path.l_in2, 0, path.l_send3, ix, 0, CAP, 2 * CAP)
        start(out_copy)

    def lists3(path, in_copy, out_copies, ix):
        landed(in_copy)
        merge(path.l_send3, 0, path.l_in3, 0, path.l_final, ix, 0, CAP, 2 * CAP)
        start(*out_copies)

    def blocks1(path, in_copies, out_copies, ix_b, ix_o, k):
        landed(in_copies[k])
        move(path.first[k], ix_b, path.send2[k])
        start(out_copies[k])
        move(path.first[k], ix_o, path.second[k])

    def blocks2(path, in_copies, out_copies, ix, k):
        landed(in_copies[k])
        move(path.second[k], ix, path.third[k])
        start(out_copies[k])

    def names(path, role):
        return path.l_final.at[pl.ds(role * LIST, LIST)]

    c4am, c4bm = copy(names(C, 0), names(C, 2), dev_xa), copy(names(C, 0), names(C, 1), dev_xb)
    c5m = copy(names(C, 1), names(C, 3), dev_xa)
    r4am, r4bm = copy(names(R, 0), names(R, 2), dev_za), copy(names(R, 0), names(R, 1), dev_zb)
    r5m = copy(names(R, 1), names(R, 3), dev_za)
    fm = copy(R.l_final.at[pl.ds(0, 4 * LIST)], R.l_final.at[pl.ds(4 * LIST, 4 * LIST)], dev_core)

    def column(role, k):
        return columns_panel.at[pl.ds(role * CAP, CAP), part(k)]

    def line_of(role, k):
        return rows[role].at[pl.ds(0, CAP), part(k)]

    each = range(CHUNKS)
    c4a = [copy(column(0, k), column(2, k), dev_xa) for k in each]
    c4b = [copy(column(0, k), column(1, k), dev_xb) for k in each]
    c5 = [copy(column(1, k), column(3, k), dev_xa) for k in each]
    r4a = [copy(line_of(0, k), line_of(2, k), dev_za) for k in each]
    r4b = [copy(line_of(0, k), line_of(1, k), dev_zb) for k in each]
    r5 = [copy(line_of(1, k), line_of(3, k), dev_za) for k in each]
    f = [[copy(line_of(role, k), line_of(4 + role, k), dev_core) for k in each] for role in range(4)]

    def blocks3_column(k):
        landed(c3[k])
        for j in range(CAP):
            columns_panel[j, part(k), :] = C.third[k][table[IX_C3 + j]]
        start(c4b[k], c4a[k])

    def blocks3_row(k):
        landed(r3[k])
        for j in range(CAP):
            rows[0][j, part(k), :] = R.third[k][table[IX_R3 + j]]
        start(r4b[k], r4a[k], f[0][k])

    def squares(ref):
        total = jnp.zeros((8, BS), jnp.float32)
        for i in range(2 * CAP):
            block = ref[i].astype(jnp.float32)
            total = total + jnp.sum((block * block).reshape(PART // 8, 8, BS), axis=0)
        return total

    trace_devices = (dev_core, dev_xa, dev_za, dev_xb, dev_zb, dev_yh, dev_yl)
    trace = [copy(tacc.at[i], trecv.at[i], trace_devices[i]) for i in range(7)]

    def trace_step(i):
        landed(trace[i])
        tacc[i + 1] = tacc[i] + trecv[i]
        if i < 6:
            start(trace[i + 1])

    for k in each:
        pack_row(ranked_rows[0], k, R.first[k], 0)
        pack_row(ranked_rows[1], k, R.first[k], CAP)
    total = jnp.zeros((8, BS), jnp.float32)
    for k in each:
        total = total + squares(C.send[k])
        total = total + squares(C.first[k])
    tacc[0] = total
    start(trace[0])

    def match(row_role, carry):
        have = [R.l_final[row_role * LIST + 1 + i] for i in range(CAP)]
        for t in range(4 * CAP):
            wanted = C.l_final[(t // CAP) * LIST + 1 + t % CAP]
            slot = jnp.int32(CAP)
            for i in range(CAP):
                slot = jnp.where(have[i] == wanted, i, slot)
            table[IX_MATCH + row_role * 4 * CAP + t] = slot
        return carry

    def match_rows(first_role):
        lax.fori_loop(first_role, first_role + 4, match, 0)

    done = []

    def sent(*copies):
        for one in copies:
            one.wait_send()
            done.append(one)

    row_lag = 0.75
    steps = []
    for k in each:
        steps += [
            (1 + k, lambda k=k: blocks1(C, c1, c2, IX_C1B, IX_C1O, k)),
            (2 + k, lambda k=k: blocks2(C, c2, c3, IX_C2, k)),
            (3 + k, lambda k=k: blocks3_column(k)),
            (4 + k, lambda k=k: (landed(c4b[k]), start(c5[k]))),
            (1 + k + row_lag, lambda k=k: blocks1(R, r1, r2, IX_R1B, IX_R1O, k)),
            (2 + k + row_lag, lambda k=k: blocks2(R, r2, r3, IX_R2, k)),
            (3 + k + row_lag, lambda k=k: blocks3_row(k)),
            (4 + k + row_lag, lambda k=k: (landed(r4b[k]), start(r5[k], f[1][k]))),
            (4.2 + k + row_lag, lambda k=k: (landed(r4a[k]), start(f[2][k]))),
            (5 + k + row_lag, lambda k=k: (landed(r5[k]), start(f[3][k]))),
        ]
    steps += [
        (0.9, lambda: lists1(C, c1m, c2m, IX_C1B, IX_C1O)),
        (1.1, lambda: lists1(R, r1m, r2m, IX_R1B, IX_R1O)),
        (1.3, lambda: lists2(C, c2m, c3m, IX_C2)),
        (1.8, lambda: trace_step(0)),
        (2.1, lambda: lists2(R, r2m, r3m, IX_R2)),
        (2.2, lambda: lists3(C, c3m, (c4bm, c4am), IX_C3)),
        (2.9, lambda: lists3(R, r3m, (r4bm, r4am), IX_R3)),
        (3.1, lambda: trace_step(1)),
        (3.2, lambda: (landed(c4bm), start(c5m))),
        (3.8, lambda: (landed(r4bm), start(r5m))),
        (3.85, lambda: trace_step(2)),
        (4.05, lambda: (landed(r4am, r5m), start(fm))),
        (4.1, lambda: (landed(c4am, c5m), match_rows(0))),
        (4.3, lambda: trace_step(3)),
        (5.05, lambda: (landed(fm), match_rows(4))),
        (5.1, lambda: trace_step(4)),
        (5.5, lambda: sent(c1m, *c1, r0m, *r0, r1m, *r1, c2m, *c2, r2m, *r2)),
        (5.85, lambda: trace_step(5)),
    ]
    for _, step in sorted(steps, key=lambda one: one[0]):
        step()

    for k in each:
        landed(c4a[k], c5[k])

    column_of = (x, xb, xa, xd)
    line_by_role = (
        [core * 4 + position for position in (z, zb, za, zd)]
        + [(1 - core) * 4 + position for position in (z, za, zb, zd)]
    )

    def product(row_roles):
        for c in range(4):
            left = []
            for role in row_roles:
                base = IX_MATCH + (role * 4 + c) * CAP
                left.append(jnp.concatenate([rows[role][table[base + j]] for j in range(CAP)], axis=1))
            right = columns_panel[c * CAP:(c + 1) * CAP].reshape(CAP * BS, BS)
            total = jnp.dot(
                jnp.concatenate(left, axis=0), right, preferred_element_type=jnp.float32
            )
            q = column_of[c]
            for i, role in enumerate(row_roles):
                line = line_by_role[role]
                kept = jnp.where(filter_mask[q, line] != 0, total[i * BS:(i + 1) * BS], 0.0)
                out[line, :, pl.ds(pl.multiple_of(q * BS, BS), BS)] = kept.astype(jnp.bfloat16)

    product((0, 1))
    product((2, 3))
    for role in (0, 1):
        landed(*f[role])
    product((4, 5))
    sent(c3m, *c3, r3m, *r3, c4am, c4bm, r4am, r4bm, c5m, r5m, fm, *c4b, *trace[:5])
    for role in (2, 3):
        landed(*f[role])
    product((6, 7))

    trace_step(6)
    occupation[0, 0] = jnp.sum(tacc[7])
    for one in remote:
        if not any(one is other_one for other_one in done):
            one.wait_send()


def on_device(values, pattern, filter_mask, assignment):
    hbm = pl.BlockSpec(memory_space=pltpu.HBM)
    parts = lambda count: [pltpu.VMEM((count, PART, BS), jnp.bfloat16)] * CHUNKS
    lists = lambda *counts: [pltpu.SMEM((count * LIST,), jnp.int32) for count in counts]

    def path(final):
        return [
            *parts(4 * CAP + 1), *parts(2 * CAP), *parts(CAP), *parts(2 * CAP + 1),
            *parts(2 * CAP + 1), *lists(4, 2, 1, 1, 1, 1, 1, final),
        ]

    product, occupation = pl.pallas_call(
        kernel,
        out_shape=(
            jax.ShapeDtypeStruct((8, BS, 4 * BS), jnp.bfloat16),
            jax.ShapeDtypeStruct((1, 1), jnp.float32),
        ),
        in_specs=[hbm] * 4,
        out_specs=(pl.BlockSpec(memory_space=pltpu.VMEM), pl.BlockSpec(memory_space=pltpu.SMEM)),
        scratch_shapes=[
            pltpu.VMEM((4, 8, BS, BS), jnp.bfloat16),
            pltpu.SMEM((4, 8), jnp.int32),
            pltpu.SMEM((4, 8), jnp.int32),
            pltpu.SMEM((4, 8), jnp.int32),
            pltpu.SMEM((64,), jnp.int32),
            *[pltpu.VMEM((4, 4, PART, BS), jnp.bfloat16)] * CHUNKS,
            *path(4),
            *path(8),
            pltpu.VMEM((4 * CAP, BS, BS), jnp.bfloat16),
            *[pltpu.VMEM((CAP + 1, BS, BS), jnp.bfloat16)] * 8,
            pltpu.VMEM((8, 8, BS), jnp.float32),
            pltpu.VMEM((7, 8, BS), jnp.float32),
            pltpu.SMEM((IX_MATCH + 8 * 4 * CAP,), jnp.int32),
            pltpu.SemaphoreType.DMA((7,)),
            pltpu.SemaphoreType.DMA((COPIES,)),
            pltpu.SemaphoreType.DMA((COPIES,)),
        ],
        compiler_params=pltpu.CompilerParams(
            collective_id=0, has_side_effects=True, vmem_limit_bytes=52 * 1024 * 1024
        ),
        cost_estimate=pl.CostEstimate(
            flops=2 * 192 * BS**3, bytes_accessed=4 * 1024 * 1024, transcendentals=0
        ),
    )(values.reshape(8, BS, 4 * BS), pattern.T, filter_mask.T, assignment)
    return product.reshape(values.shape), occupation[0, 0]


def solution(mesh):
    in_specs = (P("row", "col"), P("row", "col"), P("row", "col"), P())
    out_specs = (P("row", "col"), P())
    return jax.shard_map(
        on_device, mesh=mesh, in_specs=in_specs, out_specs=out_specs, check_vma=False
    )
```
